128 devices in a mesh: dp: 16 (over x, y_hi, core), ctx: 4 (over z), tensor: 2 (over y_lo).
Axes of the slice: x: 4, y: 4 (y_hi: 2, y_lo: 2; y = y_hi * 2 + y_lo), z: 4, core: 2. Of those that a mesh axis runs over, the one named last changes fastest.
Arguments:
- tokens: bfloat16 [2, 8192, 1088], P(None, ('dp', 'ctx', 'tensor')), may hold values from -6 to 6
- qkv_weight: bfloat16 [2, 1088, 3264], P(None, 'dp'), may hold values from -0.1875 to 0.1875
- out_weight: bfloat16 [2, 1088, 1088], P(None, 'dp'), may hold values from -1.5 to 1.5
- up_weight: bfloat16 [2, 1088, 4352], P(None, 'dp', 'tensor'), may hold values from -0.1875 to 0.1875
- down_weight: bfloat16 [2, 1088, 4352], P(None, 'dp', 'tensor'), may hold values from -0.09375 to 0.09375
- vectors: bfloat16 [2, 12, 1088], P(None, None, 'dp'), as said below
- segments: int32 [2, 8192], P(None, ('dp', 'ctx', 'tensor')), may hold values from 0 to 2, as said below
- cotangent: float32 [2, 8192, 1088], P(None, ('dp', 'ctx', 'tensor')), may hold values from -6 to 6
Outputs:
- out: float32 [2, 8192, 1088], P(None, ('dp', 'ctx', 'tensor'))
- grad_tokens: float32 [2, 8192, 1088], P(None, ('dp', 'ctx', 'tensor'))
- grad_qkv: float32 [2, 1088, 3264], P(None, 'dp')
- grad_out: float32 [2, 1088, 1088], P(None, 'dp')
- grad_up: float32 [2, 1088, 4352], P(None, 'dp', 'tensor')
- grad_down: float32 [2, 1088, 4352], P(None, 'dp', 'tensor')
- grad_vectors: float32 [2, 12, 1088], P(None, None, 'dp')
The draws below stay inside these ranges and needn't reach their ends.
Inputs may be any that keep to these rules, and one draw needn't show every extreme that they name: `segments`: each sequence of 512 rows holds three documents numbered 0, 1, 2 in order of position. `vectors`: rows 0 and 5 of each layer lie between 0.5 and 1.5.
All inputs are finite; a program needn't handle non-finite values.
Results may differ from the reference program's by a relative error of at most 0.019.
Values may be sent and summed in bfloat16 or wider, within the bound.
A program may use at most 256 MiB of HBM per device.

```python
import math
import jax
import jax.numpy as jnp
from jax import lax

D = 1088
HEADS = 17
FF = 4352
LAYERS = 2
MICRO = 2
ROWS = 64
SEQ = 512
TOKENS = 8192


def draw_segments(key, part):
    seq_count = MICRO * TOKENS // SEQ
    opening = jax.random.randint(jax.random.fold_in(key, 11), (seq_count, 1), 1, ROWS // 2)
    closing = jax.random.randint(jax.random.fold_in(key, 23), (seq_count, 1), SEQ - ROWS // 2, SEQ)
    positions = jnp.arange(SEQ, dtype=jnp.int32)[None, :]
    labels = (positions >= opening).astype(jnp.int32) + (positions >= closing).astype(jnp.int32)
    return labels.reshape(MICRO, TOKENS)


def draw_vectors(key, part):
    dims_all = (LAYERS, 12, D)
    biases = 0.3 * jax.random.normal(jax.random.fold_in(key, 5), dims_all, jnp.float32)
    gains = jax.random.uniform(jax.random.fold_in(key, 7), dims_all, jnp.float32, 0.5, 1.5)
    row_ids = jnp.arange(12, dtype=jnp.int32)[None, :, None]
    is_gain = (row_ids == 0) | (row_ids == 5)
    return jnp.where(is_gain, gains, biases).astype(jnp.bfloat16)


def steps_of(key, dims, shards, least, largest):
    factor_of, own = 1.0, jax.random.fold_in(key, 6)
    for dim, blocks in shards:
        draws = jnp.exp(jax.random.uniform(jax.random.fold_in(own, dim), (blocks,), jnp.float32, least / len(shards), largest / len(shards)))
        factor_of = factor_of * jnp.repeat(draws, dims[dim] // blocks).reshape([-1 if axis == dim else 1 for axis in range(len(dims))])
    return factor_of


def normal_values(key, extent, width, most, cuts=(), kind=jnp.bfloat16):
    values = width * jax.random.normal(key, extent, jnp.float32)
    if cuts:
        values = values * steps_of(key, extent, cuts, -0.22, 0.18)
    return jnp.clip(values, -most, most).astype(kind)


def setup_inputs(seed: int = 0) -> dict:
    streams_of = jax.random.split(jax.random.key(seed), 9)
    return {
        "tokens": normal_values(streams_of[0], (MICRO, TOKENS, D), 1.0, 6.0, ((1, 128),)),
        "qkv_weight": normal_values(streams_of[1], (LAYERS, D, 3 * D), D ** -0.5, 0.1875, ((1, 16),)),
        "out_weight": normal_values(streams_of[2], (LAYERS, D, D), (D // 64) ** -0.5, 1.5, ((1, 16),)),
        "up_weight": normal_values(streams_of[3], (LAYERS, D, FF), D ** -0.5, 0.1875, ((1, 16), (2, 2))),
        "down_weight": normal_values(streams_of[4], (LAYERS, D, FF), FF ** -0.5, 0.09375, ((1, 16), (2, 2))),
        "vectors": draw_vectors(jax.random.fold_in(streams_of[8], 71), 0),
        "segments": draw_segments(jax.random.fold_in(streams_of[8], 71), 0),
        "cotangent": normal_values(streams_of[7], (MICRO, TOKENS, D), 1.0, 6.0, ((1, 128),), jnp.float32),
    }


EPSILON = 1e-05
MASKED = -1e+30
PRECISION = lax.Precision.HIGHEST

@jax.custom_vjp
def low(v):
    return lax.optimization_barrier(v.astype(jnp.bfloat16)).astype(jnp.float32)

@jax.custom_vjp
def low_back(v):
    return v

def low_keep(v):
    return (low(v), None)

def low_pass(kept, grad):
    return (grad,)

def back_keep(v):
    return (v, None)

def back_low(kept, grad):
    return (low(grad),)
low.defvjp(low_keep, low_pass)
low_back.defvjp(back_keep, back_low)

def layer_norm(inputs, gain_row, shift_row):
    row_mean = lax.optimization_barrier(jnp.mean(inputs, -1, keepdims=True))
    centred = inputs - row_mean
    spread = lax.optimization_barrier(jnp.mean(centred * centred, -1, keepdims=True))
    return centred * lax.rsqrt(spread + EPSILON) * gain_row + shift_row

def gelu_exact(inputs):
    return jax.nn.gelu(inputs, approximate=False)

def matmul_high(first_op, second_op):
    return jnp.dot(first_op, second_op, precision=PRECISION)

def block_stack(residual, doc_ids, attn_in, attn_out, up_proj, down_proj, vector_rows):
    length, model_width = residual.shape
    head_size = model_width // HEADS
    score_scale = 1.0 / math.sqrt(head_size)
    positions = jnp.arange(length, dtype=jnp.int32)
    allowed = (doc_ids[:, None] == doc_ids[None, :]) & (positions[None, :] <= positions[:, None])
    for layer_id in range(LAYERS):
        rows_vec = vector_rows[layer_id]
        normed = low(layer_norm(residual, rows_vec[0], rows_vec[1]))
        projected = matmul_high(normed, attn_in[layer_id])
        queries = low(low_back(projected[:, :model_width] + rows_vec[2]))
        keys_own = low(low_back(projected[:, model_width:2 * model_width]))
        values_own = low(low_back(projected[:, 2 * model_width:] + rows_vec[3]))
        query_heads = queries.reshape(length, HEADS, head_size)
        key_heads = keys_own.reshape(length, HEADS, head_size)
        value_heads = values_own.reshape(length, HEADS, head_size)
        scores = low_back(jnp.einsum('qhd,khd->hqk', query_heads, key_heads, precision=PRECISION) * score_scale)
        scores = jnp.where(allowed[None], scores, MASKED)
        row_max = lax.optimization_barrier(jnp.max(scores, -1, keepdims=True))
        exponent = jnp.exp(scores - row_max)
        attention_probs = low(exponent / lax.optimization_barrier(jnp.sum(exponent, -1, keepdims=True)))
        attended = jnp.einsum('hqk,khd->qhd', attention_probs, value_heads, precision=PRECISION)
        attended = low(low_back(attended.reshape(length, model_width)))
        residual = residual + low_back(matmul_high(attended, attn_out[layer_id]) + rows_vec[4])
        normed_two = low(layer_norm(residual, rows_vec[5], rows_vec[6]))
        hidden_pre = low_back(matmul_high(normed_two, up_proj[layer_id]) + rows_vec[8:].reshape(-1))
        hidden = low(gelu_exact(hidden_pre))
        down_out = lax.dot_general(hidden, down_proj[layer_id], (((1,), (1,)), ((), ())), precision=PRECISION)
        residual = residual + low_back(down_out + rows_vec[7])
    return residual

def reference(tokens, qkv_weight, out_weight, up_weight, down_weight, vectors, segments, cotangent):
    seq_count = tokens.shape[0] * tokens.shape[1] // SEQ
    doc_rows = segments.reshape(seq_count, SEQ)

    def forward(inputs, attn_in, attn_out, up_proj, down_proj, vector_rows):
        sequences = inputs.reshape(seq_count, SEQ, inputs.shape[-1])

        def one_sequence(element):
            return block_stack(element[0], element[1], attn_in, attn_out, up_proj, down_proj, vector_rows)
        outputs = lax.map(jax.checkpoint(one_sequence), (sequences, doc_rows))
        return outputs.reshape(inputs.shape)
    output, pullback = jax.vjp(forward, tokens.astype(jnp.float32), qkv_weight.astype(jnp.float32), out_weight.astype(jnp.float32), up_weight.astype(jnp.float32), down_weight.astype(jnp.float32), vectors.astype(jnp.float32))
    grads_all = pullback(cotangent.astype(jnp.float32))
    return (output, grads_all[0], grads_all[1], grads_all[2], grads_all[3], grads_all[4], grads_all[5])
```

```python
import functools

import jax
import jax.numpy as jnp
from jax import lax
from jax.experimental import pallas as pl
from jax.experimental.pallas import tpu as pltpu
from jax.sharding import PartitionSpec as P

EPSILON = 1e-05
MASKED = -1e30
MESH = pl.DeviceIdType.MESH
F32 = jnp.float32
BF16 = jnp.bfloat16
GROUP = 8
SLOTS = 5
HEAD = 64
WINDOW = 384
STRIDE = 256
PADDED = 1152
CHUNK = 128


def places():
    dp = lax.axis_index("dp")
    return {
        "x": dp // 4,
        "y": (dp // 2) % 2,
        "c": dp % 2,
        "z": lax.axis_index("ctx"),
        "t": lax.axis_index("tensor"),
    }


def shifted(value, x=0, y=0, c=0, z=0, t=0):
    pairs = []
    for i in range(128):
        ix, iy, ic, iz, it = i // 32, (i // 16) % 2, (i // 8) % 2, (i // 2) % 4, i % 2
        ix, iy, ic, iz, it = (ix + x) % 4, (iy + y) % 2, (ic + c) % 2, (iz + z) % 4, (it + t) % 2
        pairs.append((i, (((ix * 2 + iy) * 2 + ic) * 4 + iz) * 2 + it))
    return lax.ppermute(value, ("dp", "ctx", "tensor"), pairs)


def pair_up(first, mine, other):
    return jnp.where(first, jnp.concatenate([mine, other], 0), jnp.concatenate([other, mine], 0))


def ring_gather(axis, piece):
    half = piece.shape[0] // 2
    below = shifted(piece, **{axis: 1})
    above = shifted(piece, **{axis: -1})
    far_a = shifted(below[:half], **{axis: 1})
    far_b = shifted(above[half:], **{axis: -1})
    return {0: piece, -1: below, 1: above, 2: jnp.concatenate([far_a, far_b], 0)}


def ring_sum(axis, me, piece_of):
    far = piece_of((me + 2) % 4)
    half = far.shape[0] // 2
    via_up = shifted(far[:half], **{axis: 1})
    via_down = shifted(far[half:], **{axis: -1})
    up = piece_of((me + 1) % 4).astype(F32)
    down = piece_of((me + 3) % 4).astype(F32)
    up = jnp.concatenate([up[:half] + via_up.astype(F32), up[half:]], 0).astype(BF16)
    down = jnp.concatenate([down[:half], down[half:] + via_down.astype(F32)], 0).astype(BF16)
    from_below = shifted(up, **{axis: 1})
    from_above = shifted(down, **{axis: -1})
    total = piece_of(me).astype(F32) + from_below.astype(F32) + from_above.astype(F32)
    return total.astype(BF16)


def attn_start(z):
    return (z * 13) // 3 * 128


def mlp_start(z):
    return z * 512


QUARTER = 640


def columns(array, start):
    return lax.dynamic_slice_in_dim(array, pl.multiple_of(start, 128), QUARTER, 1)


def rows_of(array, start, count):
    return lax.dynamic_slice_in_dim(array, start, count, 0)


def padded(matrix, extra=None):
    rows, width = matrix.shape
    parts = [matrix]
    if extra is not None:
        parts.append(extra)
        width += extra.shape[1]
    parts.append(jnp.zeros((rows, PADDED - width), matrix.dtype))
    return jnp.concatenate(parts, 1)


def gather_layer(at, qkv, out, up, down, vec):
    width = out.shape[1]
    rows = out.shape[0]
    c0, y0 = at["c"] == 0, at["y"] == 0
    role0 = jnp.concatenate([padded(qkv[:, :width], vec.T), padded(qkv[:, width : 2 * width])], 1)
    role1 = jnp.concatenate([padded(qkv[:, 2 * width :]), padded(out)], 1)
    start = attn_start(at["z"])
    role0, role1 = columns(role0, start), columns(role1, start)

    def two_level(a, b):
        mine, give = jnp.where(c0, a, b), jnp.where(c0, b, a)
        pair = pair_up(c0, mine, shifted(give, c=1))
        return pair_up(y0, pair, shifted(pair, y=1))

    own = two_level(role0, role1)
    quarter = jnp.zeros((width, QUARTER), BF16)
    for distance, piece in ring_gather("x", own).items():
        quarter = lax.dynamic_update_slice(
            quarter, piece, ((at["x"] + distance) % 4 * (4 * rows), 0)
        )
    attn = jnp.zeros((2, width, 2 * PADDED), BF16)
    for distance, piece in ring_gather("z", quarter).items():
        place = attn_start((at["z"] + distance) % 4)
        attn = lax.dynamic_update_slice(attn, piece[None], (at["c"], 0, place))
        attn = lax.dynamic_update_slice(attn, shifted(piece, c=1)[None], (1 - at["c"], 0, place))
    own = two_level(up, down)
    mlp = jnp.zeros((2, width, up.shape[1]), BF16)
    for distance, piece in ring_gather("x", own).items():
        place = (at["x"] + distance) % 4 * (4 * rows)
        mlp = lax.dynamic_update_slice(mlp, piece[None], (at["c"], place, 0))
        mlp = lax.dynamic_update_slice(mlp, shifted(piece, c=1)[None], (1 - at["c"], place, 0))
    return attn, mlp


def contract_rows(a, b):
    return lax.dot_general(a, b, (((0,), (0,)), ((), ())), preferred_element_type=F32)


def contract_cols(a, b):
    return lax.dot_general(a, b, (((1,), (1,)), ((), ())), preferred_element_type=F32)


def block_diagonal(a, b):
    zero = jnp.zeros_like(a)
    return jnp.concatenate(
        [jnp.concatenate([a, zero], 1), jnp.concatenate([zero, b], 1)], 0
    )


def finish(at, piece, start_of, width):
    whole = jnp.zeros((piece.shape[0], width), BF16)
    for distance, block in ring_gather("z", piece).items():
        whole = lax.dynamic_update_slice(whole, block, (0, start_of((at["z"] + distance) % 4)))
    rows = piece.shape[0] // 2
    mine = rows_of(whole, at["c"] * rows, rows)
    got = shifted(rows_of(whole, (1 - at["c"]) * rows, rows), c=1)
    c0 = at["c"] == 0
    return jnp.where(c0, mine, got), jnp.where(c0, got, mine)


def reduce_layer(at, operands):
    a, dq, dk, dv, o, dz, m, du, dy, g, vec = operands
    c0 = at["c"] == 0
    width = a.shape[1]
    pick = lambda p, q: jnp.where(c0, p, q)
    vec_cols = jnp.pad(vec.T, ((0, 0), (width, 2 * PADDED - width - vec.shape[0])))
    dz = jnp.pad(dz, ((0, 0), (0, PADDED - width)))
    give = contract_rows(
        jnp.concatenate([a, pick(o, a)], 0), block_diagonal(pick(dv, dq), pick(dz, dk))
    ) + pick(0.0, 1.0) * vec_cols
    got = shifted(give.astype(BF16), c=1)
    keep = contract_rows(
        jnp.concatenate([a, pick(a, o)], 0), block_diagonal(pick(dq, dv), pick(dk, dz))
    ) + pick(1.0, 0.0) * vec_cols
    attn = (keep + got.astype(F32)).astype(BF16)
    give = contract_rows(pick(dy, m), pick(g, du)).astype(BF16)
    got = shifted(give, c=1)
    mlp = (contract_rows(pick(m, dy), pick(du, g)) + got.astype(F32)).astype(BF16)

    rows = width // 4
    attn = ring_sum("z", at["z"], lambda i: columns(attn, attn_start(i)))
    mlp = ring_sum("x", at["x"], lambda i: rows_of(mlp, i * rows, rows))
    attn = ring_sum("x", at["x"], lambda i: rows_of(attn, i * rows, rows))
    mlp = ring_sum("z", at["z"], lambda i: columns(mlp, mlp_start(i)))
    half = rows // 2
    mine = rows_of(attn, at["y"] * half, half).astype(F32)
    got = shifted(rows_of(attn, (1 - at["y"]) * half, half), y=1, t=1).astype(F32)
    attn = (mine + got).astype(BF16)
    attn = (attn.astype(F32) + shifted(attn, t=1).astype(F32)).astype(BF16)
    mine = rows_of(mlp, at["y"] * half, half).astype(F32)
    got = shifted(rows_of(mlp, (1 - at["y"]) * half, half), y=1).astype(F32)
    mlp = (mine + got).astype(BF16)
    qk, vo = finish(at, attn, attn_start, 2 * PADDED)
    up, down = finish(at, mlp, mlp_start, du.shape[1])
    in_back = jnp.concatenate(
        [qk[:, :width], qk[:, PADDED : PADDED + width], vo[:, :width]], 1
    ).astype(F32)
    out_back = vo[:, PADDED : PADDED + width].astype(F32)
    vec_back = qk[:, width : width + 12].T.astype(F32)
    return in_back, out_back, up.astype(F32), down.astype(F32), vec_back


def group_place():
    return lax.axis_index("ctx") * 2 + lax.axis_index("tensor")


def member(index):
    return (lax.axis_index("dp"), index // 2, lax.rem(index, 2))


def meet(me):
    barrier = pltpu.get_barrier_semaphore()
    for k in range(1, GROUP):
        pl.semaphore_signal(
            barrier, inc=1, device_id=member(lax.rem(me + k, GROUP)), device_id_type=MESH
        )
    pl.semaphore_wait(barrier, GROUP - 1)


def to_heads(me, sources, landed, local_sem, send_sem, recv_sem):
    copies = []
    for k in range(1, GROUP):
        peer = lax.rem(me + k, GROUP)
        rows = pl.ds(pl.multiple_of(peer // 4 * 64, 64), 64)
        lanes = pl.ds(pl.multiple_of(lax.rem(peer, 4) * STRIDE, 128), WINDOW)
        for n, (src, dst) in enumerate(zip(sources, landed)):
            copy = pltpu.make_async_remote_copy(
                src_ref=src.at[rows, lanes],
                dst_ref=dst.at[pl.ds(pl.multiple_of(me * 64, 64), 64)],
                send_sem=send_sem.at[n, k],
                recv_sem=recv_sem.at[n, k],
                device_id=member(peer),
                device_id_type=MESH,
            )
            copy.start()
            copies.append(copy)
    rows = pl.ds(pl.multiple_of(me // 4 * 64, 64), 64)
    lanes = pl.ds(pl.multiple_of(lax.rem(me, 4) * STRIDE, 128), WINDOW)
    for n, (src, dst) in enumerate(zip(sources, landed)):
        copy = pltpu.make_async_copy(
            src.at[rows, lanes], dst.at[pl.ds(pl.multiple_of(me * 64, 64), 64)], local_sem.at[n]
        )
        copy.start()
        copies.append(copy)
    return copies


def to_rows(me, sources, landed, local_sem, send_sem, recv_sem):
    copies = []
    for k in range(1, GROUP):
        peer = lax.rem(me + k, GROUP)
        for n, (src, dst) in enumerate(zip(sources, landed)):
            copy = pltpu.make_async_remote_copy(
                src_ref=src.at[pl.ds(pl.multiple_of(peer * 64, 64), 64)],
                dst_ref=dst.at[me],
                send_sem=send_sem.at[n, k],
                recv_sem=recv_sem.at[n, k],
                device_id=member(peer),
                device_id_type=MESH,
            )
            copy.start()
            copies.append(copy)
    for n, (src, dst) in enumerate(zip(sources, landed)):
        copy = pltpu.make_async_copy(
            src.at[pl.ds(pl.multiple_of(me * 64, 64), 64)], dst.at[me], local_sem.at[n]
        )
        copy.start()
        copies.append(copy)
    return copies


def side_by_side(landed, out):
    for micro in range(2):
        rows = slice(micro * 64, micro * 64 + 64)
        for group in range(4):
            width = WINDOW if group == 3 else STRIDE
            out[rows, group * STRIDE : group * STRIDE + width] = landed[micro * 4 + group, :, :width]


def matmul(a, b, dims):
    return lax.dot_general(a, b, ((dims[:1], dims[1:]), ((), ())), preferred_element_type=F32)


def attend_kernel(
    q, k, v, bias, out, q_all, k_all, v_all, o_all, log_total,
    o_low, o_landed, local_sem, send_sem, recv_sem,
):
    me = group_place()
    meet(me)
    copies = to_heads(
        me, (q, k, v), (q_all, k_all, v_all), local_sem, send_sem, recv_sem
    )
    o_low[...] = jnp.zeros_like(o_low)
    o_all[...] = jnp.zeros_like(o_all)
    log_total[...] = jnp.zeros_like(log_total)
    for copy in copies:
        copy.wait()
    for head in range(SLOTS):
        lanes = slice(head * HEAD, head * HEAD + HEAD)
        keys, values = k_all[:, lanes], v_all[:, lanes]
        for start in range(0, 512, CHUNK):
            rows, reach = slice(start, start + CHUNK), start + CHUNK
            queries = q_all[rows, lanes] * 0.125
            scores = matmul(queries, keys[:reach], (1, 1)) + bias[rows, :reach]
            top = jnp.max(scores, 1, keepdims=True)
            weights = jnp.exp(scores - top)
            total = jnp.sum(weights, 1, keepdims=True)
            result = matmul(weights.astype(BF16), values[:reach], (1, 0)) / total
            o_all[rows, lanes] = result
            o_low[rows, lanes] = result.astype(BF16)
            log_total[rows, head : head + 1] = top + jnp.log(total)
    copies = to_rows(
        me, (o_low,), (o_landed,), local_sem.at[3:4], send_sem.at[3:4], recv_sem.at[3:4]
    )
    for copy in copies:
        copy.wait()
    side_by_side(o_landed, out)


def attend(q, k, v, bias, collective):
    shape = jax.ShapeDtypeStruct
    vmem = pl.BlockSpec(memory_space=pltpu.VMEM)
    return pl.pallas_call(
        attend_kernel,
        out_shape=(
            shape((128, PADDED), BF16),
            shape((512, WINDOW), BF16),
            shape((512, WINDOW), BF16),
            shape((512, WINDOW), BF16),
            shape((512, WINDOW), F32),
            shape((512, 128), F32),
        ),
        in_specs=[vmem] * 4,
        out_specs=[vmem] * 6,
        scratch_shapes=[
            pltpu.VMEM((512, WINDOW), BF16),
            pltpu.VMEM((GROUP, 64, WINDOW), BF16),
            pltpu.SemaphoreType.DMA((4,)),
            pltpu.SemaphoreType.DMA((4, GROUP)),
            pltpu.SemaphoreType.DMA((4, GROUP)),
        ],
        compiler_params=pltpu.CompilerParams(
            collective_id=collective, has_side_effects=True, vmem_limit_bytes=32 * 2**20
        ),
    )(q, k, v, bias)


def attend_back_kernel(
    do, q_all, k_all, v_all, o_all, log_total, bias, dq, dk, dv,
    do_all, dq_low, dk_low, dv_low, dq_landed, dk_landed, dv_landed, dk_sum, dv_sum,
    local_sem, send_sem, recv_sem,
):
    me = group_place()
    meet(me)
    copies = to_heads(
        me, (do,), (do_all,), local_sem.at[3:4], send_sem.at[3:4], recv_sem.at[3:4]
    )
    dq_low[...] = jnp.zeros_like(dq_low)
    dk_low[...] = jnp.zeros_like(dk_low)
    dv_low[...] = jnp.zeros_like(dv_low)
    for copy in copies:
        copy.wait()
    for head in range(SLOTS):
        lanes = slice(head * HEAD, head * HEAD + HEAD)
        keys, values = k_all[:, lanes], v_all[:, lanes]
        dk_sum[...] = jnp.zeros_like(dk_sum)
        dv_sum[...] = jnp.zeros_like(dv_sum)
        for start in range(0, 512, CHUNK):
            rows, reach = slice(start, start + CHUNK), start + CHUNK
            queries = q_all[rows, lanes] * 0.125
            grads = do_all[rows, lanes]
            scores = matmul(queries, keys[:reach], (1, 1)) + bias[rows, :reach]
            probs = jnp.exp(scores - log_total[rows, head : head + 1])
            probs_back = matmul(grads, values[:reach], (1, 1))
            delta = jnp.sum(grads.astype(F32) * o_all[rows, lanes], 1, keepdims=True)
            scores_back = (probs * (probs_back - delta)).astype(BF16)
            dq_low[rows, lanes] = (matmul(scores_back, keys[:reach], (1, 0)) * 0.125).astype(BF16)
            dk_sum[:reach] += matmul(scores_back, queries, (0, 0))
            dv_sum[:reach] += matmul(probs.astype(BF16), grads, (0, 0))
        dk_low[:, lanes] = dk_sum[...].astype(BF16)
        dv_low[:, lanes] = dv_sum[...].astype(BF16)
    copies = to_rows(
        me,
        (dq_low, dk_low, dv_low),
        (dq_landed, dk_landed, dv_landed),
        local_sem,
        send_sem,
        recv_sem,
    )
    for copy in copies:
        copy.wait()
    side_by_side(dq_landed, dq)
    side_by_side(dk_landed, dk)
    side_by_side(dv_landed, dv)


def attend_back(do, saved, bias, collective):
    shape = jax.ShapeDtypeStruct
    vmem = pl.BlockSpec(memory_space=pltpu.VMEM)
    return pl.pallas_call(
        attend_back_kernel,
        out_shape=(shape((128, PADDED), BF16),) * 3,
        in_specs=[vmem] * 7,
        out_specs=[vmem] * 3,
        scratch_shapes=[pltpu.VMEM((512, WINDOW), BF16)] * 4
        + [pltpu.VMEM((GROUP, 64, WINDOW), BF16)] * 3
        + [pltpu.VMEM((512, HEAD), F32)] * 2
        + [
            pltpu.SemaphoreType.DMA((4,)),
            pltpu.SemaphoreType.DMA((4, GROUP)),
            pltpu.SemaphoreType.DMA((4, GROUP)),
        ],
        compiler_params=pltpu.CompilerParams(
            collective_id=collective, has_side_effects=True, vmem_limit_bytes=32 * 2**20
        ),
    )(do, *saved, bias)


def score_bias(segments):
    docs = lax.all_gather(segments.astype(BF16), ("ctx", "tensor"), axis=1, tiled=True)
    docs = lax.dynamic_index_in_dim(docs, lax.axis_index("ctx") // 2, 0, keepdims=False)
    place = jnp.arange(docs.shape[0], dtype=jnp.int32)
    allowed = (docs[:, None] == docs[None, :]) & (place[None, :] <= place[:, None])
    return jnp.where(allowed, 0.0, MASKED).astype(F32)


def layer_norm(inputs, gain_row, shift_row):
    row_mean = jnp.mean(inputs, -1, keepdims=True)
    centred = inputs - row_mean
    spread = jnp.mean(centred * centred, -1, keepdims=True)
    return centred * lax.rsqrt(spread + EPSILON) * gain_row + shift_row


def gelu_exact(inputs):
    return jax.nn.gelu(inputs, approximate=False)


def dot(a, b):
    return jnp.dot(a, b, preferred_element_type=F32)


def body(tokens, qkv_weight, out_weight, up_weight, down_weight, vectors, segments, cotangent):
    micro_count, row_count, width = tokens.shape
    layers = qkv_weight.shape[0]
    hidden_half = up_weight.shape[2]
    total_rows = micro_count * row_count
    at = places()
    bias = score_bias(segments)
    weights = [
        gather_layer(at, qkv_weight[l], out_weight[l], up_weight[l], down_weight[l], vectors[l])
        for l in range(layers)
    ]
    wide = lambda row: jnp.pad(row, (0, PADDED - width))
    residual = tokens.reshape(total_rows, width).astype(F32)
    memory = []
    for l in range(layers):
        attn_w, mlp_w = weights[l]
        vec = attn_w[0, :, width : width + 12].T.astype(F32)
        bias_up = lax.dynamic_slice_in_dim(vec[8:].reshape(-1), at["t"] * hidden_half, hidden_half)
        normed = layer_norm(residual, vec[0], vec[1]).astype(BF16)
        both = dot(normed, attn_w[0])
        q = (both[:, :PADDED] + wide(vec[2])).astype(BF16)
        k = both[:, PADDED:].astype(BF16)
        v = (dot(normed, attn_w[1, :, :PADDED]) + wide(vec[3])).astype(BF16)
        o, *saved = attend(q, k, v, bias, 1)
        o = o[:, :width]
        midway = residual + dot(o, attn_w[1, :, PADDED : PADDED + width]) + vec[4]
        m_own = layer_norm(midway, vec[5], vec[6]).astype(BF16)
        m_peer = shifted(m_own, t=1)
        u_own = dot(m_own, mlp_w[0]) + bias_up
        u_peer = dot(m_peer, mlp_w[0]) + bias_up
        g_peer = gelu_exact(u_peer).astype(BF16)
        got = shifted(contract_cols(g_peer, mlp_w[1]).astype(BF16), t=1)
        g_own = gelu_exact(u_own).astype(BF16)
        branch = contract_cols(g_own, mlp_w[1]) + got.astype(F32)
        memory.append(
            (vec, bias_up, normed, saved, o, residual, midway, m_own, m_peer, u_own, u_peer, g_own, g_peer)
        )
        residual = midway + branch + vec[7]
    result = residual
    gradient = cotangent.reshape(total_rows, width)
    totals = [None] * layers
    for l in reversed(range(layers)):
        attn_w, mlp_w = weights[l]
        vec, bias_up, normed, saved, o, layer_in, midway, m_own, m_peer, u_own, u_peer, g_own, g_peer = memory[l]
        dy_own = gradient.astype(BF16)
        dy_peer = shifted(dy_own, t=1)
        back = lambda u, dy: jax.vjp(gelu_exact, u)[1](dot(dy, mlp_w[1]))[0].astype(BF16)
        du_own = back(u_own, dy_own)
        du_peer = back(u_peer, dy_peer)
        got = shifted(contract_cols(du_peer, mlp_w[0]).astype(BF16), t=1)
        dm = contract_cols(du_own, mlp_w[0]) + got.astype(F32)
        midway_back, gain_two, shift_two = jax.vjp(layer_norm, midway, vec[5], vec[6])[1](dm)
        midway_back = midway_back + gradient
        dz = midway_back.astype(BF16)
        do = contract_cols(dz, attn_w[1, :, PADDED : PADDED + width]).astype(BF16)
        do = jnp.pad(do, ((0, 0), (0, PADDED - width)))
        dq, dk, dv = attend_back(do, saved, bias, 2)
        da = contract_cols(jnp.concatenate([dq, dk], 1), attn_w[0]) + contract_cols(
            dv, attn_w[1, :, :PADDED]
        )
        input_back, gain_one, shift_one = jax.vjp(layer_norm, layer_in, vec[0], vec[1])[1](da)
        gradient = midway_back + input_back
        m = jnp.concatenate([m_own, m_peer], 0)
        du = jnp.concatenate([du_own, du_peer], 0)
        dy = jnp.concatenate([dy_own, dy_peer], 0)
        g = jnp.concatenate([g_own, g_peer], 0)
        bias_back = lax.dynamic_update_slice_in_dim(
            jnp.zeros((2 * hidden_half,), F32), jnp.sum(du.astype(F32), 0), at["t"] * hidden_half, 0
        )
        down_rows = lambda v: jnp.sum(v.astype(F32), 0)[:width]
        small = jnp.stack(
            [gain_one, shift_one, down_rows(dq), down_rows(dv), down_rows(dz), gain_two, shift_two, down_rows(dy_own)]
        )
        vec_back = jnp.concatenate([small, bias_back.reshape(-1, width)], 0)
        totals[l] = reduce_layer(
            at, (normed, dq, dk, dv, o, dz, m, du, dy, g, vec_back)
        )
    stacked = [jnp.stack([totals[l][n] for l in range(layers)]) for n in range(5)]
    shape = (micro_count, row_count, width)
    return (result.reshape(shape), gradient.reshape(shape), *stacked)


def solution(mesh):
    return jax.shard_map(
        body,
        mesh=mesh,
        in_specs=(
            P(None, ("dp", "ctx", "tensor"), None),
            P(None, "dp", None),
            P(None, "dp", None),
            P(None, "dp", "tensor"),
            P(None, "dp", "tensor"),
            P(None, None, "dp"),
            P(None, ("dp", "ctx", "tensor")),
            P(None, ("dp", "ctx", "tensor"), None),
        ),
        out_specs=(
            P(None, ("dp", "ctx", "tensor"), None),
            P(None, ("dp", "ctx", "tensor"), None),
            P(None, "dp", None),
            P(None, "dp", None),
            P(None, "dp", "tensor"),
            P(None, "dp", "tensor"),
            P(None, None, "dp"),
        ),
        check_vma=False,
    )
```

```python
import functools

import jax
import jax.numpy as jnp
from jax import lax
from jax.experimental import pallas as pl
from jax.experimental.pallas import tpu as pltpu
from jax.sharding import PartitionSpec as P

EPSILON = 1e-05
MASKED = -1e30
MESH = pl.DeviceIdType.MESH
F32 = jnp.float32
BF16 = jnp.bfloat16
GROUP = 8
SLOTS = 5
HEAD = 64
WINDOW = 384
STRIDE = 256
PADDED = 1152
CHUNK = 128


def places():
    dp = lax.axis_index("dp")
    return {
        "x": dp // 4,
        "y": (dp // 2) % 2,
        "c": dp % 2,
        "z": lax.axis_index("ctx"),
        "t": lax.axis_index("tensor"),
    }


def shifted(value, x=0, y=0, c=0, z=0, t=0):
    pairs = []
    for i in range(128):
        ix, iy, ic, iz, it = i // 32, (i // 16) % 2, (i // 8) % 2, (i // 2) % 4, i % 2
        ix, iy, ic, iz, it = (ix + x) % 4, (iy + y) % 2, (ic + c) % 2, (iz + z) % 4, (it + t) % 2
        pairs.append((i, (((ix * 2 + iy) * 2 + ic) * 4 + iz) * 2 + it))
    return lax.ppermute(value, ("dp", "ctx", "tensor"), pairs)


def ring_gather(axis, piece):
    half = piece.shape[0] // 2
    below = shifted(piece, **{axis: 1})
    above = shifted(piece, **{axis: -1})
    far_a = shifted(below[:half], **{axis: 1})
    far_b = shifted(above[half:], **{axis: -1})
    return {0: piece, -1: below, 1: above, 2: jnp.concatenate([far_a, far_b], 0)}


def ring_sum(axis, me, piece_of):
    far = piece_of((me + 2) % 4)
    half = far.shape[0] // 2
    via_up = shifted(far[:half], **{axis: 1})
    via_down = shifted(far[half:], **{axis: -1})
    up = piece_of((me + 1) % 4).astype(F32)
    down = piece_of((me + 3) % 4).astype(F32)
    up = jnp.concatenate([up[:half] + via_up.astype(F32), up[half:]], 0).astype(BF16)
    down = jnp.concatenate([down[:half], down[half:] + via_down.astype(F32)], 0).astype(BF16)
    from_below = shifted(up, **{axis: 1})
    from_above = shifted(down, **{axis: -1})
    total = piece_of(me).astype(F32) + from_below.astype(F32) + from_above.astype(F32)
    return total.astype(BF16)


def attn_start(z):
    return (z * 13) // 3 * 128


def mlp_start(z):
    return z * 512


QUARTER = 640


def columns(array, start):
    return lax.dynamic_slice_in_dim(array, pl.multiple_of(start, 128), QUARTER, 1)


def rows_of(array, start, count):
    return lax.dynamic_slice_in_dim(array, start, count, 0)


ROWS = 68
TALL = 80
BLOCK = 272
NEAR = 144
Q_COLS = 512
T_START = 2048
T_COLS = 256
M_COLS = 2176


def peer_at(x=0, y=0, c=0, z=0, t=0):
    at = places()
    dp = (lax.rem(at["x"] + x + 4, 4) * 2 + lax.rem(at["y"] + y, 2)) * 2 + lax.rem(at["c"] + c, 2)
    return (dp, lax.rem(at["z"] + z + 4, 4), lax.rem(at["t"] + t, 2))


class Copies:
    def __init__(self, send_sem, recv_sem):
        self.send_sem, self.recv_sem = send_sem, recv_sem
        self.count = 0
        self.open = []

    def to(self, peer, src, dst):
        n = self.count
        self.count += 1
        copy = pltpu.make_async_remote_copy(
            src_ref=src,
            dst_ref=dst,
            send_sem=self.send_sem.at[n],
            recv_sem=self.recv_sem.at[n],
            device_id=peer,
            device_id_type=MESH,
        )
        copy.start()
        self.open.append(copy.wait_send)
        return copy.wait_recv

    def here(self, src, dst):
        n = self.count
        self.count += 1
        copy = pltpu.make_async_copy(src, dst, self.send_sem.at[n])
        copy.start()
        return copy.wait

    def close(self):
        for wait in self.open:
            wait()
        self.open = []


def rows_at(block, count=BLOCK, skip=0):
    return pl.ds(pl.multiple_of(block * BLOCK + skip, 16), count)


class RingX:
    def __init__(self, copies, own, buf, lanes, share):
        self.copies, self.own, self.buf, self.lanes, self.share = copies, own, buf, lanes, share
        at = places()
        self.c, self.x = at["c"], at["x"]
        self.last = []

    def view(self, distance, count=BLOCK, skip=0):
        block = lax.rem(self.x + distance + 4, 4)
        return self.buf.at[self.c, rows_at(block, count, skip), self.lanes]

    def sibling(self, src, dst):
        if self.share:
            self.last.append(self.copies.to(peer_at(c=1), src, dst))

    def start(self):
        self.from_below = self.copies.to(peer_at(x=1), self.own, self.view(0))
        self.from_above = self.copies.to(peer_at(x=-1), self.own, self.view(0))
        self.last.append(self.copies.here(self.own, self.view(0)))
        self.sibling(self.own, self.view(0))

    def forward(self):
        self.from_below()
        part = self.view(-1, NEAR)
        far_a = self.copies.to(peer_at(x=1), part, part)
        self.from_above()
        part = self.view(1, BLOCK - NEAR, NEAR)
        far_b = self.copies.to(peer_at(x=-1), part, part)
        self.far = (far_a, far_b)
        self.sibling(self.view(-1), self.view(-1))
        self.sibling(self.view(1), self.view(1))

    def finish(self):
        for wait in self.far:
            wait()
        self.sibling(self.view(2), self.view(2))

    def close(self):
        for wait in self.last:
            wait()


class RingZ:
    def __init__(self, copies, buf):
        self.copies, self.buf = copies, buf
        at = places()
        self.c, self.z = at["c"], at["z"]
        self.last = []

    def view(self, distance, rows=slice(None)):
        block = lax.rem(self.z + distance + 4, 4)
        return self.buf.at[self.c, rows, pl.ds(pl.multiple_of(block * Q_COLS, 128), Q_COLS)]

    def sibling(self, src):
        self.last.append(self.copies.to(peer_at(c=1), src, src))

    def start(self):
        own = self.view(0)
        self.from_below = self.copies.to(peer_at(z=1), own, own)
        self.from_above = self.copies.to(peer_at(z=-1), own, own)
        self.sibling(own)

    def forward(self):
        self.from_below()
        part = self.view(-1, pl.ds(0, 544))
        far_a = self.copies.to(peer_at(z=1), part, part)
        self.from_above()
        part = self.view(1, pl.ds(544, 544))
        far_b = self.copies.to(peer_at(z=-1), part, part)
        self.far = (far_a, far_b)
        self.sibling(self.view(-1))
        self.sibling(self.view(1))

    def finish(self):
        for wait in self.far:
            wait()
        self.sibling(self.view(2))

    def close(self):
        for wait in self.last:
            wait()


def exchange_shards(copies, mine, landed):
    c = places()["c"]
    waits = [
        copies.to(peer_at(c=1), mine.at[1 - c], landed.at[1]),
        copies.to(peer_at(y=1), mine.at[c], landed.at[2]),
        copies.to(peer_at(y=1, c=1), mine.at[1 - c], landed.at[3]),
    ]
    waits.append(copies.here(mine.at[c], landed.at[0]))
    return waits


def assemble(landed, own):
    at = places()
    width = own.shape[1]
    for start in range(0, width, 256):
        lanes = slice(start, min(start + 256, width))
        parts = []
        for j in range(4):
            slot = lax.rem(j // 2 + at["y"], 2) * 2 + lax.rem(j % 2 + at["c"], 2)
            parts.append(landed[slot, :, lanes].astype(F32)[:ROWS])
        own[:, lanes] = jnp.concatenate(parts, 0).astype(BF16)


def gather_barrier():
    barrier = pltpu.get_barrier_semaphore()
    peers = [dict(c=1), dict(y=1), dict(y=1, c=1), dict(x=1), dict(x=-1), dict(z=1), dict(z=-1)]
    for peer in peers:
        pl.semaphore_signal(barrier, inc=1, device_id=peer_at(**peer), device_id_type=MESH)
    pl.semaphore_wait(barrier, len(peers))


def gather_kernel(*refs, layers):
    q_in, mt_in = refs[:layers], refs[layers : 2 * layers]
    attn, mlp = refs[2 * layers : 3 * layers], refs[3 * layers : 4 * layers]
    q_land, mt_land, q_own, mt_own, send_sem, recv_sem = refs[4 * layers :]
    gather_barrier()
    copies = Copies(send_sem, recv_sem)
    z = places()["z"]
    quarter = pl.ds(pl.multiple_of(z * Q_COLS, 128), Q_COLS)
    arrivals = []
    for l in range(layers):
        first = exchange_shards(copies, q_in[l], q_land.at[l])
        arrivals.append((first, exchange_shards(copies, mt_in[l], mt_land.at[l])))
    rings = []
    for l in range(layers):
        q = RingX(copies, q_own.at[l], attn[l], quarter, False)
        m = RingX(copies, mt_own.at[l, :, pl.ds(0, M_COLS)], mlp[l], slice(None), True)
        t = RingX(copies, mt_own.at[l, :, pl.ds(M_COLS, T_COLS)], attn[l], pl.ds(T_START, T_COLS), True)
        rings.append((q, m, t, RingZ(copies, attn[l])))

    def begin(l):
        q, m, t, _ = rings[l]
        for wait in arrivals[l][0]:
            wait()
        assemble(q_land.at[l], q_own.at[l])
        q.start()
        for wait in arrivals[l][1]:
            wait()
        assemble(mt_land.at[l], mt_own.at[l])
        m.start()
        t.start()

    begin(0)
    for l in range(layers):
        q, m, t, along_z = rings[l]
        q.forward()
        q.finish()
        q.close()
        along_z.start()
        m.forward()
        t.forward()
        if l + 1 < layers:
            begin(l + 1)
        along_z.forward()
        m.finish()
        t.finish()
        along_z.finish()
    for group in rings:
        for ring in group[1:]:
            ring.close()
    copies.close()


def shard_rows(qkv, out, up, down, vec, z):
    width = out.shape[1]
    role0 = jnp.concatenate([padded(qkv[:, :width], vec.T), padded(qkv[:, width : 2 * width])], 1)
    role1 = jnp.concatenate([padded(qkv[:, 2 * width :]), padded(out)], 1)
    attn = jnp.pad(jnp.stack([role0, role1]), ((0, 0), (0, TALL - ROWS), (0, 0)))
    mlp = jnp.pad(jnp.stack([up, down]), ((0, 0), (0, TALL - ROWS), (0, 0)))
    quarter = lax.dynamic_slice_in_dim(attn, z * Q_COLS, Q_COLS, 2)
    return quarter, jnp.concatenate([mlp, attn[:, :, T_START:]], 2)


def gather_layers(shards, collective):
    layers = len(shards)
    hbm = pl.BlockSpec(memory_space=pl.ANY)
    shape = jax.ShapeDtypeStruct
    results = pl.pallas_call(
        functools.partial(gather_kernel, layers=layers),
        out_shape=[shape((2, 4 * BLOCK, 2 * PADDED), BF16)] * layers
        + [shape((2, 4 * BLOCK, M_COLS), BF16)] * layers,
        in_specs=[hbm] * (2 * layers),
        out_specs=[hbm] * (2 * layers),
        scratch_shapes=[
            pltpu.VMEM((layers, 4, TALL, Q_COLS), BF16),
            pltpu.VMEM((layers, 4, TALL, M_COLS + T_COLS), BF16),
            pltpu.VMEM((layers, BLOCK, Q_COLS), BF16),
            pltpu.VMEM((layers, BLOCK, M_COLS + T_COLS), BF16),
            pltpu.SemaphoreType.DMA((48 * layers,)),
            pltpu.SemaphoreType.DMA((48 * layers,)),
        ],
        compiler_params=pltpu.CompilerParams(
            collective_id=collective, has_side_effects=True, vmem_limit_bytes=32 * 2**20
        ),
    )(*[q for q, _ in shards], *[mt for _, mt in shards])
    return list(zip(results[:layers], results[layers:]))


def padded(matrix, extra=None):
    rows, width = matrix.shape
    parts = [matrix]
    if extra is not None:
        parts.append(extra)
        width += extra.shape[1]
    parts.append(jnp.zeros((rows, PADDED - width), matrix.dtype))
    return jnp.concatenate(parts, 1)


def contract_rows(a, b):
    return lax.dot_general(a, b, (((0,), (0,)), ((), ())), preferred_element_type=F32)


def contract_cols(a, b):
    return lax.dot_general(a, b, (((1,), (1,)), ((), ())), preferred_element_type=F32)


def block_diagonal(a, b):
    zero = jnp.zeros_like(a)
    return jnp.concatenate(
        [jnp.concatenate([a, zero], 1), jnp.concatenate([zero, b], 1)], 0
    )


def finish(at, piece, start_of, width):
    whole = jnp.zeros((piece.shape[0], width), BF16)
    for distance, block in ring_gather("z", piece).items():
        whole = lax.dynamic_update_slice(whole, block, (0, start_of((at["z"] + distance) % 4)))
    rows = piece.shape[0] // 2
    mine = rows_of(whole, at["c"] * rows, rows)
    got = shifted(rows_of(whole, (1 - at["c"]) * rows, rows), c=1)
    c0 = at["c"] == 0
    return jnp.where(c0, mine, got), jnp.where(c0, got, mine)


def reduce_layer(at, operands):
    a, dq, dk, dv, o, dz, m, du, dy, g, vec = operands
    c0 = at["c"] == 0
    width = a.shape[1]
    pick = lambda p, q: jnp.where(c0, p, q)
    vec_cols = jnp.pad(vec.T, ((0, 0), (width, 2 * PADDED - width - vec.shape[0])))
    dz = jnp.pad(dz, ((0, 0), (0, PADDED - width)))
    give = contract_rows(
        jnp.concatenate([a, pick(o, a)], 0), block_diagonal(pick(dv, dq), pick(dz, dk))
    ) + pick(0.0, 1.0) * vec_cols
    got = shifted(give.astype(BF16), c=1)
    keep = contract_rows(
        jnp.concatenate([a, pick(a, o)], 0), block_diagonal(pick(dq, dv), pick(dk, dz))
    ) + pick(1.0, 0.0) * vec_cols
    attn = (keep + got.astype(F32)).astype(BF16)
    give = contract_rows(pick(dy, m), pick(g, du)).astype(BF16)
    got = shifted(give, c=1)
    mlp = (contract_rows(pick(m, dy), pick(du, g)) + got.astype(F32)).astype(BF16)

    rows = width // 4
    attn = ring_sum("z", at["z"], lambda i: columns(attn, attn_start(i)))
    mlp = ring_sum("x", at["x"], lambda i: rows_of(mlp, i * rows, rows))
    attn = ring_sum("x", at["x"], lambda i: rows_of(attn, i * rows, rows))
    mlp = ring_sum("z", at["z"], lambda i: columns(mlp, mlp_start(i)))
    half = rows // 2
    mine = rows_of(attn, at["y"] * half, half).astype(F32)
    got = shifted(rows_of(attn, (1 - at["y"]) * half, half), y=1, t=1).astype(F32)
    attn = (mine + got).astype(BF16)
    attn = (attn.astype(F32) + shifted(attn, t=1).astype(F32)).astype(BF16)
    mine = rows_of(mlp, at["y"] * half, half).astype(F32)
    got = shifted(rows_of(mlp, (1 - at["y"]) * half, half), y=1).astype(F32)
    mlp = (mine + got).astype(BF16)
    qk, vo = finish(at, attn, attn_start, 2 * PADDED)
    up, down = finish(at, mlp, mlp_start, du.shape[1])
    in_back = jnp.concatenate(
        [qk[:, :width], qk[:, PADDED : PADDED + width], vo[:, :width]], 1
    ).astype(F32)
    out_back = vo[:, PADDED : PADDED + width].astype(F32)
    vec_back = qk[:, width : width + 12].T.astype(F32)
    return in_back, out_back, up.astype(F32), down.astype(F32), vec_back


def group_place():
    return lax.axis_index("ctx") * 2 + lax.axis_index("tensor")


def member(index):
    return (lax.axis_index("dp"), index // 2, lax.rem(index, 2))


def meet(me):
    barrier = pltpu.get_barrier_semaphore()
    for k in range(1, GROUP):
        pl.semaphore_signal(
            barrier, inc=1, device_id=member(lax.rem(me + k, GROUP)), device_id_type=MESH
        )
    pl.semaphore_wait(barrier, GROUP - 1)


def to_heads(me, sources, landed, local_sem, send_sem, recv_sem):
    copies = []
    for k in range(1, GROUP):
        peer = lax.rem(me + k, GROUP)
        rows = pl.ds(pl.multiple_of(peer // 4 * 64, 64), 64)
        lanes = pl.ds(pl.multiple_of(lax.rem(peer, 4) * STRIDE, 128), WINDOW)
        for n, (src, dst) in enumerate(zip(sources, landed)):
            copy = pltpu.make_async_remote_copy(
                src_ref=src.at[rows, lanes],
                dst_ref=dst.at[pl.ds(pl.multiple_of(me * 64, 64), 64)],
                send_sem=send_sem.at[n, k],
                recv_sem=recv_sem.at[n, k],
                device_id=member(peer),
                device_id_type=MESH,
            )
            copy.start()
            copies.append(copy)
    rows = pl.ds(pl.multiple_of(me // 4 * 64, 64), 64)
    lanes = pl.ds(pl.multiple_of(lax.rem(me, 4) * STRIDE, 128), WINDOW)
    for n, (src, dst) in enumerate(zip(sources, landed)):
        copy = pltpu.make_async_copy(
            src.at[rows, lanes], dst.at[pl.ds(pl.multiple_of(me * 64, 64), 64)], local_sem.at[n]
        )
        copy.start()
        copies.append(copy)
    return copies


def to_rows(me, sources, landed, local_sem, send_sem, recv_sem):
    copies = []
    for k in range(1, GROUP):
        peer = lax.rem(me + k, GROUP)
        for n, (src, dst) in enumerate(zip(sources, landed)):
            copy = pltpu.make_async_remote_copy(
                src_ref=src.at[pl.ds(pl.multiple_of(peer * 64, 64), 64)],
                dst_ref=dst.at[me],
                send_sem=send_sem.at[n, k],
                recv_sem=recv_sem.at[n, k],
                device_id=member(peer),
                device_id_type=MESH,
            )
            copy.start()
            copies.append(copy)
    for n, (src, dst) in enumerate(zip(sources, landed)):
        copy = pltpu.make_async_copy(
            src.at[pl.ds(pl.multiple_of(me * 64, 64), 64)], dst.at[me], local_sem.at[n]
        )
        copy.start()
        copies.append(copy)
    return copies


def side_by_side(landed, out):
    for micro in range(2):
        rows = slice(micro * 64, micro * 64 + 64)
        for group in range(4):
            width = WINDOW if group == 3 else STRIDE
            out[rows, group * STRIDE : group * STRIDE + width] = landed[micro * 4 + group, :, :width]


def matmul(a, b, dims):
    return lax.dot_general(a, b, ((dims[:1], dims[1:]), ((), ())), preferred_element_type=F32)


def attend_kernel(
    q, k, v, bias, out, q_all, k_all, v_all, o_all, log_total,
    o_low, o_landed, local_sem, send_sem, recv_sem,
):
    me = group_place()
    meet(me)
    copies = to_heads(
        me, (q, k, v), (q_all, k_all, v_all), local_sem, send_sem, recv_sem
    )
    o_low[...] = jnp.zeros_like(o_low)
    o_all[...] = jnp.zeros_like(o_all)
    log_total[...] = jnp.zeros_like(log_total)
    for copy in copies:
        copy.wait()
    for head in range(SLOTS):
        lanes = slice(head * HEAD, head * HEAD + HEAD)
        keys, values = k_all[:, lanes], v_all[:, lanes]
        for start in range(0, 512, CHUNK):
            rows, reach = slice(start, start + CHUNK), start + CHUNK
            queries = q_all[rows, lanes] * 0.125
            scores = matmul(queries, keys[:reach], (1, 1)) + bias[rows, :reach]
            top = jnp.max(scores, 1, keepdims=True)
            weights = jnp.exp(scores - top)
            total = jnp.sum(weights, 1, keepdims=True)
            result = matmul(weights.astype(BF16), values[:reach], (1, 0)) / total
            o_all[rows, lanes] = result
            o_low[rows, lanes] = result.astype(BF16)
            log_total[rows, head : head + 1] = top + jnp.log(total)
    copies = to_rows(
        me, (o_low,), (o_landed,), local_sem.at[3:4], send_sem.at[3:4], recv_sem.at[3:4]
    )
    for copy in copies:
        copy.wait()
    side_by_side(o_landed, out)


def attend(q, k, v, bias, collective):
    shape = jax.ShapeDtypeStruct
    vmem = pl.BlockSpec(memory_space=pltpu.VMEM)
    return pl.pallas_call(
        attend_kernel,
        out_shape=(
            shape((128, PADDED), BF16),
            shape((512, WINDOW), BF16),
            shape((512, WINDOW), BF16),
            shape((512, WINDOW), BF16),
            shape((512, WINDOW), F32),
            shape((512, 128), F32),
        ),
        in_specs=[vmem] * 4,
        out_specs=[vmem] * 6,
        scratch_shapes=[
            pltpu.VMEM((512, WINDOW), BF16),
            pltpu.VMEM((GROUP, 64, WINDOW), BF16),
            pltpu.SemaphoreType.DMA((4,)),
            pltpu.SemaphoreType.DMA((4, GROUP)),
            pltpu.SemaphoreType.DMA((4, GROUP)),
        ],
        compiler_params=pltpu.CompilerParams(
            collective_id=collective, has_side_effects=True, vmem_limit_bytes=32 * 2**20
        ),
    )(q, k, v, bias)


def attend_back_kernel(
    do, q_all, k_all, v_all, o_all, log_total, bias, dq, dk, dv,
    do_all, dq_low, dk_low, dv_low, dq_landed, dk_landed, dv_landed, dk_sum, dv_sum,
    local_sem, send_sem, recv_sem,
):
    me = group_place()
    meet(me)
    copies = to_heads(
        me, (do,), (do_all,), local_sem.at[3:4], send_sem.at[3:4], recv_sem.at[3:4]
    )
    dq_low[...] = jnp.zeros_like(dq_low)
    dk_low[...] = jnp.zeros_like(dk_low)
    dv_low[...] = jnp.zeros_like(dv_low)
    for copy in copies:
        copy.wait()
    for head in range(SLOTS):
        lanes = slice(head * HEAD, head * HEAD + HEAD)
        keys, values = k_all[:, lanes], v_all[:, lanes]
        dk_sum[...] = jnp.zeros_like(dk_sum)
        dv_sum[...] = jnp.zeros_like(dv_sum)
        for start in range(0, 512, CHUNK):
            rows, reach = slice(start, start + CHUNK), start + CHUNK
            queries = q_all[rows, lanes] * 0.125
            grads = do_all[rows, lanes]
            scores = matmul(queries, keys[:reach], (1, 1)) + bias[rows, :reach]
            probs = jnp.exp(scores - log_total[rows, head : head + 1])
            probs_back = matmul(grads, values[:reach], (1, 1))
            delta = jnp.sum(grads.astype(F32) * o_all[rows, lanes], 1, keepdims=True)
            scores_back = (probs * (probs_back - delta)).astype(BF16)
            dq_low[rows, lanes] = (matmul(scores_back, keys[:reach], (1, 0)) * 0.125).astype(BF16)
            dk_sum[:reach] += matmul(scores_back, queries, (0, 0))
            dv_sum[:reach] += matmul(probs.astype(BF16), grads, (0, 0))
        dk_low[:, lanes] = dk_sum[...].astype(BF16)
        dv_low[:, lanes] = dv_sum[...].astype(BF16)
    copies = to_rows(
        me,
        (dq_low, dk_low, dv_low),
        (dq_landed, dk_landed, dv_landed),
        local_sem,
        send_sem,
        recv_sem,
    )
    for copy in copies:
        copy.wait()
    side_by_side(dq_landed, dq)
    side_by_side(dk_landed, dk)
    side_by_side(dv_landed, dv)


def attend_back(do, saved, bias, collective):
    shape = jax.ShapeDtypeStruct
    vmem = pl.BlockSpec(memory_space=pltpu.VMEM)
    return pl.pallas_call(
        attend_back_kernel,
        out_shape=(shape((128, PADDED), BF16),) * 3,
        in_specs=[vmem] * 7,
        out_specs=[vmem] * 3,
        scratch_shapes=[pltpu.VMEM((512, WINDOW), BF16)] * 4
        + [pltpu.VMEM((GROUP, 64, WINDOW), BF16)] * 3
        + [pltpu.VMEM((512, HEAD), F32)] * 2
        + [
            pltpu.SemaphoreType.DMA((4,)),
            pltpu.SemaphoreType.DMA((4, GROUP)),
            pltpu.SemaphoreType.DMA((4, GROUP)),
        ],
        compiler_params=pltpu.CompilerParams(
            collective_id=collective, has_side_effects=True, vmem_limit_bytes=32 * 2**20
        ),
    )(do, *saved, bias)


def score_bias(segments):
    docs = lax.all_gather(segments.astype(BF16), ("ctx", "tensor"), axis=1, tiled=True)
    docs = lax.dynamic_index_in_dim(docs, lax.axis_index("ctx") // 2, 0, keepdims=False)
    place = jnp.arange(docs.shape[0], dtype=jnp.int32)
    allowed = (docs[:, None] == docs[None, :]) & (place[None, :] <= place[:, None])
    return jnp.where(allowed, 0.0, MASKED).astype(F32)


def layer_norm(inputs, gain_row, shift_row):
    row_mean = jnp.mean(inputs, -1, keepdims=True)
    centred = inputs - row_mean
    spread = jnp.mean(centred * centred, -1, keepdims=True)
    return centred * lax.rsqrt(spread + EPSILON) * gain_row + shift_row


def gelu_exact(inputs):
    return jax.nn.gelu(inputs, approximate=False)


def dot(a, b):
    return jnp.dot(a, b, preferred_element_type=F32)


def body(tokens, qkv_weight, out_weight, up_weight, down_weight, vectors, segments, cotangent):
    micro_count, row_count, width = tokens.shape
    layers = qkv_weight.shape[0]
    hidden_half = up_weight.shape[2]
    total_rows = micro_count * row_count
    at = places()
    bias = score_bias(segments)
    weights = gather_layers(
        [
            shard_rows(qkv_weight[l], out_weight[l], up_weight[l], down_weight[l], vectors[l], at["z"])
            for l in range(layers)
        ],
        3,
    )
    wide = lambda row: jnp.pad(row, (0, PADDED - width))
    residual = tokens.reshape(total_rows, width).astype(F32)
    memory = []
    for l in range(layers):
        attn_w, mlp_w = weights[l]
        vec = attn_w[0, :, width : width + 12].T.astype(F32)
        bias_up = lax.dynamic_slice_in_dim(vec[8:].reshape(-1), at["t"] * hidden_half, hidden_half)
        normed = layer_norm(residual, vec[0], vec[1]).astype(BF16)
        both = dot(normed, attn_w[0])
        q = (both[:, :PADDED] + wide(vec[2])).astype(BF16)
        k = both[:, PADDED:].astype(BF16)
        v = (dot(normed, attn_w[1, :, :PADDED]) + wide(vec[3])).astype(BF16)
        o, *saved = attend(q, k, v, bias, 1)
        o = o[:, :width]
        midway = residual + dot(o, attn_w[1, :, PADDED : PADDED + width]) + vec[4]
        m_own = layer_norm(midway, vec[5], vec[6]).astype(BF16)
        m_peer = shifted(m_own, t=1)
        u_own = dot(m_own, mlp_w[0]) + bias_up
        u_peer = dot(m_peer, mlp_w[0]) + bias_up
        g_peer = gelu_exact(u_peer).astype(BF16)
        got = shifted(contract_cols(g_peer, mlp_w[1]).astype(BF16), t=1)
        g_own = gelu_exact(u_own).astype(BF16)
        branch = contract_cols(g_own, mlp_w[1]) + got.astype(F32)
        memory.append(
            (vec, bias_up, normed, saved, o, residual, midway, m_own, m_peer, u_own, u_peer, g_own, g_peer)
        )
        residual = midway + branch + vec[7]
    result = residual
    gradient = cotangent.reshape(total_rows, width)
    totals = [None] * layers
    for l in reversed(range(layers)):
        attn_w, mlp_w = weights[l]
        vec, bias_up, normed, saved, o, layer_in, midway, m_own, m_peer, u_own, u_peer, g_own, g_peer = memory[l]
        dy_own = gradient.astype(BF16)
        dy_peer = shifted(dy_own, t=1)
        back = lambda u, dy: jax.vjp(gelu_exact, u)[1](dot(dy, mlp_w[1]))[0].astype(BF16)
        du_own = back(u_own, dy_own)
        du_peer = back(u_peer, dy_peer)
        got = shifted(contract_cols(du_peer, mlp_w[0]).astype(BF16), t=1)
        dm = contract_cols(du_own, mlp_w[0]) + got.astype(F32)
        midway_back, gain_two, shift_two = jax.vjp(layer_norm, midway, vec[5], vec[6])[1](dm)
        midway_back = midway_back + gradient
        dz = midway_back.astype(BF16)
        do = contract_cols(dz, attn_w[1, :, PADDED : PADDED + width]).astype(BF16)
        do = jnp.pad(do, ((0, 0), (0, PADDED - width)))
        dq, dk, dv = attend_back(do, saved, bias, 2)
        da = contract_cols(jnp.concatenate([dq, dk], 1), attn_w[0]) + contract_cols(
            dv, attn_w[1, :, :PADDED]
        )
        input_back, gain_one, shift_one = jax.vjp(layer_norm, layer_in, vec[0], vec[1])[1](da)
        gradient = midway_back + input_back
        m = jnp.concatenate([m_own, m_peer], 0)
        du = jnp.concatenate([du_own, du_peer], 0)
        dy = jnp.concatenate([dy_own, dy_peer], 0)
        g = jnp.concatenate([g_own, g_peer], 0)
        bias_back = lax.dynamic_update_slice_in_dim(
            jnp.zeros((2 * hidden_half,), F32), jnp.sum(du.astype(F32), 0), at["t"] * hidden_half, 0
        )
        down_rows = lambda v: jnp.sum(v.astype(F32), 0)[:width]
        small = jnp.stack(
            [gain_one, shift_one, down_rows(dq), down_rows(dv), down_rows(dz), gain_two, shift_two, down_rows(dy_own)]
        )
        vec_back = jnp.concatenate([small, bias_back.reshape(-1, width)], 0)
        totals[l] = reduce_layer(
            at, (normed, dq, dk, dv, o, dz, m, du, dy, g, vec_back)
        )
    stacked = [jnp.stack([totals[l][n] for l in range(layers)]) for n in range(5)]
    shape = (micro_count, row_count, width)
    return (result.reshape(shape), gradient.reshape(shape), *stacked)


def solution(mesh):
    return jax.shard_map(
        body,
        mesh=mesh,
        in_specs=(
            P(None, ("dp", "ctx", "tensor"), None),
            P(None, "dp", None),
            P(None, "dp", None),
            P(None, "dp", "tensor"),
            P(None, "dp", "tensor"),
            P(None, None, "dp"),
            P(None, ("dp", "ctx", "tensor")),
            P(None, ("dp", "ctx", "tensor"), None),
        ),
        out_specs=(
            P(None, ("dp", "ctx", "tensor"), None),
            P(None, ("dp", "ctx", "tensor"), None),
            P(None, "dp", None),
            P(None, "dp", None),
            P(None, "dp", "tensor"),
            P(None, "dp", "tensor"),
            P(None, None, "dp"),
        ),
        check_vma=False,
    )
```

```python
import functools

import jax
import jax.numpy as jnp
from jax import lax
from jax.experimental import pallas as pl
from jax.experimental.pallas import tpu as pltpu
from jax.sharding import PartitionSpec as P

EPSILON = 1e-05
MASKED = -1e30
MESH = pl.DeviceIdType.MESH
F32 = jnp.float32
BF16 = jnp.bfloat16
GROUP = 8
SLOTS = 5
HEAD = 64
WINDOW = 384
STRIDE = 256
PADDED = 1152
CHUNK = 128


def places():
    dp = lax.axis_index("dp")
    return {
        "x": dp // 4,
        "y": (dp // 2) % 2,
        "c": dp % 2,
        "z": lax.axis_index("ctx"),
        "t": lax.axis_index("tensor"),
    }


def shifted(value, x=0, y=0, c=0, z=0, t=0):
    pairs = []
    for i in range(128):
        ix, iy, ic, iz, it = i // 32, (i // 16) % 2, (i // 8) % 2, (i // 2) % 4, i % 2
        ix, iy, ic, iz, it = (ix + x) % 4, (iy + y) % 2, (ic + c) % 2, (iz + z) % 4, (it + t) % 2
        pairs.append((i, (((ix * 2 + iy) * 2 + ic) * 4 + iz) * 2 + it))
    return lax.ppermute(value, ("dp", "ctx", "tensor"), pairs)


ROWS = 68
TALL = 80
BLOCK = 272
NEAR = 144
Q_COLS = 512
T_START = 2048
T_COLS = 256
M_COLS = 2176


def peer_at(x=0, y=0, c=0, z=0, t=0):
    at = places()
    dp = (lax.rem(at["x"] + x + 4, 4) * 2 + lax.rem(at["y"] + y, 2)) * 2 + lax.rem(at["c"] + c, 2)
    return (dp, lax.rem(at["z"] + z + 4, 4), lax.rem(at["t"] + t, 2))


class Copies:
    def __init__(self, send_sem, recv_sem):
        self.send_sem, self.recv_sem = send_sem, recv_sem
        self.count = 0
        self.open = []

    def to(self, peer, src, dst):
        n = self.count
        self.count += 1
        copy = pltpu.make_async_remote_copy(
            src_ref=src,
            dst_ref=dst,
            send_sem=self.send_sem.at[n],
            recv_sem=self.recv_sem.at[n],
            device_id=peer,
            device_id_type=MESH,
        )
        copy.start()
        self.open.append(copy.wait_send)
        return copy.wait_recv

    def here(self, src, dst):
        n = self.count
        self.count += 1
        copy = pltpu.make_async_copy(src, dst, self.send_sem.at[n])
        copy.start()
        return copy.wait

    def close(self):
        for wait in self.open:
            wait()
        self.open = []


def rows_at(block, count=BLOCK, skip=0):
    return pl.ds(pl.multiple_of(block * BLOCK + skip, 16), count)


class RingX:
    def __init__(self, copies, own, buf, lanes, share):
        self.copies, self.own, self.buf, self.lanes, self.share = copies, own, buf, lanes, share
        at = places()
        self.c, self.x = at["c"], at["x"]
        self.last = []

    def view(self, distance, count=BLOCK, skip=0):
        block = lax.rem(self.x + distance + 4, 4)
        return self.buf.at[self.c, rows_at(block, count, skip), self.lanes]

    def sibling(self, src, dst):
        if self.share:
            self.last.append(self.copies.to(peer_at(c=1), src, dst))

    def start(self):
        self.from_below = self.copies.to(peer_at(x=1), self.own, self.view(0))
        self.from_above = self.copies.to(peer_at(x=-1), self.own, self.view(0))
        self.last.append(self.copies.here(self.own, self.view(0)))
        self.sibling(self.own, self.view(0))

    def forward(self):
        self.from_below()
        part = self.view(-1, NEAR)
        far_a = self.copies.to(peer_at(x=1), part, part)
        self.from_above()
        part = self.view(1, BLOCK - NEAR, NEAR)
        far_b = self.copies.to(peer_at(x=-1), part, part)
        self.far = (far_a, far_b)
        self.sibling(self.view(-1), self.view(-1))
        self.sibling(self.view(1), self.view(1))

    def finish(self):
        for wait in self.far:
            wait()
        self.sibling(self.view(2), self.view(2))

    def close(self):
        for wait in self.last:
            wait()


class RingZ:
    def __init__(self, copies, buf):
        self.copies, self.buf = copies, buf
        at = places()
        self.c, self.z = at["c"], at["z"]
        self.last = []

    def view(self, distance, rows=slice(None)):
        block = lax.rem(self.z + distance + 4, 4)
        return self.buf.at[self.c, rows, pl.ds(pl.multiple_of(block * Q_COLS, 128), Q_COLS)]

    def sibling(self, src):
        self.last.append(self.copies.to(peer_at(c=1), src, src))

    def start(self):
        own = self.view(0)
        self.from_below = self.copies.to(peer_at(z=1), own, own)
        self.from_above = self.copies.to(peer_at(z=-1), own, own)
        self.sibling(own)

    def forward(self):
        self.from_below()
        part = self.view(-1, pl.ds(0, 544))
        far_a = self.copies.to(peer_at(z=1), part, part)
        self.from_above()
        part = self.view(1, pl.ds(544, 544))
        far_b = self.copies.to(peer_at(z=-1), part, part)
        self.far = (far_a, far_b)
        self.sibling(self.view(-1))
        self.sibling(self.view(1))

    def finish(self):
        for wait in self.far:
            wait()
        self.sibling(self.view(2))

    def close(self):
        for wait in self.last:
            wait()


def exchange_shards(copies, mine, landed):
    c = places()["c"]
    waits = [
        copies.to(peer_at(c=1), mine.at[1 - c], landed.at[1]),
        copies.to(peer_at(y=1), mine.at[c], landed.at[2]),
        copies.to(peer_at(y=1, c=1), mine.at[1 - c], landed.at[3]),
    ]
    waits.append(copies.here(mine.at[c], landed.at[0]))
    return waits


def assemble(landed, own):
    at = places()
    width = own.shape[1]
    for start in range(0, width, 256):
        lanes = slice(start, min(start + 256, width))
        parts = []
        for j in range(4):
            slot = lax.rem(j // 2 + at["y"], 2) * 2 + lax.rem(j % 2 + at["c"], 2)
            parts.append(landed[slot, :, lanes].astype(F32)[:ROWS])
        own[:, lanes] = jnp.concatenate(parts, 0).astype(BF16)


def gather_kernel(
    q0, mt0, q1, mt1, docs, attn, mlp, vec_tail, q_next, mt_next, docs_all,
    q_land, mt_land, q_own, mt_own, q_own1, mt_own1, send_sem, recv_sem,
):
    me = group_place()
    greet([dict(c=1), dict(y=1), dict(y=1, c=1), dict(x=1), dict(x=-1)], me)
    copies = Copies(send_sem, recv_sem)
    quarter = pl.ds(pl.multiple_of(places()["z"] * Q_COLS, 128), Q_COLS)
    arrive_q = exchange_shards(copies, q0, q_land.at[0])
    arrive_mt = exchange_shards(copies, mt0, mt_land.at[0])
    later = [copies.here(docs, docs_all.at[me])]
    for n in range(1, GROUP):
        later.append(copies.to(member(lax.rem(me + n, GROUP)), docs, docs_all.at[me]))
    arrive_q1 = exchange_shards(copies, q1, q_land.at[1])
    arrive_mt1 = exchange_shards(copies, mt1, mt_land.at[1])
    q = RingX(copies, q_own, attn, quarter, False)
    m = RingX(copies, mt_own.at[:, pl.ds(0, M_COLS)], mlp, slice(None), True)
    t = RingX(copies, mt_own.at[:, pl.ds(M_COLS, T_COLS)], attn, pl.ds(T_START, T_COLS), True)
    along_z = RingZ(copies, attn)

    def landed(waits, land, own):
        for wait in waits:
            wait()
        assemble(land, own)

    landed(arrive_q, q_land.at[0], q_own)
    q.start()
    q.forward()
    landed(arrive_mt, mt_land.at[0], mt_own)
    t.start()
    m.start()
    q.finish()
    q.close()
    along_z.start()
    t.forward()
    landed(arrive_q1, q_land.at[1], q_own1)
    later.append(copies.here(q_own1, q_next))
    m.forward()
    along_z.forward()
    landed(arrive_mt1, mt_land.at[1], mt_own1)
    later.append(copies.here(mt_own1, mt_next))
    t.finish()
    m.finish()
    along_z.finish()
    for ring in (t, m, along_z):
        ring.close()
    later.append(copies.here(attn.at[0, :, pl.ds(PADDED - 128, 128)], vec_tail))
    for wait in later:
        wait()
    copies.close()


def shard_rows(qkv, out, up, down, vec, z):
    width = out.shape[1]
    role0 = jnp.concatenate([padded(qkv[:, :width], vec.T), padded(qkv[:, width : 2 * width])], 1)
    role1 = jnp.concatenate([padded(qkv[:, 2 * width :]), padded(out)], 1)
    attn = jnp.pad(jnp.stack([role0, role1]), ((0, 0), (0, TALL - ROWS), (0, 0)))
    mlp = jnp.pad(jnp.stack([up, down]), ((0, 0), (0, TALL - ROWS), (0, 0)))
    quarter = lax.dynamic_slice_in_dim(attn, z * Q_COLS, Q_COLS, 2)
    return quarter, jnp.concatenate([mlp, attn[:, :, T_START:]], 2)


def gather_first(shards, docs, collective):
    hbm = pl.BlockSpec(memory_space=pl.ANY)
    shape = jax.ShapeDtypeStruct
    (q0, mt0), (q1, mt1) = shards
    low = lambda *dims: pltpu.VMEM(dims, BF16)
    return pl.pallas_call(
        gather_kernel,
        out_shape=[
            shape((2, 4 * BLOCK, 2 * PADDED), BF16),
            shape((2, 4 * BLOCK, M_COLS), BF16),
            shape((4 * BLOCK, 128), BF16),
            shape((BLOCK, Q_COLS), BF16),
            shape((BLOCK, M_COLS + T_COLS), BF16),
            shape((GROUP, *docs.shape), docs.dtype),
        ],
        in_specs=[hbm] * 5,
        out_specs=[hbm] * 6,
        scratch_shapes=[
            low(2, 4, TALL, Q_COLS),
            low(2, 4, TALL, M_COLS + T_COLS),
            low(BLOCK, Q_COLS),
            low(BLOCK, M_COLS + T_COLS),
            low(BLOCK, Q_COLS),
            low(BLOCK, M_COLS + T_COLS),
            pltpu.SemaphoreType.DMA((64,)),
            pltpu.SemaphoreType.DMA((64,)),
        ],
        compiler_params=pltpu.CompilerParams(
            collective_id=collective, has_side_effects=True, vmem_limit_bytes=32 * 2**20
        ),
    )(q0, mt0, q1, mt1, docs)


def padded(matrix, extra=None):
    rows, width = matrix.shape
    parts = [matrix]
    if extra is not None:
        parts.append(extra)
        width += extra.shape[1]
    parts.append(jnp.zeros((rows, PADDED - width), matrix.dtype))
    return jnp.concatenate(parts, 1)


PIECE = 640
HALF = 136
HALF_TALL = 144


def attn_start(z):
    return z * 13 // 3 * 128


def mlp_start(z):
    return z * 512


def contract_rows(a, b):
    return lax.dot_general(a, b, (((0,), (0,)), ((), ())), preferred_element_type=F32)


def contract_cols(a, b):
    return lax.dot_general(a, b, (((1,), (1,)), ((), ())), preferred_element_type=F32)


def block_diagonal(a, b):
    zero = jnp.zeros_like(a)
    return jnp.concatenate(
        [jnp.concatenate([a, zero], 1), jnp.concatenate([zero, b], 1)], 0
    )


def chip_sums(at, operands):
    a, dq, dk, dv, o, dz, m, du, dy, g, vec = operands
    c0 = at["c"] == 0
    width = a.shape[1]
    pick = lambda p, q: jnp.where(c0, p, q)
    vec_cols = jnp.pad(vec.T, ((0, 0), (width, 2 * PADDED - width - vec.shape[0])))
    give = contract_rows(
        jnp.concatenate([a, pick(o, a)], 0), block_diagonal(pick(dv, dq), pick(dz, dk))
    ) + pick(0.0, 1.0) * vec_cols
    got = shifted(give.astype(BF16), c=1)
    keep = contract_rows(
        jnp.concatenate([a, pick(a, o)], 0), block_diagonal(pick(dq, dv), pick(dk, dz))
    ) + pick(1.0, 0.0) * vec_cols
    attn = (keep + got.astype(F32)).astype(BF16)
    give = contract_rows(pick(dy, m), pick(g, du)).astype(BF16)
    got = shifted(give, c=1)
    mlp = (contract_rows(pick(m, dy), pick(du, g)) + got.astype(F32)).astype(BF16)
    return attn, mlp


def in_chunks(count, step, do):
    def one(i, carry):
        do(pl.ds(pl.multiple_of(i * step, 16), step))
        return carry

    lax.fori_loop(0, count // step, one, 0)


class RingSum:
    def __init__(self, copies, axis, view, rows, near, via, step, stage=None):
        self.copies, self.axis, self.view, self.rows = copies, axis, view, rows
        self.near, self.via, self.step, self.stage = near, via, step, stage
        cut = via.shape[1]
        self.first, self.last = pl.ds(0, cut), pl.ds(cut, rows - cut)
        self.counts = (cut, rows - cut)
        self.up, self.down = peer_at(**{axis: 1}), peer_at(**{axis: -1})

    def start(self):
        first, last = self.first, self.last
        far, up, down = self.view(2), self.view(1), self.view(-1)
        rest = pl.ds(0, self.counts[1])
        self.via_up = self.copies.to(self.up, far.at[first], self.via.at[0])
        self.via_down = self.copies.to(self.down, far.at[last], self.via.at[1, rest])
        self.near_a = self.copies.to(self.up, up.at[last], self.near.at[0, last])
        self.near_b = self.copies.to(self.down, down.at[first], self.near.at[1, first])
        self.parts = (up.at[first], down.at[last])
        self.staged = []
        if self.stage is not None:
            staged = (self.stage.at[0], self.stage.at[1, rest])
            for src, dst in zip(self.parts, staged):
                self.staged.append(self.copies.here(src, dst))
            self.parts = staged

    def forward(self):
        for wait in self.staged:
            wait()
        arrived = (self.via_up, self.via_down)
        ends = ((self.up, 0, self.first), (self.down, 1, self.last))
        self.nears = [self.near_a, self.near_b]
        for n, (peer, side, rows) in enumerate(ends):
            arrived[n]()
            part = self.parts[n]

            def add(r):
                self.via[n, r, :] = (part[r, :].astype(F32) + self.via[n, r, :].astype(F32)).astype(BF16)

            in_chunks(self.counts[n], self.step, add)
            src = self.via.at[n, pl.ds(0, self.counts[n])]
            self.nears.append(self.copies.to(peer, src, self.near.at[side, rows]))

    def land(self):
        for wait in self.nears:
            wait()


def add_near(own, near, rows, step, write):
    def add(r):
        write(r, own[r, :].astype(F32) + near[0, r, :].astype(F32) + near[1, r, :].astype(F32))

    in_chunks(rows, step, add)


def turn(value, distance):
    return lax.rem(value + distance + 4, 4)


def columns_of(array, start_of, z):
    return array.at[:, pl.ds(pl.multiple_of(start_of(z), 128), PIECE)]


def attn_ring(copies, array, near, via, stage):
    view = lambda d: columns_of(array, attn_start, turn(places()["z"], d))
    return RingSum(copies, "z", view, 4 * BLOCK, near, via, 32, stage)


def mlp_ring(copies, array, near, via, stage):
    view = lambda d: array.at[rows_at(turn(places()["x"], d))]
    return RingSum(copies, "x", view, BLOCK, near, via, 16, stage)


def reduce_kernel(
    attn0, mlp0, attn1, mlp1, attn_near1, mlp_near1, out,
    attn_near, attn_via, attn_stage, mlp_near, mlp_via, mlp_stage, attn_own, mlp_own,
    attn_part, mlp_part, near2, via2, halves, got, owned, owned_got, send_sem, recv_sem,
):
    barrier = pltpu.get_barrier_semaphore()
    peers = [dict(c=1), dict(x=1), dict(x=-1), dict(y=1, t=1), dict(y=1), dict(t=1)]
    peers += [dict(z=1), dict(z=2), dict(z=3)]
    for peer in peers:
        pl.semaphore_signal(barrier, inc=1, device_id=peer_at(**peer), device_id_type=MESH)
    pl.semaphore_wait(barrier, len(peers))
    copies = Copies(send_sem, recv_sem)
    at = places()
    ring_a = attn_ring(copies, attn0, attn_near, attn_via, attn_stage)
    ring_m = mlp_ring(copies, mlp0, mlp_near, mlp_via, mlp_stage)
    ring_a.start()
    ring_m.start()
    loads = {}
    for l, (attn, mlp) in ((1, (attn1, mlp1)), (0, (attn0, mlp0))):
        loads[l] = (
            copies.here(columns_of(attn, attn_start, at["z"]), attn_own.at[l]),
            copies.here(mlp.at[rows_at(at["x"])], mlp_own.at[l]),
        )

    def second(l, near_a, near_m):
        def write_attn(r, value):
            attn_part[l, r, :] = value.astype(BF16)

        def write_mlp(r, value):
            mlp_part[l, r, :] = value.astype(BF16)

        for wait in loads[l]:
            wait()
        add_near(mlp_own.at[l], near_m, BLOCK, 16, write_mlp)
        m2 = RingSum(
            copies, "z", lambda d: columns_of(mlp_part.at[l], mlp_start, turn(at["z"], d)),
            BLOCK, near2.at[l, 1], via2.at[l, 1], 16,
        )
        m2.start()
        add_near(attn_own.at[l], near_a, 4 * BLOCK, 32, write_attn)
        a2 = RingSum(
            copies, "x", lambda d: attn_part.at[l, rows_at(turn(at["x"], d))],
            BLOCK, near2.at[l, 0], via2.at[l, 0], 16,
        )
        a2.start()
        return a2, m2

    def third(l, rings):
        waits = []
        for n, ring in enumerate(rings):
            ring.land()
            own = ring.view(0)
            total = (
                own[...].astype(F32) + ring.near[0].astype(F32) + ring.near[1].astype(F32)
            )
            halves[l, n, 0, :HALF] = total[:HALF].astype(BF16)
            halves[l, n, 1, :HALF] = total[HALF:].astype(BF16)
            halves[l, n, 0, HALF:] = jnp.zeros((HALF_TALL - HALF, PIECE), BF16)
            halves[l, n, 1, HALF:] = jnp.zeros((HALF_TALL - HALF, PIECE), BF16)
            peer = peer_at(y=1, t=1) if n == 0 else peer_at(y=1)
            waits.append(copies.to(peer, halves.at[l, n, 1 - at["y"]], got.at[l, n]))
        return waits

    def fourth(l, waits):
        waits[0]()
        mine = halves[l, 0, at["y"]].astype(F32) + got[l, 0].astype(F32)
        halves[l, 0, at["y"]] = mine.astype(BF16)
        return copies.to(peer_at(t=1), halves.at[l, 0, at["y"]], got.at[l, 2])

    def fifth(l, waits, wait):
        waits[1]()
        wait()
        ends = []
        for n, landed in ((0, 2), (1, 1)):
            total = halves[l, n, at["y"]].astype(F32) + got[l, landed].astype(F32)
            for core in range(2):
                owned[l, n, core, :ROWS] = total[core * ROWS : core * ROWS + ROWS].astype(BF16)
                owned[l, n, core, ROWS:] = jnp.zeros((TALL - ROWS, PIECE), BF16)
            ends.append(copies.to(peer_at(c=1), owned.at[l, n, 1 - at["c"]], owned_got.at[l, n]))
        return ends

    def sixth(l, ends):
        for wait in ends:
            wait()
        rest = []
        for n in range(2):
            for role, src in ((at["c"], owned.at[l, n, at["c"]]), (1 - at["c"], owned_got.at[l, n])):
                dst = out.at[l, at["z"], n, role]
                rest.append(copies.here(src, dst))
                for d in (1, 2, 3):
                    rest.append(copies.to(peer_at(z=d), src, dst))
        return rest

    rings, waits, rest = {}, {}, []
    rings[1] = second(1, attn_near1, mlp_near1)
    ring_m.forward()
    ring_a.forward()
    for ring in reversed(rings[1]):
        ring.forward()
    waits[1] = third(1, rings[1])
    turned = fourth(1, waits[1])
    rest += sixth(1, fifth(1, waits[1], turned))
    ring_m.land()
    ring_a.land()
    rings[0] = second(0, attn_near, mlp_near)
    for ring in reversed(rings[0]):
        ring.forward()
    waits[0] = third(0, rings[0])
    turned = fourth(0, waits[0])
    rest += sixth(0, fifth(0, waits[0], turned))
    for wait in rest:
        wait()
    copies.close()


def reduce_layers(sums, near, collective):
    hbm = pl.BlockSpec(memory_space=pl.ANY)
    vmem = pl.BlockSpec(memory_space=pltpu.VMEM)
    low = lambda *dims: pltpu.VMEM(dims, BF16)
    return pl.pallas_call(
        reduce_kernel,
        out_shape=jax.ShapeDtypeStruct((2, 4, 2, 2, TALL, PIECE), BF16),
        in_specs=[hbm] * 4 + [vmem] * 2,
        out_specs=hbm,
        scratch_shapes=[
            low(2, 4 * BLOCK, PIECE),
            low(2, 2 * BLOCK, PIECE),
            low(2, 2 * BLOCK, PIECE),
            low(2, BLOCK, M_COLS),
            low(2, NEAR, M_COLS),
            low(2, NEAR, M_COLS),
            low(2, 4 * BLOCK, PIECE),
            low(2, BLOCK, M_COLS),
            low(2, 4 * BLOCK, PIECE),
            low(2, BLOCK, M_COLS),
            low(2, 2, 2, BLOCK, PIECE),
            low(2, 2, 2, NEAR, PIECE),
            low(2, 2, 2, HALF_TALL, PIECE),
            low(2, 3, HALF_TALL, PIECE),
            low(2, 2, 2, TALL, PIECE),
            low(2, 2, TALL, PIECE),
            pltpu.SemaphoreType.DMA((96,)),
            pltpu.SemaphoreType.DMA((96,)),
        ],
        compiler_params=pltpu.CompilerParams(
            collective_id=collective, has_side_effects=True, vmem_limit_bytes=56 * 2**20
        ),
    )(*sums[0], *sums[1], *near)


def owned_gradients(parts, width):
    parts = parts[:, :, :, :ROWS]

    def joined(n, role, widths):
        return jnp.concatenate([parts[z, n, role, :, :w] for z, w in enumerate(widths)], 1)

    attn = [joined(0, role, (512, 512, 640, 640)) for role in range(2)]
    up, down = (joined(1, role, (512, 512, 512, 640)) for role in range(2))
    qk, vo = attn
    in_back = jnp.concatenate([qk[:, :width], qk[:, PADDED : PADDED + width], vo[:, :width]], 1)
    vec_back = qk[:, width : width + 12].T
    results = (in_back, vo[:, PADDED : PADDED + width], up, down, vec_back)
    return tuple(value.astype(F32) for value in results)


def group_place():
    return lax.axis_index("ctx") * 2 + lax.axis_index("tensor")


def member(index):
    return (lax.axis_index("dp"), index // 2, lax.rem(index, 2))


def meet(me):
    barrier = pltpu.get_barrier_semaphore()
    for k in range(1, GROUP):
        pl.semaphore_signal(
            barrier, inc=1, device_id=member(lax.rem(me + k, GROUP)), device_id_type=MESH
        )
    pl.semaphore_wait(barrier, GROUP - 1)


def to_heads(me, sources, landed, local_sem, send_sem, recv_sem):
    copies = []
    for k in range(1, GROUP):
        peer = lax.rem(me + k, GROUP)
        rows = pl.ds(pl.multiple_of(peer // 4 * 64, 64), 64)
        lanes = pl.ds(pl.multiple_of(lax.rem(peer, 4) * STRIDE, 128), WINDOW)
        for n, (src, dst) in enumerate(zip(sources, landed)):
            copy = pltpu.make_async_remote_copy(
                src_ref=src.at[rows, lanes],
                dst_ref=dst.at[pl.ds(pl.multiple_of(me * 64, 64), 64)],
                send_sem=send_sem.at[n, k],
                recv_sem=recv_sem.at[n, k],
                device_id=member(peer),
                device_id_type=MESH,
            )
            copy.start()
            copies.append(copy)
    rows = pl.ds(pl.multiple_of(me // 4 * 64, 64), 64)
    lanes = pl.ds(pl.multiple_of(lax.rem(me, 4) * STRIDE, 128), WINDOW)
    for n, (src, dst) in enumerate(zip(sources, landed)):
        copy = pltpu.make_async_copy(
            src.at[rows, lanes], dst.at[pl.ds(pl.multiple_of(me * 64, 64), 64)], local_sem.at[n]
        )
        copy.start()
        copies.append(copy)
    return copies


def to_rows(me, sources, landed, local_sem, send_sem, recv_sem):
    copies = []
    for k in range(1, GROUP):
        peer = lax.rem(me + k, GROUP)
        for n, (src, dst) in enumerate(zip(sources, landed)):
            copy = pltpu.make_async_remote_copy(
                src_ref=src.at[pl.ds(pl.multiple_of(peer * 64, 64), 64)],
                dst_ref=dst.at[me],
                send_sem=send_sem.at[n, k],
                recv_sem=recv_sem.at[n, k],
                device_id=member(peer),
                device_id_type=MESH,
            )
            copy.start()
            copies.append(copy)
    for n, (src, dst) in enumerate(zip(sources, landed)):
        copy = pltpu.make_async_copy(
            src.at[pl.ds(pl.multiple_of(me * 64, 64), 64)], dst.at[me], local_sem.at[n]
        )
        copy.start()
        copies.append(copy)
    return copies


def side_by_side(landed, out):
    for micro in range(2):
        rows = slice(micro * 64, micro * 64 + 64)
        for group in range(4):
            width = WINDOW if group == 3 else STRIDE
            out[rows, group * STRIDE : group * STRIDE + width] = landed[micro * 4 + group, :, :width]


def matmul(a, b, dims):
    return lax.dot_general(a, b, ((dims[:1], dims[1:]), ((), ())), preferred_element_type=F32)


def score_bias(docs):
    docs = lax.dynamic_index_in_dim(docs, lax.axis_index("ctx") // 2, 1, keepdims=False)
    docs = docs[:, :64].reshape(-1)
    place = jnp.arange(docs.shape[0], dtype=jnp.int32)
    allowed = (docs[:, None] == docs[None, :]) & (place[None, :] <= place[:, None])
    return jnp.where(allowed, 0.0, MASKED).astype(F32)


def tiles_of(width, step):
    return [(start, min(start + step, width)) for start in range(0, width, step)]


def normalise(inputs):
    centred = inputs - jnp.mean(inputs, 1, keepdims=True)
    spread = jnp.mean(centred * centred, 1, keepdims=True)
    scale = lax.rsqrt(spread + EPSILON)
    return centred * scale, scale


def gelu_and_slope(u):
    share = 0.5 * (1.0 + lax.erf(u * 0.7071067811865476))
    return u * share, share + u * jnp.exp(-0.5 * u * u) * 0.3989422804014327


def greet(peers, me):
    barrier = pltpu.get_barrier_semaphore()
    members = [member(lax.rem(me + k, GROUP)) for k in range(1, GROUP)]
    for peer in members + [peer_at(**peer) for peer in peers]:
        pl.semaphore_signal(barrier, inc=1, device_id=peer, device_id_type=MESH)
    pl.semaphore_wait(barrier, len(members) + len(peers))


def forward_kernel(*refs, carry):
    resid, vec, bias_up, mask, attn_in, mlp_in = refs[:6]
    refs = refs[6:]
    if carry:
        q_own, mt_own = refs[:2]
        refs = refs[2:]
    (
        resid_out, normed, q_all, k_all, v_all, o_all, log_total, o_out, midway, m_out, g_out, d_out,
    ) = refs[:12]
    refs = refs[12:]
    if carry:
        next_attn, next_mlp, next_tail = refs[:3]
        refs = refs[3:]
    (
        attn, mlp, q, k, v, o_low, o_landed, part, part_got, load_sem, local_sem, send_sem, recv_sem,
    ) = refs[:13]
    me = group_place()
    greet([dict(c=1), dict(x=1), dict(x=-1)] if carry else [], me)
    loads = []
    for n, (src, dst) in enumerate(
        [(attn_in.at[0], attn.at[0]), (attn_in.at[1], attn.at[1]), (mlp_in.at[0], mlp.at[0]), (mlp_in.at[1], mlp.at[1])]
    ):
        copy = pltpu.make_async_copy(src, dst, load_sem.at[n])
        copy.start()
        loads.append(copy.wait)
    if carry:
        copies = Copies(*refs[13:15])
        quarter = pl.ds(pl.multiple_of(places()["z"] * Q_COLS, 128), Q_COLS)
        ring_q = RingX(copies, q_own, next_attn, quarter, False)
        ring_m = RingX(copies, mt_own.at[:, pl.ds(0, M_COLS)], next_mlp, slice(None), True)
        ring_t = RingX(copies, mt_own.at[:, pl.ds(M_COLS, T_COLS)], next_attn, pl.ds(T_START, T_COLS), True)
        ring_z = RingZ(copies, next_attn)
        ring_q.start()
    row = lambda n: vec[n : n + 1, :]
    width = resid.shape[1]
    x, _ = normalise(resid[...])
    a = (x * row(0)[:, :width] + row(1)[:, :width]).astype(BF16)
    normed[...] = a
    loads[0]()
    for start, stop in tiles_of(PADDED, 384):
        lanes = slice(start, stop)
        q[:, lanes] = (matmul(a, attn[0, :, lanes], (1, 0)) + vec[2:3, lanes]).astype(BF16)
        k[:, lanes] = matmul(a, attn[0, :, PADDED + start : PADDED + stop], (1, 0)).astype(BF16)
    loads[1]()
    for start, stop in tiles_of(PADDED, 384):
        lanes = slice(start, stop)
        v[:, lanes] = (matmul(a, attn[1, :, lanes], (1, 0)) + vec[3:4, lanes]).astype(BF16)
    exchanged = to_heads(me, (q, k, v), (q_all, k_all, v_all), local_sem, send_sem, recv_sem)
    o_low[...] = jnp.zeros_like(o_low)
    o_all[...] = jnp.zeros_like(o_all)
    log_total[...] = jnp.zeros_like(log_total)
    if carry:
        ring_q.forward()
        ring_t.start()
        ring_m.start()
    for copy in exchanged:
        copy.wait()
    if carry:
        ring_q.finish()
        ring_q.close()
        ring_z.start()
    for head in range(SLOTS):
        lanes = slice(head * HEAD, head * HEAD + HEAD)
        keys, values = k_all[:, lanes], v_all[:, lanes]
        for start in range(0, 512, CHUNK):
            rows, reach = slice(start, start + CHUNK), start + CHUNK
            queries = q_all[rows, lanes] * 0.125
            scores = matmul(queries, keys[:reach], (1, 1)) + mask[rows, :reach]
            top = jnp.max(scores, 1, keepdims=True)
            weights = jnp.exp(scores - top)
            total = jnp.sum(weights, 1, keepdims=True)
            result = matmul(weights.astype(BF16), values[:reach], (1, 0)) / total
            o_all[rows, lanes] = result
            o_low[rows, lanes] = result.astype(BF16)
            log_total[rows, head : head + 1] = top + jnp.log(total)
    exchanged = to_rows(
        me, (o_low,), (o_landed,), local_sem.at[3:4], send_sem.at[3:4], recv_sem.at[3:4]
    )
    if carry:
        ring_t.forward()
        ring_m.forward()
    for copy in exchanged:
        copy.wait()
    if carry:
        ring_z.forward()
    side_by_side(o_landed, o_out)
    o = o_out[:, :width]
    for start, stop in tiles_of(width, 384):
        lanes = slice(start, stop)
        midway[:, lanes] = (
            resid[:, lanes]
            + matmul(o, attn[1, :, PADDED + start : PADDED + stop], (1, 0))
            + vec[4:5, lanes]
        )
    x, _ = normalise(midway[...])
    m_out[0] = (x * row(5)[:, :width] + row(6)[:, :width]).astype(BF16)

    def to_pair(src, dst, n):
        copy = pltpu.make_async_remote_copy(
            src_ref=src,
            dst_ref=dst,
            send_sem=send_sem.at[4, n],
            recv_sem=recv_sem.at[4, n],
            device_id=peer_at(t=1),
            device_id_type=MESH,
        )
        copy.start()
        return copy

    rows_sent = to_pair(m_out.at[0], m_out.at[1], 0)
    loads[2]()

    def up(side):
        for start, stop in tiles_of(M_COLS, 256):
            lanes = slice(start, stop)
            u = matmul(m_out[side], mlp[0, :, lanes], (1, 0)) + bias_up[0:1, lanes]
            g, d = gelu_and_slope(u)
            g_out[side, :, lanes] = g.astype(BF16)
            d_out[side, :, lanes] = d.astype(BF16)

    up(0)
    rows_sent.wait()
    up(1)
    loads[3]()
    for start, stop in tiles_of(width, 256):
        part[:, start:stop] = matmul(g_out[1], mlp[1, start:stop, :], (1, 1)).astype(BF16)
    part_sent = to_pair(part, part_got, 1)
    for start, stop in tiles_of(width, 256):
        resid_out[:, start:stop] = matmul(g_out[0], mlp[1, start:stop, :], (1, 1))
    part_sent.wait()
    resid_out[...] += midway[...] + part_got[...].astype(F32) + row(7)[:, :width]
    if carry:
        ring_t.finish()
        ring_z.finish()
        ring_m.finish()
        for ring in (ring_t, ring_z, ring_m):
            ring.close()
        copies.here(next_attn.at[0, :, pl.ds(PADDED - 128, 128)], next_tail)()
        copies.close()


def forward_layer(resid, vec, bias_up, mask, weights, pieces, collective):
    shape = jax.ShapeDtypeStruct
    vmem = pl.BlockSpec(memory_space=pltpu.VMEM)
    hbm = pl.BlockSpec(memory_space=pl.ANY)
    rows, width = resid.shape
    carry = pieces is not None
    low = lambda *dims: pltpu.VMEM(dims, BF16)
    out_shape = [
        shape((rows, width), F32),
        shape((rows, width), BF16),
        shape((512, WINDOW), BF16),
        shape((512, WINDOW), BF16),
        shape((512, WINDOW), BF16),
        shape((512, WINDOW), F32),
        shape((512, 128), F32),
        shape((rows, PADDED), BF16),
        shape((rows, width), F32),
        shape((2, rows, width), BF16),
        shape((2, rows, M_COLS), BF16),
        shape((2, rows, M_COLS), BF16),
    ]
    scratch = [
        low(2, 4 * BLOCK, 2 * PADDED),
        low(2, 4 * BLOCK, M_COLS),
        low(rows, PADDED),
        low(rows, PADDED),
        low(rows, PADDED),
        low(512, WINDOW),
        low(GROUP, 64, WINDOW),
        low(rows, width),
        low(rows, width),
        pltpu.SemaphoreType.DMA((4,)),
        pltpu.SemaphoreType.DMA((4,)),
        pltpu.SemaphoreType.DMA((5, GROUP)),
        pltpu.SemaphoreType.DMA((5, GROUP)),
    ]
    if carry:
        out_shape += [shape(w.shape, w.dtype) for w in weights]
        out_shape += [shape((4 * BLOCK, 128), BF16)]
        scratch += [pltpu.SemaphoreType.DMA((40,))] * 2
    results = pl.pallas_call(
        functools.partial(forward_kernel, carry=carry),
        out_shape=out_shape,
        in_specs=[vmem] * 4 + [hbm] * (4 if carry else 2),
        out_specs=[vmem] * 12 + [hbm] * (3 if carry else 0),
        scratch_shapes=scratch,
        compiler_params=pltpu.CompilerParams(
            collective_id=collective, has_side_effects=True, vmem_limit_bytes=56 * 2**20
        ),
    )(resid, vec, bias_up, mask, *weights, *(pieces or ()))
    return results[:12], tuple(results[12:])


def norm_back(inputs, gain, back):
    x, scale = normalise(inputs)
    e = back * gain
    grad = scale * (
        e - jnp.mean(e, 1, keepdims=True) - x * jnp.mean(e * x, 1, keepdims=True)
    )
    return grad, jnp.sum(back * x, 0, keepdims=True), jnp.sum(back, 0, keepdims=True)


def backward_kernel(*refs, carry):
    (
        grad, vec, mask, layer_in, midway, d_in, q_all, k_all, v_all, o_all, log_total, attn_in, mlp_in,
    ) = refs[:13]
    refs = refs[13:]
    if carry:
        attn_sum, mlp_sum = refs[:2]
        refs = refs[2:]
    grad_out, dy, du, dz, dq, dk, dv, small, bias_back = refs[:9]
    refs = refs[9:]
    if carry:
        attn_near, mlp_near = refs[:2]
        refs = refs[2:]
    (
        attn, mlp, part, part_got, through, do, do_all, dq_low, dk_low, dv_low, dq_landed, dk_landed, dv_landed,
        dk_sum, dv_sum, load_sem, local_sem, send_sem, recv_sem,
    ) = refs[:19]
    me = group_place()
    greet([dict(x=1), dict(x=-1)] if carry else [], me)
    width = grad.shape[1]
    dy[0] = grad[...].astype(BF16)

    def to_pair(src, dst, n):
        copy = pltpu.make_async_remote_copy(
            src_ref=src,
            dst_ref=dst,
            send_sem=send_sem.at[4, n],
            recv_sem=recv_sem.at[4, n],
            device_id=peer_at(t=1),
            device_id_type=MESH,
        )
        copy.start()
        return copy

    rows_sent = to_pair(dy.at[0], dy.at[1], 0)
    loads = []
    for n, (src, dst) in enumerate(
        [(mlp_in.at[1], mlp.at[1]), (mlp_in.at[0], mlp.at[0]), (attn_in.at[1], attn.at[1]), (attn_in.at[0], attn.at[0])]
    ):
        copy = pltpu.make_async_copy(src, dst, load_sem.at[n])
        copy.start()
        loads.append(copy.wait)
    if carry:
        attn_via, attn_stage, mlp_via, mlp_stage = refs[19:23]
        copies = Copies(*refs[23:25])
        ring_a = attn_ring(copies, attn_sum, attn_near, attn_via, attn_stage)
        ring_m = mlp_ring(copies, mlp_sum, mlp_near, mlp_via, mlp_stage)
        ring_a.start()
        ring_m.start()
    loads[0]()

    def hidden_back(side):
        for start, stop in tiles_of(M_COLS, 256):
            lanes = slice(start, stop)
            back = matmul(dy[side], mlp[1, :, lanes], (1, 0)) * d_in[side, :, lanes].astype(F32)
            du[side, :, lanes] = back.astype(BF16)

    hidden_back(0)
    rows_sent.wait()
    hidden_back(1)
    loads[1]()
    for start, stop in tiles_of(width, 256):
        part[:, start:stop] = matmul(du[1], mlp[0, start:stop, :], (1, 1)).astype(BF16)
    part_sent = to_pair(part, part_got, 1)
    for start, stop in tiles_of(width, 256):
        through[:, start:stop] = matmul(du[0], mlp[0, start:stop, :], (1, 1))
    part_sent.wait()
    dm = through[...] + part_got[...].astype(F32)
    step, gain, shift = norm_back(midway[...], vec[5:6, :width], dm)
    small[5:6, :] = gain
    small[6:7, :] = shift
    through[...] = grad[...] + step
    dz[...] = jnp.zeros_like(dz)
    dz[:, :width] = through[...].astype(BF16)
    do[...] = jnp.zeros_like(do)
    loads[2]()
    for start, stop in tiles_of(width, 256):
        do[:, start:stop] = matmul(dz[...], attn[1, start:stop, PADDED:], (1, 1)).astype(BF16)
    exchanged = to_heads(
        me, (do,), (do_all,), local_sem.at[3:4], send_sem.at[3:4], recv_sem.at[3:4]
    )
    dq_low[...] = jnp.zeros_like(dq_low)
    dk_low[...] = jnp.zeros_like(dk_low)
    dv_low[...] = jnp.zeros_like(dv_low)
    low_sum = lambda value: jnp.sum(value.astype(F32), 0, keepdims=True)
    small[4:5, :] = low_sum(dz[:, :width])
    small[7:8, :] = low_sum(dy[0])
    bias_back[...] = jnp.broadcast_to(low_sum(du[0]) + low_sum(du[1]), bias_back.shape)
    if carry:
        ring_a.forward()
    for copy in exchanged:
        copy.wait()
    for head in range(SLOTS):
        lanes = slice(head * HEAD, head * HEAD + HEAD)
        keys, values = k_all[:, lanes], v_all[:, lanes]
        dk_sum[...] = jnp.zeros_like(dk_sum)
        dv_sum[...] = jnp.zeros_like(dv_sum)
        for start in range(0, 512, CHUNK):
            rows, reach = slice(start, start + CHUNK), start + CHUNK
            queries = q_all[rows, lanes] * 0.125
            grads = do_all[rows, lanes]
            scores = matmul(queries, keys[:reach], (1, 1)) + mask[rows, :reach]
            probs = jnp.exp(scores - log_total[rows, head : head + 1])
            probs_back = matmul(grads, values[:reach], (1, 1))
            delta = jnp.sum(grads.astype(F32) * o_all[rows, lanes], 1, keepdims=True)
            scores_back = (probs * (probs_back - delta)).astype(BF16)
            dq_low[rows, lanes] = (matmul(scores_back, keys[:reach], (1, 0)) * 0.125).astype(BF16)
            dk_sum[:reach] += matmul(scores_back, queries, (0, 0))
            dv_sum[:reach] += matmul(probs.astype(BF16), grads, (0, 0))
        dk_low[:, lanes] = dk_sum[...].astype(BF16)
        dv_low[:, lanes] = dv_sum[...].astype(BF16)
        if carry and head == 2:
            ring_m.forward()
    exchanged = to_rows(
        me,
        (dq_low, dk_low, dv_low),
        (dq_landed, dk_landed, dv_landed),
        local_sem,
        send_sem,
        recv_sem,
    )
    loads[3]()
    for copy in exchanged:
        copy.wait()
    side_by_side(dq_landed, dq)
    side_by_side(dk_landed, dk)
    side_by_side(dv_landed, dv)
    small[2:3, :] = low_sum(dq[:, :width])
    small[3:4, :] = low_sum(dv[:, :width])
    for start, stop in tiles_of(width, 256):
        back = matmul(dq[...], attn[0, start:stop, :PADDED], (1, 1))
        back += matmul(dk[...], attn[0, start:stop, PADDED:], (1, 1))
        grad_out[:, start:stop] = back + matmul(dv[...], attn[1, start:stop, :PADDED], (1, 1))
    step, gain, shift = norm_back(layer_in[...], vec[0:1, :width], grad_out[...])
    small[0:1, :] = gain
    small[1:2, :] = shift
    grad_out[...] = through[...] + step
    if carry:
        ring_a.land()
        ring_m.land()
        copies.close()


def backward_layer(grad, vec, mask, kept, weights, sums, collective):
    shape = jax.ShapeDtypeStruct
    vmem = pl.BlockSpec(memory_space=pltpu.VMEM)
    hbm = pl.BlockSpec(memory_space=pl.ANY)
    rows, width = grad.shape
    carry = sums is not None
    low = lambda *dims: pltpu.VMEM(dims, BF16)
    out_shape = [
        shape((rows, width), F32),
        shape((2, rows, width), BF16),
        shape((2, rows, M_COLS), BF16),
        *[shape((rows, PADDED), BF16)] * 4,
        shape((8, width), F32),
        shape((8, M_COLS), F32),
    ]
    scratch = [
        low(2, 4 * BLOCK, 2 * PADDED),
        low(2, 4 * BLOCK, M_COLS),
        low(rows, width),
        low(rows, width),
        pltpu.VMEM((rows, width), F32),
        low(rows, PADDED),
        *[low(512, WINDOW)] * 4,
        *[low(GROUP, 64, WINDOW)] * 3,
        *[pltpu.VMEM((512, HEAD), F32)] * 2,
        pltpu.SemaphoreType.DMA((4,)),
        pltpu.SemaphoreType.DMA((4,)),
        pltpu.SemaphoreType.DMA((5, GROUP)),
        pltpu.SemaphoreType.DMA((5, GROUP)),
    ]
    if carry:
        out_shape += [shape((2, 4 * BLOCK, PIECE), BF16), shape((2, BLOCK, M_COLS), BF16)]
        scratch += [low(2, 2 * BLOCK, PIECE)] * 2 + [low(2, NEAR, M_COLS)] * 2
        scratch += [pltpu.SemaphoreType.DMA((16,))] * 2
    results = pl.pallas_call(
        functools.partial(backward_kernel, carry=carry),
        out_shape=out_shape,
        in_specs=[vmem] * 11 + [hbm] * (4 if carry else 2),
        out_specs=[vmem] * 9 + [hbm] * (2 if carry else 0),
        scratch_shapes=scratch,
        compiler_params=pltpu.CompilerParams(
            collective_id=collective, has_side_effects=True, vmem_limit_bytes=58 * 2**20
        ),
    )(grad, vec, mask, *kept, *weights, *(sums or ()))
    return results[:9], tuple(results[9:])


def body(tokens, qkv_weight, out_weight, up_weight, down_weight, vectors, segments, cotangent):
    micro_count, row_count, width = tokens.shape
    layers = qkv_weight.shape[0]
    hidden_half = up_weight.shape[2]
    total_rows = micro_count * row_count
    at = places()
    docs = jnp.pad(segments, ((0, 8 - micro_count), (0, 128 - row_count)))
    *first, tail, q_next, mt_next, docs = gather_first(
        [
            shard_rows(qkv_weight[l], out_weight[l], up_weight[l], down_weight[l], vectors[l], at["z"])
            for l in range(layers)
        ],
        docs,
        3,
    )
    bias = score_bias(docs)
    weights = [tuple(first)]
    residual = tokens.reshape(total_rows, width).astype(F32)
    memory = []
    for l in range(layers):
        vec = tail[:, width - PADDED + 128 :][:, :12].T.astype(F32)
        bias_up = lax.dynamic_slice_in_dim(vec[8:].reshape(-1), at["t"] * hidden_half, hidden_half)
        vec = jnp.pad(vec, ((0, 4), (0, PADDED - width)))
        kept, following = forward_layer(
            residual,
            vec,
            jnp.broadcast_to(bias_up, (8, hidden_half)),
            bias,
            weights[l],
            (q_next, mt_next) if l == 0 else None,
            5 + l,
        )
        if l == 0:
            *following, tail = following
            weights.append(tuple(following))
        memory.append((vec, residual, *kept[1:]))
        residual = kept[0]
    result = residual
    gradient = cotangent.reshape(total_rows, width)
    sums = [None] * layers
    near = None
    for l in reversed(range(layers)):
        vec, layer_in, normed, *saved, o, midway, m, g, d = memory[l]
        kept, passed = backward_layer(
            gradient,
            vec,
            bias,
            (layer_in, midway, d, *saved),
            weights[l],
            sums[1] if l == 0 else None,
            7 + l,
        )
        near = passed or near
        gradient, dy, du, dz, dq, dk, dv, small, bias_back = kept
        bias_back = lax.dynamic_update_slice_in_dim(
            jnp.zeros((2 * hidden_half,), F32), bias_back[0], at["t"] * hidden_half, 0
        )
        vec_back = jnp.concatenate([small, bias_back.reshape(-1, width)], 0)
        sums[l] = chip_sums(
            at,
            (
                normed, dq, dk, dv, o[:, :width], dz, m.reshape(-1, width),
                du.reshape(-1, hidden_half), dy.reshape(-1, width), g.reshape(-1, hidden_half), vec_back,
            ),
        )
    parts = reduce_layers(sums, near, 4)
    totals = [owned_gradients(parts[l], width) for l in range(layers)]
    stacked = [jnp.stack([totals[l][n] for l in range(layers)]) for n in range(5)]
    shape = (micro_count, row_count, width)
    return (result.reshape(shape), gradient.reshape(shape), *stacked)


def solution(mesh):
    return jax.shard_map(
        body,
        mesh=mesh,
        in_specs=(
            P(None, ("dp", "ctx", "tensor"), None),
            P(None, "dp", None),
            P(None, "dp", None),
            P(None, "dp", "tensor"),
            P(None, "dp", "tensor"),
            P(None, None, "dp"),
            P(None, ("dp", "ctx", "tensor")),
            P(None, ("dp", "ctx", "tensor"), None),
        ),
        out_specs=(
            P(None, ("dp", "ctx", "tensor"), None),
            P(None, ("dp", "ctx", "tensor"), None),
            P(None, "dp", None),
            P(None, "dp", None),
            P(None, "dp", "tensor"),
            P(None, "dp", "tensor"),
            P(None, None, "dp"),
        ),
        check_vma=False,
    )
```

```python
import functools

import jax
import jax.numpy as jnp
from jax import lax
from jax.experimental import pallas as pl
from jax.experimental.pallas import tpu as pltpu
from jax.sharding import PartitionSpec as P

EPSILON = 1e-05
MASKED = -1e30
MESH = pl.DeviceIdType.MESH
F32 = jnp.float32
BF16 = jnp.bfloat16
GROUP = 8
SLOTS = 5
HEAD = 64
WINDOW = 384
STRIDE = 256
PADDED = 1152
CHUNK = 128


def places():
    dp = lax.axis_index("dp")
    return {
        "x": dp // 4,
        "y": (dp // 2) % 2,
        "c": dp % 2,
        "z": lax.axis_index("ctx"),
        "t": lax.axis_index("tensor"),
    }


def shifted(value, x=0, y=0, c=0, z=0, t=0):
    pairs = []
    for i in range(128):
        ix, iy, ic, iz, it = i // 32, (i // 16) % 2, (i // 8) % 2, (i // 2) % 4, i % 2
        ix, iy, ic, iz, it = (ix + x) % 4, (iy + y) % 2, (ic + c) % 2, (iz + z) % 4, (it + t) % 2
        pairs.append((i, (((ix * 2 + iy) * 2 + ic) * 4 + iz) * 2 + it))
    return lax.ppermute(value, ("dp", "ctx", "tensor"), pairs)


ROWS = 68
TALL = 80
BLOCK = 272
NEAR = 144
Q_COLS = 512
T_START = 2048
T_COLS = 256
M_COLS = 2176


def peer_at(x=0, y=0, c=0, z=0, t=0):
    at = places()
    dp = (lax.rem(at["x"] + x + 4, 4) * 2 + lax.rem(at["y"] + y, 2)) * 2 + lax.rem(at["c"] + c, 2)
    return (dp, lax.rem(at["z"] + z + 4, 4), lax.rem(at["t"] + t, 2))


class Copies:
    def __init__(self, send_sem, recv_sem):
        self.send_sem, self.recv_sem = send_sem, recv_sem
        self.count = 0
        self.open = []

    def to(self, peer, src, dst):
        n = self.count
        self.count += 1
        assert n < self.send_sem.shape[0]
        copy = pltpu.make_async_remote_copy(
            src_ref=src,
            dst_ref=dst,
            send_sem=self.send_sem.at[n],
            recv_sem=self.recv_sem.at[n],
            device_id=peer,
            device_id_type=MESH,
        )
        copy.start()
        self.open.append(copy.wait_send)
        return copy.wait_recv

    def here(self, src, dst):
        n = self.count
        self.count += 1
        assert n < self.send_sem.shape[0]
        copy = pltpu.make_async_copy(src, dst, self.send_sem.at[n])
        copy.start()
        return copy.wait

    def close(self):
        for wait in self.open:
            wait()
        self.open = []


def rows_at(block, count=BLOCK, skip=0):
    return pl.ds(pl.multiple_of(block * BLOCK + skip, 16), count)


class RingX:
    def __init__(self, copies, own, buf, lanes, share):
        self.copies, self.own, self.buf, self.lanes, self.share = copies, own, buf, lanes, share
        at = places()
        self.c, self.x = at["c"], at["x"]
        self.last = []

    def view(self, distance, count=BLOCK, skip=0):
        block = lax.rem(self.x + distance + 4, 4)
        return self.buf.at[self.c, rows_at(block, count, skip), self.lanes]

    def sibling(self, src, dst):
        if self.share:
            self.last.append(self.copies.to(peer_at(c=1), src, dst))

    def start(self):
        self.from_below = self.copies.to(peer_at(x=1), self.own, self.view(0))
        self.from_above = self.copies.to(peer_at(x=-1), self.own, self.view(0))
        self.last.append(self.copies.here(self.own, self.view(0)))
        self.sibling(self.own, self.view(0))

    def forward(self):
        self.from_below()
        part = self.view(-1, NEAR)
        far_a = self.copies.to(peer_at(x=1), part, part)
        self.from_above()
        part = self.view(1, BLOCK - NEAR, NEAR)
        far_b = self.copies.to(peer_at(x=-1), part, part)
        self.far = (far_a, far_b)
        self.sibling(self.view(-1), self.view(-1))
        self.sibling(self.view(1), self.view(1))

    def finish(self):
        for wait in self.far:
            wait()
        self.sibling(self.view(2), self.view(2))

    def close(self):
        for wait in self.last:
            wait()


class RingZ:
    def __init__(self, copies, buf):
        self.copies, self.buf = copies, buf
        at = places()
        self.c, self.z = at["c"], at["z"]
        self.last = []

    def view(self, distance, rows=slice(None)):
        block = lax.rem(self.z + distance + 4, 4)
        return self.buf.at[self.c, rows, pl.ds(pl.multiple_of(block * Q_COLS, 128), Q_COLS)]

    def sibling(self, src):
        self.last.append(self.copies.to(peer_at(c=1), src, src))

    def start(self):
        own = self.view(0)
        self.from_below = self.copies.to(peer_at(z=1), own, own)
        self.from_above = self.copies.to(peer_at(z=-1), own, own)
        self.sibling(own)

    def forward(self):
        self.from_below()
        part = self.view(-1, pl.ds(0, 544))
        far_a = self.copies.to(peer_at(z=1), part, part)
        self.from_above()
        part = self.view(1, pl.ds(544, 544))
        far_b = self.copies.to(peer_at(z=-1), part, part)
        self.far = (far_a, far_b)
        self.sibling(self.view(-1))
        self.sibling(self.view(1))

    def finish(self):
        for wait in self.far:
            wait()
        self.sibling(self.view(2))

    def close(self):
        for wait in self.last:
            wait()


def exchange_shards(copies, mine, landed, lanes=slice(None)):
    c = places()["c"]
    part = lambda ref, n: ref.at[n, :, lanes]
    waits = [
        copies.to(peer_at(c=1), part(mine, 1 - c), part(landed, 1)),
        copies.to(peer_at(y=1), part(mine, c), part(landed, 2)),
        copies.to(peer_at(y=1, c=1), part(mine, 1 - c), part(landed, 3)),
    ]
    waits.append(copies.here(part(mine, c), part(landed, 0)))
    return waits


def assemble(landed, own, begin=0, end=None):
    at = places()
    end = end or own.shape[1]
    for start in range(begin, end, 256):
        lanes = slice(start, min(start + 256, end))
        parts = []
        for j in range(4):
            slot = lax.rem(j // 2 + at["y"], 2) * 2 + lax.rem(j % 2 + at["c"], 2)
            parts.append(landed[slot, :, lanes].astype(F32)[:ROWS])
        own[:, lanes] = jnp.concatenate(parts, 0).astype(BF16)


M_CUT = 1152


def gather_kernel(
    q0, mt0, q1, mt1, docs, attn, mlp, vec_tail, q_next, mt_next, docs_all,
    q_land, mt_land, q_own, mt_own, q_own1, mt_own1, send_sem, recv_sem,
):
    me = group_place()
    greet([dict(c=1), dict(y=1), dict(y=1, c=1), dict(x=1), dict(x=-1)], me)
    copies = Copies(send_sem, recv_sem)
    quarter = pl.ds(pl.multiple_of(places()["z"] * Q_COLS, 128), Q_COLS)
    arrive_q = exchange_shards(copies, q0, q_land.at[0])
    arrive_m = exchange_shards(copies, mt0, mt_land.at[0], pl.ds(0, M_CUT))
    arrive_mt = exchange_shards(copies, mt0, mt_land.at[0], pl.ds(M_CUT, M_COLS + T_COLS - M_CUT))
    later = [copies.here(docs, docs_all.at[me])]
    for n in range(1, GROUP):
        later.append(copies.to(member(lax.rem(me + n, GROUP)), docs, docs_all.at[me]))
    arrive_q1 = exchange_shards(copies, q1, q_land.at[1])
    arrive_mt1 = exchange_shards(copies, mt1, mt_land.at[1])
    q = RingX(copies, q_own, attn, quarter, False)
    m_lanes = (pl.ds(0, M_CUT), pl.ds(M_CUT, M_COLS - M_CUT))
    m = RingX(copies, mt_own.at[:, m_lanes[0]], mlp, m_lanes[0], True)
    m2 = RingX(copies, mt_own.at[:, m_lanes[1]], mlp, m_lanes[1], True)
    t = RingX(copies, mt_own.at[:, pl.ds(M_COLS, T_COLS)], attn, pl.ds(T_START, T_COLS), True)
    along_z = RingZ(copies, attn)

    def landed(waits, land, own, begin=0, end=None):
        for wait in waits:
            wait()
        assemble(land, own, begin, end)

    landed(arrive_q, q_land.at[0], q_own)
    q.start()
    landed(arrive_m, mt_land.at[0], mt_own, 0, M_CUT)
    q.forward()
    m.start()
    landed(arrive_mt, mt_land.at[0], mt_own, M_CUT)
    q.finish()
    q.close()
    along_z.start()
    t.start()
    m2.start()
    m.forward()
    landed(arrive_q1, q_land.at[1], q_own1)
    later.append(copies.here(q_own1, q_next))
    landed(arrive_mt1, mt_land.at[1], mt_own1)
    later.append(copies.here(mt_own1, mt_next))
    along_z.forward()
    t.forward()
    m2.forward()
    m.finish()
    along_z.finish()
    t.finish()
    m2.finish()
    for ring in (t, m, m2, along_z):
        ring.close()
    later.append(copies.here(attn.at[0, :, pl.ds(PADDED - 128, 128)], vec_tail))
    for wait in later:
        wait()
    copies.close()


def shard_rows(qkv, out, up, down, extra, z):
    width = out.shape[1]
    role0 = jnp.concatenate([padded(qkv[:, :width], extra), padded(qkv[:, width : 2 * width])], 1)
    role1 = jnp.concatenate([padded(qkv[:, 2 * width :]), padded(out)], 1)
    attn = jnp.pad(jnp.stack([role0, role1]), ((0, 0), (0, TALL - ROWS), (0, 0)))
    mlp = jnp.pad(jnp.stack([up, down]), ((0, 0), (0, TALL - ROWS), (0, 0)))
    quarter = lax.dynamic_slice_in_dim(attn, z * Q_COLS, Q_COLS, 2)
    return quarter, jnp.concatenate([mlp, attn[:, :, T_START:]], 2)


def gather_first(shards, docs, collective):
    hbm = pl.BlockSpec(memory_space=pl.ANY)
    shape = jax.ShapeDtypeStruct
    (q0, mt0), (q1, mt1) = shards
    low = lambda *dims: pltpu.VMEM(dims, BF16)
    return pl.pallas_call(
        gather_kernel,
        out_shape=[
            shape((2, 4 * BLOCK, 2 * PADDED), BF16),
            shape((2, 4 * BLOCK, M_COLS), BF16),
            shape((4 * BLOCK, 128), BF16),
            shape((BLOCK, Q_COLS), BF16),
            shape((BLOCK, M_COLS + T_COLS), BF16),
            shape((GROUP, *docs.shape), docs.dtype),
        ],
        in_specs=[hbm] * 5,
        out_specs=[hbm] * 6,
        scratch_shapes=[
            low(2, 4, TALL, Q_COLS),
            low(2, 4, TALL, M_COLS + T_COLS),
            low(BLOCK, Q_COLS),
            low(BLOCK, M_COLS + T_COLS),
            low(BLOCK, Q_COLS),
            low(BLOCK, M_COLS + T_COLS),
            pltpu.SemaphoreType.DMA((80,)),
            pltpu.SemaphoreType.DMA((80,)),
        ],
        compiler_params=pltpu.CompilerParams(
            collective_id=collective, has_side_effects=True, vmem_limit_bytes=32 * 2**20
        ),
    )(q0, mt0, q1, mt1, docs)


def padded(matrix, extra=None):
    rows, width = matrix.shape
    parts = [matrix]
    if extra is not None:
        parts.append(extra)
        width += extra.shape[1]
    parts.append(jnp.zeros((rows, PADDED - width), matrix.dtype))
    return jnp.concatenate(parts, 1)


PIECE = 640
HALF = 136
HALF_TALL = 144


def attn_start(z):
    return z * 13 // 3 * 128


def mlp_start(z):
    return z * 512


def contract_rows(a, b):
    return lax.dot_general(a, b, (((0,), (0,)), ((), ())), preferred_element_type=F32)


def contract_cols(a, b):
    return lax.dot_general(a, b, (((1,), (1,)), ((), ())), preferred_element_type=F32)


def block_diagonal(a, b):
    zero = jnp.zeros_like(a)
    return jnp.concatenate(
        [jnp.concatenate([a, zero], 1), jnp.concatenate([zero, b], 1)], 0
    )


def attn_sums(at, operands):
    a, dq, dk, dv, o, dz, vec = operands
    c0 = at["c"] == 0
    width = a.shape[1]
    pick = lambda p, q: jnp.where(c0, p, q)
    vec_cols = jnp.pad(vec.T, ((0, 0), (width, 2 * PADDED - width - vec.shape[0])))
    give = contract_rows(
        jnp.concatenate([a, pick(o, a)], 0), block_diagonal(pick(dv, dq), pick(dz, dk))
    ) + pick(0.0, 1.0) * vec_cols
    got = shifted(give.astype(BF16), c=1)
    keep = contract_rows(
        jnp.concatenate([a, pick(a, o)], 0), block_diagonal(pick(dq, dv), pick(dk, dz))
    ) + pick(1.0, 0.0) * vec_cols
    return (keep + got.astype(F32)).astype(BF16)


def in_chunks(count, step, do):
    def one(i, carry):
        do(pl.ds(pl.multiple_of(i * step, 16), step))
        return carry

    lax.fori_loop(0, count // step, one, 0)


class RingSum:
    def __init__(self, copies, axis, view, rows, near, via, step, stage=None):
        self.copies, self.axis, self.view, self.rows = copies, axis, view, rows
        self.near, self.via, self.step, self.stage = near, via, step, stage
        cut = via.shape[1]
        self.first, self.last = pl.ds(0, cut), pl.ds(cut, rows - cut)
        self.counts = (cut, rows - cut)
        self.up, self.down = peer_at(**{axis: 1}), peer_at(**{axis: -1})

    def start(self):
        self.start_far()
        self.start_near()

    def start_far(self):
        far = self.view(2)
        rest = pl.ds(0, self.counts[1])
        self.via_up = self.copies.to(self.up, far.at[self.first], self.via.at[0])
        self.via_down = self.copies.to(self.down, far.at[self.last], self.via.at[1, rest])
        self.parts = (self.view(1).at[self.first], self.view(-1).at[self.last])
        self.staged = []
        if self.stage is not None:
            staged = (self.stage.at[0], self.stage.at[1, rest])
            for src, dst in zip(self.parts, staged):
                self.staged.append(self.copies.here(src, dst))
            self.parts = staged

    def start_near(self, steps=(0, 1)):
        if 0 in steps:
            self.nears = []
        cut, rest = self.counts
        for n in steps:
            for peer, view, side, begin, count in (
                (self.up, self.view(1), 0, cut, rest),
                (self.down, self.view(-1), 1, 0, cut),
            ):
                half = count // 32 * 16
                rows = pl.ds(begin, half) if n == 0 else pl.ds(begin + half, count - half)
                self.nears.append(self.copies.to(peer, view.at[rows], self.near.at[side, rows]))

    def forward(self):
        for wait in self.staged:
            wait()
        arrived = (self.via_up, self.via_down)
        ends = ((self.up, 0, self.first), (self.down, 1, self.last))
        for n, (peer, side, rows) in enumerate(ends):
            arrived[n]()
            part = self.parts[n]

            def add(r):
                self.via[n, r, :] = (part[r, :].astype(F32) + self.via[n, r, :].astype(F32)).astype(BF16)

            in_chunks(self.counts[n], self.step, add)
            src = self.via.at[n, pl.ds(0, self.counts[n])]
            self.nears.append(self.copies.to(peer, src, self.near.at[side, rows]))

    def land(self):
        for wait in self.nears:
            wait()


def add_near(own, near, rows, step, write):
    def add(r):
        write(r, own[r, :].astype(F32) + near[0, r, :].astype(F32) + near[1, r, :].astype(F32))

    in_chunks(rows, step, add)


def turn(value, distance):
    return lax.rem(value + distance + 4, 4)


def columns_of(array, start_of, z):
    return array.at[:, pl.ds(pl.multiple_of(start_of(z), 128), PIECE)]


def attn_ring(copies, array, near, via, stage):
    view = lambda d: columns_of(array, attn_start, turn(places()["z"], d))
    return RingSum(copies, "z", view, 4 * BLOCK, near, via, 32, stage)


def mlp_ring(copies, array, near, via, stage):
    view = lambda d: array.at[rows_at(turn(places()["x"], d))]
    return RingSum(copies, "x", view, BLOCK, near, via, 16, stage)


def reduce_kernel(
    attn0, mlp0, attn1, mlp1, attn_near1, mlp_near1, out,
    attn_near, attn_via, attn_stage, mlp_near, mlp_via, mlp_stage, attn_own, mlp_own,
    attn_part, mlp_part, near2, via2, halves, got, owned, owned_got, send_sem, recv_sem,
):
    barrier = pltpu.get_barrier_semaphore()
    peers = [dict(c=1), dict(x=1), dict(x=-1), dict(y=1, t=1), dict(y=1), dict(t=1)]
    peers += [dict(z=1), dict(z=2), dict(z=3)]
    for peer in peers:
        pl.semaphore_signal(barrier, inc=1, device_id=peer_at(**peer), device_id_type=MESH)
    pl.semaphore_wait(barrier, len(peers))
    copies = Copies(send_sem, recv_sem)
    at = places()
    ring_a = attn_ring(copies, attn0, attn_near, attn_via, attn_stage)
    ring_m = mlp_ring(copies, mlp0, mlp_near, mlp_via, mlp_stage)
    ring_m.start()
    ring_a.start_far()
    loads = {}
    for l, (attn, mlp) in ((1, (attn1, mlp1)), (0, (attn0, mlp0))):
        loads[l] = (
            copies.here(columns_of(attn, attn_start, at["z"]), attn_own.at[l]),
            copies.here(mlp.at[rows_at(at["x"])], mlp_own.at[l]),
        )

    def second(l, near_a, near_m):
        def write_attn(r, value):
            attn_part[l, r, :] = value.astype(BF16)

        def write_mlp(r, value):
            mlp_part[l, r, :] = value.astype(BF16)

        for wait in loads[l]:
            wait()
        add_near(mlp_own.at[l], near_m, BLOCK, 16, write_mlp)
        m2 = RingSum(
            copies, "z", lambda d: columns_of(mlp_part.at[l], mlp_start, turn(at["z"], d)),
            BLOCK, near2.at[l, 1], via2.at[l, 1], 16,
        )
        m2.start()
        add_near(attn_own.at[l], near_a, 4 * BLOCK, 32, write_attn)
        a2 = RingSum(
            copies, "x", lambda d: attn_part.at[l, rows_at(turn(at["x"], d))],
            BLOCK, near2.at[l, 0], via2.at[l, 0], 16,
        )
        a2.start()
        return a2, m2

    def third(l, rings):
        waits = []
        for n, ring in enumerate(rings):
            ring.land()
            own = ring.view(0)
            total = (
                own[...].astype(F32) + ring.near[0].astype(F32) + ring.near[1].astype(F32)
            )
            halves[l, n, 0, :HALF] = total[:HALF].astype(BF16)
            halves[l, n, 1, :HALF] = total[HALF:].astype(BF16)
            halves[l, n, 0, HALF:] = jnp.zeros((HALF_TALL - HALF, PIECE), BF16)
            halves[l, n, 1, HALF:] = jnp.zeros((HALF_TALL - HALF, PIECE), BF16)
            peer = peer_at(y=1, t=1) if n == 0 else peer_at(y=1)
            waits.append(copies.to(peer, halves.at[l, n, 1 - at["y"]], got.at[l, n]))
        return waits

    def fourth(l, waits):
        waits[0]()
        mine = halves[l, 0, at["y"]].astype(F32) + got[l, 0].astype(F32)
        halves[l, 0, at["y"]] = mine.astype(BF16)
        return copies.to(peer_at(t=1), halves.at[l, 0, at["y"]], got.at[l, 2])

    def fifth(l, waits, wait):
        waits[1]()
        wait()
        ends = []
        for n, landed in ((0, 2), (1, 1)):
            total = halves[l, n, at["y"]].astype(F32) + got[l, landed].astype(F32)
            for core in range(2):
                owned[l, n, core, :ROWS] = total[core * ROWS : core * ROWS + ROWS].astype(BF16)
                owned[l, n, core, ROWS:] = jnp.zeros((TALL - ROWS, PIECE), BF16)
            ends.append(copies.to(peer_at(c=1), owned.at[l, n, 1 - at["c"]], owned_got.at[l, n]))
        return ends

    def sixth(l, ends):
        for wait in ends:
            wait()
        rest = []
        for n in range(2):
            for role, src in ((at["c"], owned.at[l, n, at["c"]]), (1 - at["c"], owned_got.at[l, n])):
                dst = out.at[l, at["z"], n, role]
                rest.append(copies.here(src, dst))
                for d in (1, 2, 3):
                    rest.append(copies.to(peer_at(z=d), src, dst))
        return rest

    rings, waits, turned, ends, rest = {}, {}, {}, {}, []
    order = (1, 0)
    rings[1] = second(1, attn_near1, mlp_near1)
    ring_a.start_near()
    ring_m.forward()
    ring_a.forward()
    for ring in reversed(rings[1]):
        ring.forward()
    ring_m.land()
    ring_a.land()
    rings[0] = second(0, attn_near, mlp_near)
    waits[1] = third(1, rings[1])
    turned[1] = fourth(1, waits[1])
    for ring in reversed(rings[0]):
        ring.forward()
    ends[1] = fifth(1, waits[1], turned[1])
    waits[0] = third(0, rings[0])
    turned[0] = fourth(0, waits[0])
    rest += sixth(1, ends[1])
    ends[0] = fifth(0, waits[0], turned[0])
    rest += sixth(0, ends[0])
    for wait in rest:
        wait()
    copies.close()


def reduce_layers(sums, near, collective):
    hbm = pl.BlockSpec(memory_space=pl.ANY)
    vmem = pl.BlockSpec(memory_space=pltpu.VMEM)
    low = lambda *dims: pltpu.VMEM(dims, BF16)
    return pl.pallas_call(
        reduce_kernel,
        out_shape=jax.ShapeDtypeStruct((2, 4, 2, 2, TALL, PIECE), BF16),
        in_specs=[hbm] * 4 + [vmem] * 2,
        out_specs=hbm,
        scratch_shapes=[
            low(2, 4 * BLOCK, PIECE),
            low(2, 2 * BLOCK, PIECE),
            low(2, 2 * BLOCK, PIECE),
            low(2, BLOCK, M_COLS),
            low(2, NEAR, M_COLS),
            low(2, NEAR, M_COLS),
            low(2, 4 * BLOCK, PIECE),
            low(2, BLOCK, M_COLS),
            low(2, 4 * BLOCK, PIECE),
            low(2, BLOCK, M_COLS),
            low(2, 2, 2, BLOCK, PIECE),
            low(2, 2, 2, NEAR, PIECE),
            low(2, 2, 2, HALF_TALL, PIECE),
            low(2, 3, HALF_TALL, PIECE),
            low(2, 2, 2, TALL, PIECE),
            low(2, 2, TALL, PIECE),
            pltpu.SemaphoreType.DMA((128,)),
            pltpu.SemaphoreType.DMA((128,)),
        ],
        compiler_params=pltpu.CompilerParams(
            collective_id=collective, has_side_effects=True, vmem_limit_bytes=56 * 2**20
        ),
    )(*sums[0], *sums[1], *near)


def owned_gradients(parts, width):
    parts = parts[:, :, :, :ROWS]

    def joined(n, role, widths):
        return jnp.concatenate([parts[z, n, role, :, :w] for z, w in enumerate(widths)], 1)

    attn = [joined(0, role, (512, 512, 640, 640)) for role in range(2)]
    up, down = (joined(1, role, (512, 512, 512, 640)) for role in range(2))
    qk, vo = attn
    in_back = jnp.concatenate([qk[:, :width], qk[:, PADDED : PADDED + width], vo[:, :width]], 1)
    vec_back = qk[:, width : width + 12].T
    results = (in_back, vo[:, PADDED : PADDED + width], up, down, vec_back)
    return tuple(value.astype(F32) for value in results)


def group_place():
    return lax.axis_index("ctx") * 2 + lax.axis_index("tensor")


def member(index):
    return (lax.axis_index("dp"), index // 2, lax.rem(index, 2))


def meet(me):
    barrier = pltpu.get_barrier_semaphore()
    for k in range(1, GROUP):
        pl.semaphore_signal(
            barrier, inc=1, device_id=member(lax.rem(me + k, GROUP)), device_id_type=MESH
        )
    pl.semaphore_wait(barrier, GROUP - 1)


def to_heads(me, sources, landed, local_sem, send_sem, recv_sem):
    copies = []
    for k in range(1, GROUP):
        peer = lax.rem(me + k, GROUP)
        rows = pl.ds(pl.multiple_of(peer // 4 * 64, 64), 64)
        lanes = pl.ds(pl.multiple_of(lax.rem(peer, 4) * STRIDE, 128), WINDOW)
        for n, (src, dst) in enumerate(zip(sources, landed)):
            copy = pltpu.make_async_remote_copy(
                src_ref=src.at[rows, lanes],
                dst_ref=dst.at[pl.ds(pl.multiple_of(me * 64, 64), 64)],
                send_sem=send_sem.at[n, k],
                recv_sem=recv_sem.at[n, k],
                device_id=member(peer),
                device_id_type=MESH,
            )
            copy.start()
            copies.append(copy)
    rows = pl.ds(pl.multiple_of(me // 4 * 64, 64), 64)
    lanes = pl.ds(pl.multiple_of(lax.rem(me, 4) * STRIDE, 128), WINDOW)
    for n, (src, dst) in enumerate(zip(sources, landed)):
        copy = pltpu.make_async_copy(
            src.at[rows, lanes], dst.at[pl.ds(pl.multiple_of(me * 64, 64), 64)], local_sem.at[n]
        )
        copy.start()
        copies.append(copy)
    return copies


def to_rows(me, sources, landed, local_sem, send_sem, recv_sem):
    copies = []
    for k in range(1, GROUP):
        peer = lax.rem(me + k, GROUP)
        for n, (src, dst) in enumerate(zip(sources, landed)):
            copy = pltpu.make_async_remote_copy(
                src_ref=src.at[pl.ds(pl.multiple_of(peer * 64, 64), 64)],
                dst_ref=dst.at[me],
                send_sem=send_sem.at[n, k],
                recv_sem=recv_sem.at[n, k],
                device_id=member(peer),
                device_id_type=MESH,
            )
            copy.start()
            copies.append(copy)
    for n, (src, dst) in enumerate(zip(sources, landed)):
        copy = pltpu.make_async_copy(
            src.at[pl.ds(pl.multiple_of(me * 64, 64), 64)], dst.at[me], local_sem.at[n]
        )
        copy.start()
        copies.append(copy)
    return copies


def side_by_side(landed, out):
    for micro in range(2):
        rows = slice(micro * 64, micro * 64 + 64)
        for group in range(4):
            width = WINDOW if group == 3 else STRIDE
            out[rows, group * STRIDE : group * STRIDE + width] = landed[micro * 4 + group, :, :width]


def matmul(a, b, dims):
    return lax.dot_general(a, b, ((dims[:1], dims[1:]), ((), ())), preferred_element_type=F32)


def score_bias(docs):
    docs = lax.dynamic_index_in_dim(docs, lax.axis_index("ctx") // 2, 1, keepdims=False)
    docs = docs[:, :64].reshape(-1)
    place = jnp.arange(docs.shape[0], dtype=jnp.int32)
    allowed = (docs[:, None] == docs[None, :]) & (place[None, :] <= place[:, None])
    return jnp.where(allowed, 0.0, MASKED).astype(F32)


def tiles_of(width, step):
    return [(start, min(start + step, width)) for start in range(0, width, step)]


def normalise(inputs):
    centred = inputs - jnp.mean(inputs, 1, keepdims=True)
    spread = jnp.mean(centred * centred, 1, keepdims=True)
    scale = lax.rsqrt(spread + EPSILON)
    return centred * scale, scale


def gelu_and_slope(u):
    share = 0.5 * (1.0 + lax.erf(u * 0.7071067811865476))
    return u * share, share + u * jnp.exp(-0.5 * u * u) * 0.3989422804014327


def greet(peers, me):
    barrier = pltpu.get_barrier_semaphore()
    members = [member(lax.rem(me + k, GROUP)) for k in range(1, GROUP)]
    for peer in members + [peer_at(**peer) for peer in peers]:
        pl.semaphore_signal(barrier, inc=1, device_id=peer, device_id_type=MESH)
    pl.semaphore_wait(barrier, len(members) + len(peers))


def forward_kernel(*refs, carry):
    resid, vec, bias_up, mask, attn_in, mlp_in = refs[:6]
    refs = refs[6:]
    if carry:
        q_own, mt_own = refs[:2]
        refs = refs[2:]
    (
        resid_out, normed, q_all, k_all, v_all, o_all, log_total, o_out, midway, m_out, g_out, d_out,
    ) = refs[:12]
    refs = refs[12:]
    if carry:
        next_attn, next_mlp = refs[:2]
        refs = refs[2:]
    (
        attn, mlp, q, k, v, o_low, o_landed, part, part_got, load_sem, local_sem, send_sem, recv_sem,
    ) = refs[:13]
    me = group_place()
    greet([dict(c=1), dict(x=1), dict(x=-1)] if carry else [], me)
    loads = []
    for n, (src, dst) in enumerate(
        [(attn_in.at[0], attn.at[0]), (attn_in.at[1], attn.at[1]), (mlp_in.at[0], mlp.at[0]), (mlp_in.at[1], mlp.at[1])]
    ):
        copy = pltpu.make_async_copy(src, dst, load_sem.at[n])
        copy.start()
        loads.append(copy.wait)
    if carry:
        copies = Copies(*refs[13:15])
        quarter = pl.ds(pl.multiple_of(places()["z"] * Q_COLS, 128), Q_COLS)
        ring_q = RingX(copies, q_own, next_attn, quarter, False)
        ring_m = RingX(copies, mt_own.at[:, pl.ds(0, M_COLS)], next_mlp, slice(None), True)
        ring_t = RingX(copies, mt_own.at[:, pl.ds(M_COLS, T_COLS)], next_attn, pl.ds(T_START, T_COLS), True)
        ring_z = RingZ(copies, next_attn)
        ring_q.start()
    row = lambda n: vec[n : n + 1, :]
    width = resid.shape[1]
    x, _ = normalise(resid[...])
    a = (x * row(0)[:, :width] + row(1)[:, :width]).astype(BF16)
    normed[...] = a
    loads[0]()
    for start, stop in tiles_of(PADDED, 384):
        lanes = slice(start, stop)
        q[:, lanes] = (matmul(a, attn[0, :, lanes], (1, 0)) + vec[2:3, lanes]).astype(BF16)
        k[:, lanes] = matmul(a, attn[0, :, PADDED + start : PADDED + stop], (1, 0)).astype(BF16)
    loads[1]()
    if carry:
        ring_q.forward()
        ring_t.start()
        ring_m.start()
    for start, stop in tiles_of(PADDED, 384):
        lanes = slice(start, stop)
        v[:, lanes] = (matmul(a, attn[1, :, lanes], (1, 0)) + vec[3:4, lanes]).astype(BF16)
    exchanged = to_heads(me, (q, k, v), (q_all, k_all, v_all), local_sem, send_sem, recv_sem)
    o_low[...] = jnp.zeros_like(o_low)
    o_all[...] = jnp.zeros_like(o_all)
    log_total[...] = jnp.zeros_like(log_total)
    if carry:
        ring_q.finish()
        ring_q.close()
        ring_z.start()
    for copy in exchanged:
        copy.wait()
    for head in range(SLOTS):
        lanes = slice(head * HEAD, head * HEAD + HEAD)
        keys, values = k_all[:, lanes], v_all[:, lanes]
        for start in range(0, 512, CHUNK):
            rows, reach = slice(start, start + CHUNK), start + CHUNK
            queries = q_all[rows, lanes] * 0.125
            scores = matmul(queries, keys[:reach], (1, 1)) + mask[rows, :reach]
            top = jnp.max(scores, 1, keepdims=True)
            weights = jnp.exp(scores - top)
            total = jnp.sum(weights, 1, keepdims=True)
            result = matmul(weights.astype(BF16), values[:reach], (1, 0)) / total
            o_all[rows, lanes] = result
            o_low[rows, lanes] = result.astype(BF16)
            log_total[rows, head : head + 1] = top + jnp.log(total)
        if carry and head == 3:
            ring_t.forward()
            ring_m.forward()
    exchanged = to_rows(
        me, (o_low,), (o_landed,), local_sem.at[3:4], send_sem.at[3:4], recv_sem.at[3:4]
    )
    if carry:
        ring_z.forward()
    for copy in exchanged:
        copy.wait()
    side_by_side(o_landed, o_out)
    o = o_out[:, :width]
    for start, stop in tiles_of(width, 384):
        lanes = slice(start, stop)
        midway[:, lanes] = (
            resid[:, lanes]
            + matmul(o, attn[1, :, PADDED + start : PADDED + stop], (1, 0))
            + vec[4:5, lanes]
        )
    x, _ = normalise(midway[...])
    m_out[0] = (x * row(5)[:, :width] + row(6)[:, :width]).astype(BF16)

    def to_pair(src, dst, n):
        copy = pltpu.make_async_remote_copy(
            src_ref=src,
            dst_ref=dst,
            send_sem=send_sem.at[4, n],
            recv_sem=recv_sem.at[4, n],
            device_id=peer_at(t=1),
            device_id_type=MESH,
        )
        copy.start()
        return copy

    rows_sent = to_pair(m_out.at[0], m_out.at[1], 0)
    loads[2]()

    def up(side):
        for start, stop in tiles_of(M_COLS, 256):
            lanes = slice(start, stop)
            u = matmul(m_out[side], mlp[0, :, lanes], (1, 0)) + bias_up[0:1, lanes]
            g, d = gelu_and_slope(u)
            g_out[side, :, lanes] = g.astype(BF16)
            d_out[side, :, lanes] = d.astype(BF16)

    up(0)
    rows_sent.wait()
    up(1)
    loads[3]()
    for start, stop in tiles_of(width, 256):
        part[:, start:stop] = matmul(g_out[1], mlp[1, start:stop, :], (1, 1)).astype(BF16)
    part_sent = to_pair(part, part_got, 1)
    for start, stop in tiles_of(width, 256):
        resid_out[:, start:stop] = matmul(g_out[0], mlp[1, start:stop, :], (1, 1))
    part_sent.wait()
    resid_out[...] += midway[...] + part_got[...].astype(F32) + row(7)[:, :width]
    if carry:
        ring_t.finish()
        ring_z.finish()
        ring_m.finish()
        for ring in (ring_t, ring_z, ring_m):
            ring.close()
        copies.close()


def forward_layer(resid, vec, bias_up, mask, weights, pieces, collective):
    shape = jax.ShapeDtypeStruct
    vmem = pl.BlockSpec(memory_space=pltpu.VMEM)
    hbm = pl.BlockSpec(memory_space=pl.ANY)
    rows, width = resid.shape
    carry = pieces is not None
    low = lambda *dims: pltpu.VMEM(dims, BF16)
    out_shape = [
        shape((rows, width), F32),
        shape((rows, width), BF16),
        shape((512, WINDOW), BF16),
        shape((512, WINDOW), BF16),
        shape((512, WINDOW), BF16),
        shape((512, WINDOW), F32),
        shape((512, 128), F32),
        shape((rows, PADDED), BF16),
        shape((rows, width), F32),
        shape((2, rows, width), BF16),
        shape((2, rows, M_COLS), BF16),
        shape((2, rows, M_COLS), BF16),
    ]
    scratch = [
        low(2, 4 * BLOCK, 2 * PADDED),
        low(2, 4 * BLOCK, M_COLS),
        low(rows, PADDED),
        low(rows, PADDED),
        low(rows, PADDED),
        low(512, WINDOW),
        low(GROUP, 64, WINDOW),
        low(rows, width),
        low(rows, width),
        pltpu.SemaphoreType.DMA((4,)),
        pltpu.SemaphoreType.DMA((4,)),
        pltpu.SemaphoreType.DMA((5, GROUP)),
        pltpu.SemaphoreType.DMA((5, GROUP)),
    ]
    if carry:
        out_shape += [shape(w.shape, w.dtype) for w in weights]
        scratch += [pltpu.SemaphoreType.DMA((40,))] * 2
    results = pl.pallas_call(
        functools.partial(forward_kernel, carry=carry),
        out_shape=out_shape,
        in_specs=[vmem] * 4 + [hbm] * (4 if carry else 2),
        out_specs=[vmem] * 12 + [hbm] * (2 if carry else 0),
        scratch_shapes=scratch,
        compiler_params=pltpu.CompilerParams(
            collective_id=collective, has_side_effects=True, vmem_limit_bytes=56 * 2**20
        ),
    )(resid, vec, bias_up, mask, *weights, *(pieces or ()))
    return results[:12], tuple(results[12:])


def norm_back(inputs, gain, back):
    x, scale = normalise(inputs)
    e = back * gain
    grad = scale * (
        e - jnp.mean(e, 1, keepdims=True) - x * jnp.mean(e * x, 1, keepdims=True)
    )
    return grad, jnp.sum(back * x, 0, keepdims=True), jnp.sum(back, 0, keepdims=True)


def backward_kernel(*refs, carry):
    (
        grad, vec, mask, layer_in, midway, d_in, m_in, g_in, q_all, k_all, v_all, o_all, log_total,
        attn_in, mlp_in,
    ) = refs[:15]
    refs = refs[15:]
    if carry:
        attn_sum, mlp_sum = refs[:2]
        refs = refs[2:]
    grad_out, dz, dq, dk, dv, small, bias_back, mlp_total = refs[:8]
    refs = refs[8:]
    if carry:
        attn_near, mlp_near = refs[:2]
        refs = refs[2:]
    (
        attn, mlp, part, part_got, through, do, do_all, dq_low, dk_low, dv_low, dq_landed, dk_landed, dv_landed,
        dk_sum, dv_sum, load_sem, local_sem, send_sem, recv_sem, dy, du, mlp_got, turned,
    ) = refs[:23]
    me = group_place()
    greet([dict(c=1)] + ([dict(x=1), dict(x=-1)] if carry else []), me)
    width = grad.shape[1]
    dy[0] = grad[...].astype(BF16)

    def to_pair(src, dst, n, peer=peer_at(t=1)):
        copy = pltpu.make_async_remote_copy(
            src_ref=src,
            dst_ref=dst,
            send_sem=send_sem.at[4, n],
            recv_sem=recv_sem.at[4, n],
            device_id=peer,
            device_id_type=MESH,
        )
        copy.start()
        return copy

    def mlp_products(up, write):
        for side in range(2):
            left = jnp.where(up, m_in[side].astype(F32), dy[side].astype(F32))
            turned[:, side * 128 : side * 128 + 128] = jnp.transpose(left).astype(BF16)
        for start, stop in tiles_of(M_COLS, 256):
            lanes = slice(start, stop)
            right = [jnp.where(up, du[n, :, lanes].astype(F32), g_in[n, :, lanes].astype(F32)) for n in range(2)]
            right = jnp.concatenate(right, 0).astype(BF16)
            write(lanes, matmul(turned[...], right, (1, 0)))

    rows_sent = to_pair(dy.at[0], dy.at[1], 0)
    loads = []
    for n, (src, dst) in enumerate(
        [(mlp_in.at[1], mlp.at[1]), (mlp_in.at[0], mlp.at[0]), (attn_in.at[1], attn.at[1]), (attn_in.at[0], attn.at[0])]
    ):
        copy = pltpu.make_async_copy(src, dst, load_sem.at[n])
        copy.start()
        loads.append(copy.wait)
    if carry:
        attn_via, attn_stage, mlp_via, mlp_stage = refs[23:27]
        copies = Copies(*refs[27:29])
        ring_a = attn_ring(copies, attn_sum, attn_near, attn_via, attn_stage)
        ring_m = mlp_ring(copies, mlp_sum, mlp_near, mlp_via, mlp_stage)
        ring_a.start_far()
        ring_a.start_near((0,))
        ring_m.start()
    loads[0]()

    def hidden_back(side):
        for start, stop in tiles_of(M_COLS, 256):
            lanes = slice(start, stop)
            back = matmul(dy[side], mlp[1, :, lanes], (1, 0)) * d_in[side, :, lanes].astype(F32)
            du[side, :, lanes] = back.astype(BF16)

    hidden_back(0)
    rows_sent.wait()
    hidden_back(1)
    loads[1]()
    for start, stop in tiles_of(width, 256):
        part[:, start:stop] = matmul(du[1], mlp[0, start:stop, :], (1, 1)).astype(BF16)
    part_sent = to_pair(part, part_got, 1)
    for start, stop in tiles_of(width, 256):
        through[:, start:stop] = matmul(du[0], mlp[0, start:stop, :], (1, 1))
    part_sent.wait()
    dm = through[...] + part_got[...].astype(F32)
    step, gain, shift = norm_back(midway[...], vec[5:6, :width], dm)
    small[5:6, :] = gain
    small[6:7, :] = shift
    through[...] = grad[...] + step
    dz[...] = jnp.zeros_like(dz)
    dz[:, :width] = through[...].astype(BF16)
    do[...] = jnp.zeros_like(do)
    loads[2]()
    for start, stop in tiles_of(width, 256):
        do[:, start:stop] = matmul(dz[...], attn[1, start:stop, PADDED:], (1, 1)).astype(BF16)
    exchanged = to_heads(
        me, (do,), (do_all,), local_sem.at[3:4], send_sem.at[3:4], recv_sem.at[3:4]
    )
    dq_low[...] = jnp.zeros_like(dq_low)
    dk_low[...] = jnp.zeros_like(dk_low)
    dv_low[...] = jnp.zeros_like(dv_low)
    low_sum = lambda value: jnp.sum(value.astype(F32), 0, keepdims=True)
    small[4:5, :] = low_sum(dz[:, :width])
    small[7:8, :] = low_sum(dy[0])
    bias_back[...] = jnp.broadcast_to(low_sum(du[0]) + low_sum(du[1]), bias_back.shape)

    def give(lanes, value):
        mlp[0, :, lanes] = value.astype(BF16)

    mlp_products(places()["c"] == 1, give)
    mlp_sent = to_pair(mlp.at[0], mlp_got, 2, peer_at(c=1))
    for copy in exchanged:
        copy.wait()
    if carry:
        ring_a.start_near((1,))
        ring_a.forward()
    for head in range(SLOTS):
        lanes = slice(head * HEAD, head * HEAD + HEAD)
        keys, values = k_all[:, lanes], v_all[:, lanes]
        dk_sum[...] = jnp.zeros_like(dk_sum)
        dv_sum[...] = jnp.zeros_like(dv_sum)
        for start in range(0, 512, CHUNK):
            rows, reach = slice(start, start + CHUNK), start + CHUNK
            queries = q_all[rows, lanes] * 0.125
            grads = do_all[rows, lanes]
            scores = matmul(queries, keys[:reach], (1, 1)) + mask[rows, :reach]
            probs = jnp.exp(scores - log_total[rows, head : head + 1])
            probs_back = matmul(grads, values[:reach], (1, 1))
            delta = jnp.sum(grads.astype(F32) * o_all[rows, lanes], 1, keepdims=True)
            scores_back = (probs * (probs_back - delta)).astype(BF16)
            dq_low[rows, lanes] = (matmul(scores_back, keys[:reach], (1, 0)) * 0.125).astype(BF16)
            dk_sum[:reach] += matmul(scores_back, queries, (0, 0))
            dv_sum[:reach] += matmul(probs.astype(BF16), grads, (0, 0))
        dk_low[:, lanes] = dk_sum[...].astype(BF16)
        dv_low[:, lanes] = dv_sum[...].astype(BF16)
        if carry and head == 2:
            ring_m.forward()
    exchanged = to_rows(
        me,
        (dq_low, dk_low, dv_low),
        (dq_landed, dk_landed, dv_landed),
        local_sem,
        send_sem,
        recv_sem,
    )
    loads[3]()
    mlp_sent.wait()

    def keep(lanes, value):
        mlp[1, :, lanes] = (value + mlp_got[:, lanes].astype(F32)).astype(BF16)

    mlp_products(places()["c"] == 0, keep)
    store = pltpu.make_async_copy(mlp.at[1], mlp_total, load_sem.at[0])
    store.start()
    for copy in exchanged:
        copy.wait()
    side_by_side(dq_landed, dq)
    side_by_side(dk_landed, dk)
    side_by_side(dv_landed, dv)
    small[2:3, :] = low_sum(dq[:, :width])
    small[3:4, :] = low_sum(dv[:, :width])
    for start, stop in tiles_of(width, 256):
        back = matmul(dq[...], attn[0, start:stop, :PADDED], (1, 1))
        back += matmul(dk[...], attn[0, start:stop, PADDED:], (1, 1))
        grad_out[:, start:stop] = back + matmul(dv[...], attn[1, start:stop, :PADDED], (1, 1))
    step, gain, shift = norm_back(layer_in[...], vec[0:1, :width], grad_out[...])
    small[0:1, :] = gain
    small[1:2, :] = shift
    grad_out[...] = through[...] + step
    store.wait()
    if carry:
        ring_a.land()
        ring_m.land()
        copies.close()


def backward_layer(grad, vec, mask, kept, weights, sums, collective):
    shape = jax.ShapeDtypeStruct
    vmem = pl.BlockSpec(memory_space=pltpu.VMEM)
    hbm = pl.BlockSpec(memory_space=pl.ANY)
    rows, width = grad.shape
    carry = sums is not None
    low = lambda *dims: pltpu.VMEM(dims, BF16)
    out_shape = [
        shape((rows, width), F32),
        *[shape((rows, PADDED), BF16)] * 4,
        shape((8, width), F32),
        shape((8, M_COLS), F32),
        shape((4 * BLOCK, M_COLS), BF16),
    ]
    scratch = [
        low(2, 4 * BLOCK, 2 * PADDED),
        low(2, 4 * BLOCK, M_COLS),
        low(rows, width),
        low(rows, width),
        pltpu.VMEM((rows, width), F32),
        low(rows, PADDED),
        *[low(512, WINDOW)] * 4,
        *[low(GROUP, 64, WINDOW)] * 3,
        *[pltpu.VMEM((512, HEAD), F32)] * 2,
        pltpu.SemaphoreType.DMA((4,)),
        pltpu.SemaphoreType.DMA((4,)),
        pltpu.SemaphoreType.DMA((5, GROUP)),
        pltpu.SemaphoreType.DMA((5, GROUP)),
        low(2, rows, width),
        low(2, rows, M_COLS),
        low(4 * BLOCK, M_COLS),
        low(4 * BLOCK, 256),
    ]
    if carry:
        out_shape += [shape((2, 4 * BLOCK, PIECE), BF16), shape((2, BLOCK, M_COLS), BF16)]
        scratch += [low(2, 2 * BLOCK, PIECE)] * 2 + [low(2, NEAR, M_COLS)] * 2
        scratch += [pltpu.SemaphoreType.DMA((24,))] * 2
    results = pl.pallas_call(
        functools.partial(backward_kernel, carry=carry),
        out_shape=out_shape,
        in_specs=[vmem] * 13 + [hbm] * (4 if carry else 2),
        out_specs=[vmem] * 7 + [hbm] * (3 if carry else 1),
        scratch_shapes=scratch,
        compiler_params=pltpu.CompilerParams(
            collective_id=collective, has_side_effects=True, vmem_limit_bytes=58 * 2**20
        ),
    )(grad, vec, mask, *kept, *weights, *(sums or ()))
    return results[:8], tuple(results[8:])


def body(tokens, qkv_weight, out_weight, up_weight, down_weight, vectors, segments, cotangent):
    micro_count, row_count, width = tokens.shape
    layers = qkv_weight.shape[0]
    hidden_half = up_weight.shape[2]
    total_rows = micro_count * row_count
    at = places()
    docs = jnp.pad(segments, ((0, 8 - micro_count), (0, 128 - row_count)))
    *first, tail, q_next, mt_next, docs = gather_first(
        [
            shard_rows(
                qkv_weight[l],
                out_weight[l],
                up_weight[l],
                down_weight[l],
                vectors.reshape(12 * layers, -1).T if l == 0 else None,
                at["z"],
            )
            for l in range(layers)
        ],
        docs,
        3,
    )
    bias = score_bias(docs)
    all_vectors = tail[:, width - PADDED + 128 :].T.astype(F32)
    weights = [tuple(first)]
    residual = tokens.reshape(total_rows, width).astype(F32)
    memory = []
    for l in range(layers):
        vec = all_vectors[12 * l : 12 * l + 12]
        bias_up = lax.dynamic_slice_in_dim(vec[8:].reshape(-1), at["t"] * hidden_half, hidden_half)
        vec = jnp.pad(vec, ((0, 4), (0, PADDED - width)))
        kept, following = forward_layer(
            residual,
            vec,
            jnp.broadcast_to(bias_up, (8, hidden_half)),
            bias,
            weights[l],
            (q_next, mt_next) if l == 0 else None,
            5 + l,
        )
        if l == 0:
            weights.append(following)
        memory.append((vec, residual, *kept[1:]))
        residual = kept[0]
    result = residual
    gradient = cotangent.reshape(total_rows, width)
    sums = [None] * layers
    near = None
    for l in reversed(range(layers)):
        vec, layer_in, normed, *saved, o, midway, m, g, d = memory[l]
        kept, passed = backward_layer(
            gradient,
            vec,
            bias,
            (layer_in, midway, d, m, g, *saved),
            weights[l],
            sums[1] if l == 0 else None,
            7 + l,
        )
        near = passed or near
        gradient, dz, dq, dk, dv, small, bias_back, mlp_sum = kept
        bias_back = lax.dynamic_update_slice_in_dim(
            jnp.zeros((2 * hidden_half,), F32), bias_back[0], at["t"] * hidden_half, 0
        )
        vec_back = jnp.concatenate([small, bias_back.reshape(-1, width)], 0)
        sums[l] = (attn_sums(at, (normed, dq, dk, dv, o[:, :width], dz, vec_back)), mlp_sum)
    parts = reduce_layers(sums, near, 4)
    totals = [owned_gradients(parts[l], width) for l in range(layers)]
    stacked = [jnp.stack([totals[l][n] for l in range(layers)]) for n in range(5)]
    shape = (micro_count, row_count, width)
    return (result.reshape(shape), gradient.reshape(shape), *stacked)


def solution(mesh):
    return jax.shard_map(
        body,
        mesh=mesh,
        in_specs=(
            P(None, ("dp", "ctx", "tensor"), None),
            P(None, "dp", None),
            P(None, "dp", None),
            P(None, "dp", "tensor"),
            P(None, "dp", "tensor"),
            P(None, None, "dp"),
            P(None, ("dp", "ctx", "tensor")),
            P(None, ("dp", "ctx", "tensor"), None),
        ),
        out_specs=(
            P(None, ("dp", "ctx", "tensor"), None),
            P(None, ("dp", "ctx", "tensor"), None),
            P(None, "dp", None),
            P(None, "dp", None),
            P(None, "dp", "tensor"),
            P(None, "dp", "tensor"),
            P(None, None, "dp"),
        ),
        check_vma=False,
    )
```

```python
import functools

import jax
import jax.numpy as jnp
from jax import lax
from jax.experimental import pallas as pl
from jax.experimental.pallas import tpu as pltpu
from jax.sharding import PartitionSpec as P

EPSILON = 1e-05
MASKED = -1e30
MESH = pl.DeviceIdType.MESH
F32 = jnp.float32
BF16 = jnp.bfloat16
GROUP = 8
SLOTS = 5
HEAD = 64
WINDOW = 384
STRIDE = 256
PADDED = 1152
CHUNK = 128


def places():
    dp = lax.axis_index("dp")
    return {
        "x": dp // 4,
        "y": (dp // 2) % 2,
        "c": dp % 2,
        "z": lax.axis_index("ctx"),
        "t": lax.axis_index("tensor"),
    }


def shifted(value, x=0, y=0, c=0, z=0, t=0):
    pairs = []
    for i in range(128):
        ix, iy, ic, iz, it = i // 32, (i // 16) % 2, (i // 8) % 2, (i // 2) % 4, i % 2
        ix, iy, ic, iz, it = (ix + x) % 4, (iy + y) % 2, (ic + c) % 2, (iz + z) % 4, (it + t) % 2
        pairs.append((i, (((ix * 2 + iy) * 2 + ic) * 4 + iz) * 2 + it))
    return lax.ppermute(value, ("dp", "ctx", "tensor"), pairs)


ROWS = 68
TALL = 80
BLOCK = 272
NEAR = 144
Q_COLS = 512
T_START = 2048
T_COLS = 256
M_COLS = 2176


def peer_at(x=0, y=0, c=0, z=0, t=0):
    at = places()
    dp = (lax.rem(at["x"] + x + 4, 4) * 2 + lax.rem(at["y"] + y, 2)) * 2 + lax.rem(at["c"] + c, 2)
    return (dp, lax.rem(at["z"] + z + 4, 4), lax.rem(at["t"] + t, 2))


class Copies:
    def __init__(self, send_sem, recv_sem):
        self.send_sem, self.recv_sem = send_sem, recv_sem
        self.count = 0
        self.open = []

    def to(self, peer, src, dst):
        n = self.count
        self.count += 1
        assert n < self.send_sem.shape[0]
        copy = pltpu.make_async_remote_copy(
            src_ref=src,
            dst_ref=dst,
            send_sem=self.send_sem.at[n],
            recv_sem=self.recv_sem.at[n],
            device_id=peer,
            device_id_type=MESH,
        )
        copy.start()
        self.open.append(copy.wait_send)
        return copy.wait_recv

    def here(self, src, dst):
        n = self.count
        self.count += 1
        assert n < self.send_sem.shape[0]
        copy = pltpu.make_async_copy(src, dst, self.send_sem.at[n])
        copy.start()
        return copy.wait

    def close(self):
        for wait in self.open:
            wait()
        self.open = []


def rows_at(block, count=BLOCK, skip=0):
    return pl.ds(pl.multiple_of(block * BLOCK + skip, 16), count)


class RingX:
    def __init__(self, copies, own, buf, lanes, share):
        self.copies, self.own, self.buf, self.lanes, self.share = copies, own, buf, lanes, share
        at = places()
        self.c, self.x = at["c"], at["x"]
        self.last = []

    def view(self, distance, count=BLOCK, skip=0):
        block = lax.rem(self.x + distance + 4, 4)
        return self.buf.at[self.c, rows_at(block, count, skip), self.lanes]

    def sibling(self, src, dst):
        if self.share:
            self.last.append(self.copies.to(peer_at(c=1), src, dst))

    def start(self):
        self.from_below = self.copies.to(peer_at(x=1), self.own, self.view(0))
        self.from_above = self.copies.to(peer_at(x=-1), self.own, self.view(0))
        self.last.append(self.copies.here(self.own, self.view(0)))
        self.sibling(self.own, self.view(0))

    def forward(self):
        self.from_below()
        part = self.view(-1, NEAR)
        far_a = self.copies.to(peer_at(x=1), part, part)
        self.from_above()
        part = self.view(1, BLOCK - NEAR, NEAR)
        far_b = self.copies.to(peer_at(x=-1), part, part)
        self.far = (far_a, far_b)
        self.sibling(self.view(-1), self.view(-1))
        self.sibling(self.view(1), self.view(1))

    def finish(self):
        for wait in self.far:
            wait()
        self.sibling(self.view(2), self.view(2))

    def close(self):
        for wait in self.last:
            wait()


UPPER, LOWER = pl.ds(0, 2 * BLOCK), pl.ds(2 * BLOCK, 2 * BLOCK)


class RingZ:
    def __init__(self, copies, buf):
        self.copies, self.buf = copies, buf
        at = places()
        self.c, self.z = at["c"], at["z"]
        self.last = []

    def view(self, distance, rows=slice(None)):
        block = lax.rem(self.z + distance + 4, 4)
        return self.buf.at[self.c, rows, pl.ds(pl.multiple_of(block * Q_COLS, 128), Q_COLS)]

    def sibling(self, src):
        self.last.append(self.copies.to(peer_at(c=1), src, src))

    def start(self):
        self.from_below = self.copies.to(peer_at(z=1), self.view(0, UPPER), self.view(0, UPPER))
        self.from_above = self.copies.to(peer_at(z=-1), self.view(0, LOWER), self.view(0, LOWER))
        self.sibling(self.view(0))

    def more(self):
        self.rest = (
            self.copies.to(peer_at(z=1), self.view(0, LOWER), self.view(0, LOWER)),
            self.copies.to(peer_at(z=-1), self.view(0, UPPER), self.view(0, UPPER)),
        )

    def forward(self):
        self.from_below()
        part = self.view(-1, UPPER)
        far_a = self.copies.to(peer_at(z=1), part, part)
        self.from_above()
        part = self.view(1, LOWER)
        far_b = self.copies.to(peer_at(z=-1), part, part)
        self.far = (far_a, far_b)

    def finish(self):
        for wait in self.rest:
            wait()
        self.sibling(self.view(-1))
        self.sibling(self.view(1))
        for wait in self.far:
            wait()
        self.sibling(self.view(2))

    def close(self):
        for wait in self.last:
            wait()


def exchange_shards(copies, mine, landed, lanes=slice(None)):
    c = places()["c"]
    part = lambda ref, n: ref.at[n, :, lanes]
    waits = [
        copies.to(peer_at(c=1), part(mine, 1 - c), part(landed, 1)),
        copies.to(peer_at(y=1), part(mine, c), part(landed, 2)),
        copies.to(peer_at(y=1, c=1), part(mine, 1 - c), part(landed, 3)),
    ]
    waits.append(copies.here(part(mine, c), part(landed, 0)))
    return waits


def assemble(landed, own, begin=0, end=None):
    at = places()
    end = end or own.shape[1]
    for start in range(begin, end, 256):
        lanes = slice(start, min(start + 256, end))
        parts = []
        for j in range(4):
            slot = lax.rem(j // 2 + at["y"], 2) * 2 + lax.rem(j % 2 + at["c"], 2)
            parts.append(landed[slot, :, lanes].astype(F32)[:ROWS])
        own[:, lanes] = jnp.concatenate(parts, 0).astype(BF16)


M_CUT = 1152


def gather_kernel(
    q0, mt0, q1, mt1, docs, attn, mlp, vec_tail, q_next, mt_next, docs_all,
    q_land, mt_land, q_own, mt_own, q_own1, mt_own1, send_sem, recv_sem,
):
    me = group_place()
    greet([dict(c=1), dict(y=1), dict(y=1, c=1), dict(x=1), dict(x=-1)], me)
    copies = Copies(send_sem, recv_sem)
    quarter = pl.ds(pl.multiple_of(places()["z"] * Q_COLS, 128), Q_COLS)
    arrive_q = exchange_shards(copies, q0, q_land.at[0])
    arrive_m = exchange_shards(copies, mt0, mt_land.at[0], pl.ds(0, M_CUT))
    arrive_mt = exchange_shards(copies, mt0, mt_land.at[0], pl.ds(M_CUT, M_COLS + T_COLS - M_CUT))
    later = [copies.here(docs, docs_all.at[me])]
    for n in range(1, GROUP):
        later.append(copies.to(member(lax.rem(me + n, GROUP)), docs, docs_all.at[me]))
    arrive_q1 = exchange_shards(copies, q1, q_land.at[1])
    arrive_mt1 = exchange_shards(copies, mt1, mt_land.at[1])
    q = RingX(copies, q_own, attn, quarter, False)
    m_lanes = (pl.ds(0, M_CUT), pl.ds(M_CUT, M_COLS - M_CUT))
    m = RingX(copies, mt_own.at[:, m_lanes[0]], mlp, m_lanes[0], True)
    m2 = RingX(copies, mt_own.at[:, m_lanes[1]], mlp, m_lanes[1], True)
    t = RingX(copies, mt_own.at[:, pl.ds(M_COLS, T_COLS)], attn, pl.ds(T_START, T_COLS), True)
    along_z = RingZ(copies, attn)

    def landed(waits, land, own, begin=0, end=None):
        for wait in waits:
            wait()
        assemble(land, own, begin, end)

    landed(arrive_q, q_land.at[0], q_own)
    q.start()
    landed(arrive_m, mt_land.at[0], mt_own, 0, M_CUT)
    q.forward()
    m.start()
    landed(arrive_mt, mt_land.at[0], mt_own, M_CUT)
    q.finish()
    q.close()
    along_z.start()
    along_z.more()
    t.start()
    m2.start()
    m.forward()
    landed(arrive_q1, q_land.at[1], q_own1)
    later.append(copies.here(q_own1, q_next))
    landed(arrive_mt1, mt_land.at[1], mt_own1)
    later.append(copies.here(mt_own1, mt_next))
    along_z.forward()
    t.forward()
    m2.forward()
    m.finish()
    along_z.finish()
    t.finish()
    m2.finish()
    for ring in (t, m, m2, along_z):
        ring.close()
    later.append(copies.here(attn.at[0, :, pl.ds(PADDED - 128, 128)], vec_tail))
    for wait in later:
        wait()
    copies.close()


def shard_rows(qkv, out, up, down, extra, z):
    width = out.shape[1]
    role0 = jnp.concatenate([padded(qkv[:, :width], extra), padded(qkv[:, width : 2 * width])], 1)
    role1 = jnp.concatenate([padded(qkv[:, 2 * width :]), padded(out)], 1)
    attn = jnp.pad(jnp.stack([role0, role1]), ((0, 0), (0, TALL - ROWS), (0, 0)))
    mlp = jnp.pad(jnp.stack([up, down]), ((0, 0), (0, TALL - ROWS), (0, 0)))
    quarter = lax.dynamic_slice_in_dim(attn, z * Q_COLS, Q_COLS, 2)
    return quarter, jnp.concatenate([mlp, attn[:, :, T_START:]], 2)


def gather_first(shards, docs, collective):
    hbm = pl.BlockSpec(memory_space=pl.ANY)
    shape = jax.ShapeDtypeStruct
    (q0, mt0), (q1, mt1) = shards
    low = lambda *dims: pltpu.VMEM(dims, BF16)
    return pl.pallas_call(
        gather_kernel,
        out_shape=[
            shape((2, 4 * BLOCK, 2 * PADDED), BF16),
            shape((2, 4 * BLOCK, M_COLS), BF16),
            shape((4 * BLOCK, 128), BF16),
            shape((BLOCK, Q_COLS), BF16),
            shape((BLOCK, M_COLS + T_COLS), BF16),
            shape((GROUP, *docs.shape), docs.dtype),
        ],
        in_specs=[hbm] * 5,
        out_specs=[hbm] * 6,
        scratch_shapes=[
            low(2, 4, TALL, Q_COLS),
            low(2, 4, TALL, M_COLS + T_COLS),
            low(BLOCK, Q_COLS),
            low(BLOCK, M_COLS + T_COLS),
            low(BLOCK, Q_COLS),
            low(BLOCK, M_COLS + T_COLS),
            pltpu.SemaphoreType.DMA((80,)),
            pltpu.SemaphoreType.DMA((80,)),
        ],
        compiler_params=pltpu.CompilerParams(
            collective_id=collective, has_side_effects=True, vmem_limit_bytes=32 * 2**20
        ),
    )(q0, mt0, q1, mt1, docs)


def padded(matrix, extra=None):
    rows, width = matrix.shape
    parts = [matrix]
    if extra is not None:
        parts.append(extra)
        width += extra.shape[1]
    parts.append(jnp.zeros((rows, PADDED - width), matrix.dtype))
    return jnp.concatenate(parts, 1)


PIECE = 640
HALF = 136
HALF_TALL = 144


def attn_start(z):
    return z * 13 // 3 * 128


def mlp_start(z):
    return z * 512


def contract_rows(a, b):
    return lax.dot_general(a, b, (((0,), (0,)), ((), ())), preferred_element_type=F32)


def contract_cols(a, b):
    return lax.dot_general(a, b, (((1,), (1,)), ((), ())), preferred_element_type=F32)


def block_diagonal(a, b):
    zero = jnp.zeros_like(a)
    return jnp.concatenate(
        [jnp.concatenate([a, zero], 1), jnp.concatenate([zero, b], 1)], 0
    )


def attn_sums(at, operands):
    a, dq, dk, dv, o, dz, vec = operands
    c0 = at["c"] == 0
    width = a.shape[1]
    pick = lambda p, q: jnp.where(c0, p, q)
    vec_cols = jnp.pad(vec.T, ((0, 0), (width, 2 * PADDED - width - vec.shape[0])))
    give = contract_rows(
        jnp.concatenate([a, pick(o, a)], 0), block_diagonal(pick(dv, dq), pick(dz, dk))
    ) + pick(0.0, 1.0) * vec_cols
    got = shifted(give.astype(BF16), c=1)
    keep = contract_rows(
        jnp.concatenate([a, pick(a, o)], 0), block_diagonal(pick(dq, dv), pick(dk, dz))
    ) + pick(1.0, 0.0) * vec_cols
    return (keep + got.astype(F32)).astype(BF16)


def in_chunks(count, step, do):
    def one(i, carry):
        do(pl.ds(pl.multiple_of(i * step, 16), step))
        return carry

    lax.fori_loop(0, count // step, one, 0)


class RingSum:
    def __init__(self, copies, axis, view, rows, near, via, step, stage=None):
        self.copies, self.axis, self.view, self.rows = copies, axis, view, rows
        self.near, self.via, self.step, self.stage = near, via, step, stage
        cut = via.shape[1]
        self.first, self.last = pl.ds(0, cut), pl.ds(cut, rows - cut)
        self.counts = (cut, rows - cut)
        self.up, self.down = peer_at(**{axis: 1}), peer_at(**{axis: -1})

    def start(self):
        self.start_far()
        self.start_near()

    def start_far(self):
        far = self.view(2)
        rest = pl.ds(0, self.counts[1])
        self.via_up = self.copies.to(self.up, far.at[self.first], self.via.at[0])
        self.via_down = self.copies.to(self.down, far.at[self.last], self.via.at[1, rest])
        self.parts = (self.view(1).at[self.first], self.view(-1).at[self.last])
        self.staged = []
        if self.stage is not None:
            staged = (self.stage.at[0], self.stage.at[1, rest])
            for src, dst in zip(self.parts, staged):
                self.staged.append(self.copies.here(src, dst))
            self.parts = staged

    def start_near(self, steps=(0, 1)):
        if 0 in steps:
            self.nears = []
        cut, rest = self.counts
        for n in steps:
            for peer, view, side, begin, count in (
                (self.up, self.view(1), 0, cut, rest),
                (self.down, self.view(-1), 1, 0, cut),
            ):
                half = count // 32 * 16
                rows = pl.ds(begin, half) if n == 0 else pl.ds(begin + half, count - half)
                self.nears.append(self.copies.to(peer, view.at[rows], self.near.at[side, rows]))

    def forward(self):
        for wait in self.staged:
            wait()
        arrived = (self.via_up, self.via_down)
        ends = ((self.up, 0, self.first), (self.down, 1, self.last))
        for n, (peer, side, rows) in enumerate(ends):
            arrived[n]()
            part = self.parts[n]

            def add(r):
                self.via[n, r, :] = (part[r, :].astype(F32) + self.via[n, r, :].astype(F32)).astype(BF16)

            in_chunks(self.counts[n], self.step, add)
            src = self.via.at[n, pl.ds(0, self.counts[n])]
            self.nears.append(self.copies.to(peer, src, self.near.at[side, rows]))

    def land(self):
        for wait in self.nears:
            wait()


def add_near(own, near, rows, step, write):
    def add(r):
        write(r, own[r, :].astype(F32) + near[0, r, :].astype(F32) + near[1, r, :].astype(F32))

    in_chunks(rows, step, add)


def turn(value, distance):
    return lax.rem(value + distance + 4, 4)


def columns_of(array, start_of, z):
    return array.at[:, pl.ds(pl.multiple_of(start_of(z), 128), PIECE)]


def attn_ring(copies, array, near, via, stage):
    view = lambda d: columns_of(array, attn_start, turn(places()["z"], d))
    return RingSum(copies, "z", view, 4 * BLOCK, near, via, 32, stage)


def mlp_ring(copies, array, near, via, stage):
    view = lambda d: array.at[rows_at(turn(places()["x"], d))]
    return RingSum(copies, "x", view, BLOCK, near, via, 16, stage)


def reduce_kernel(
    attn0, mlp0, attn1, mlp1, attn_near1, mlp_near1, out,
    attn_near, attn_via, attn_stage, mlp_near, mlp_via, mlp_stage, attn_own, mlp_own,
    attn_part, mlp_part, near2, via2, halves, got, owned, owned_got, send_sem, recv_sem,
):
    barrier = pltpu.get_barrier_semaphore()
    peers = [dict(c=1), dict(x=1), dict(x=-1), dict(y=1, t=1), dict(y=1), dict(t=1)]
    peers += [dict(z=1), dict(z=-1)]
    for peer in peers:
        pl.semaphore_signal(barrier, inc=1, device_id=peer_at(**peer), device_id_type=MESH)
    pl.semaphore_wait(barrier, len(peers))
    copies = Copies(send_sem, recv_sem)
    at = places()
    ring_a = attn_ring(copies, attn0, attn_near, attn_via, attn_stage)
    ring_m = mlp_ring(copies, mlp0, mlp_near, mlp_via, mlp_stage)
    ring_m.start()
    ring_a.start_far()
    loads = {}
    for l, (attn, mlp) in ((1, (attn1, mlp1)), (0, (attn0, mlp0))):
        loads[l] = (
            copies.here(columns_of(attn, attn_start, at["z"]), attn_own.at[l]),
            copies.here(mlp.at[rows_at(at["x"])], mlp_own.at[l]),
        )

    def second(l, near_a, near_m):
        def write_attn(r, value):
            attn_part[l, r, :] = value.astype(BF16)

        def write_mlp(r, value):
            mlp_part[l, r, :] = value.astype(BF16)

        for wait in loads[l]:
            wait()
        add_near(mlp_own.at[l], near_m, BLOCK, 16, write_mlp)
        m2 = RingSum(
            copies, "z", lambda d: columns_of(mlp_part.at[l], mlp_start, turn(at["z"], d)),
            BLOCK, near2.at[l, 1], via2.at[l, 1], 16,
        )
        m2.start()
        add_near(attn_own.at[l], near_a, 4 * BLOCK, 32, write_attn)
        a2 = RingSum(
            copies, "x", lambda d: attn_part.at[l, rows_at(turn(at["x"], d))],
            BLOCK, near2.at[l, 0], via2.at[l, 0], 16,
        )
        a2.start()
        return a2, m2

    def third(l, rings):
        waits = []
        for n, ring in enumerate(rings):
            ring.land()
            own = ring.view(0)
            total = (
                own[...].astype(F32) + ring.near[0].astype(F32) + ring.near[1].astype(F32)
            )
            halves[l, n, 0, :HALF] = total[:HALF].astype(BF16)
            halves[l, n, 1, :HALF] = total[HALF:].astype(BF16)
            halves[l, n, 0, HALF:] = jnp.zeros((HALF_TALL - HALF, PIECE), BF16)
            halves[l, n, 1, HALF:] = jnp.zeros((HALF_TALL - HALF, PIECE), BF16)
            peer = peer_at(y=1, t=1) if n == 0 else peer_at(y=1)
            waits.append(copies.to(peer, halves.at[l, n, 1 - at["y"]], got.at[l, n]))
        return waits

    def fourth(l, waits):
        waits[0]()
        mine = halves[l, 0, at["y"]].astype(F32) + got[l, 0].astype(F32)
        halves[l, 0, at["y"]] = mine.astype(BF16)
        return copies.to(peer_at(t=1), halves.at[l, 0, at["y"]], got.at[l, 2])

    def fifth(l, waits, wait):
        waits[1]()
        wait()
        ends = []
        for n, landed in ((0, 2), (1, 1)):
            total = halves[l, n, at["y"]].astype(F32) + got[l, landed].astype(F32)
            for core in range(2):
                owned[l, n, core, :ROWS] = total[core * ROWS : core * ROWS + ROWS].astype(BF16)
                owned[l, n, core, ROWS:] = jnp.zeros((TALL - ROWS, PIECE), BF16)
            ends.append(copies.to(peer_at(c=1), owned.at[l, n, 1 - at["c"]], owned_got.at[l, n]))
        return ends

    def sixth(l, ends):
        for wait in ends:
            wait()
        arrived = []
        for n in range(2):
            for role, src in ((at["c"], owned.at[l, n, at["c"]]), (1 - at["c"], owned_got.at[l, n])):
                dst = out.at[l, at["z"], n, role]
                rest.append(copies.here(src, dst))
                below = copies.to(peer_at(z=1), src, dst)
                arrived.append((n, role, below, copies.to(peer_at(z=-1), src, dst)))
        return arrived

    def seventh(l, arrived):
        for n, role, below, above in arrived:
            below()
            part = out.at[l, turn(at["z"], -1), n, role, pl.ds(0, 48)]
            rest.append(copies.to(peer_at(z=1), part, part))
            above()
            part = out.at[l, turn(at["z"], 1), n, role, pl.ds(48, 32)]
            rest.append(copies.to(peer_at(z=-1), part, part))

    rings, waits, turned, ends, rest = {}, {}, {}, {}, []
    order = (1, 0)
    rings[1] = second(1, attn_near1, mlp_near1)
    ring_a.start_near()
    ring_m.forward()
    ring_a.forward()
    for ring in reversed(rings[1]):
        ring.forward()
    ring_m.land()
    ring_a.land()
    rings[0] = second(0, attn_near, mlp_near)
    waits[1] = third(1, rings[1])
    turned[1] = fourth(1, waits[1])
    for ring in reversed(rings[0]):
        ring.forward()
    ends[1] = fifth(1, waits[1], turned[1])
    waits[0] = third(0, rings[0])
    turned[0] = fourth(0, waits[0])
    late = sixth(1, ends[1])
    ends[0] = fifth(0, waits[0], turned[0])
    last = sixth(0, ends[0])
    seventh(1, late)
    seventh(0, last)
    for wait in rest:
        wait()
    copies.close()


def reduce_layers(sums, near, collective):
    hbm = pl.BlockSpec(memory_space=pl.ANY)
    vmem = pl.BlockSpec(memory_space=pltpu.VMEM)
    low = lambda *dims: pltpu.VMEM(dims, BF16)
    return pl.pallas_call(
        reduce_kernel,
        out_shape=jax.ShapeDtypeStruct((2, 4, 2, 2, TALL, PIECE), BF16),
        in_specs=[hbm] * 4 + [vmem] * 2,
        out_specs=hbm,
        scratch_shapes=[
            low(2, 4 * BLOCK, PIECE),
            low(2, 2 * BLOCK, PIECE),
            low(2, 2 * BLOCK, PIECE),
            low(2, BLOCK, M_COLS),
            low(2, NEAR, M_COLS),
            low(2, NEAR, M_COLS),
            low(2, 4 * BLOCK, PIECE),
            low(2, BLOCK, M_COLS),
            low(2, 4 * BLOCK, PIECE),
            low(2, BLOCK, M_COLS),
            low(2, 2, 2, BLOCK, PIECE),
            low(2, 2, 2, NEAR, PIECE),
            low(2, 2, 2, HALF_TALL, PIECE),
            low(2, 3, HALF_TALL, PIECE),
            low(2, 2, 2, TALL, PIECE),
            low(2, 2, TALL, PIECE),
            pltpu.SemaphoreType.DMA((128,)),
            pltpu.SemaphoreType.DMA((128,)),
        ],
        compiler_params=pltpu.CompilerParams(
            collective_id=collective, has_side_effects=True, vmem_limit_bytes=56 * 2**20
        ),
    )(*sums[0], *sums[1], *near)


def owned_gradients(parts, width):
    parts = parts[:, :, :, :ROWS]

    def joined(n, role, widths):
        return jnp.concatenate([parts[z, n, role, :, :w] for z, w in enumerate(widths)], 1)

    attn = [joined(0, role, (512, 512, 640, 640)) for role in range(2)]
    up, down = (joined(1, role, (512, 512, 512, 640)) for role in range(2))
    qk, vo = attn
    in_back = jnp.concatenate([qk[:, :width], qk[:, PADDED : PADDED + width], vo[:, :width]], 1)
    vec_back = qk[:, width : width + 12].T
    results = (in_back, vo[:, PADDED : PADDED + width], up, down, vec_back)
    return tuple(value.astype(F32) for value in results)


def group_place():
    return lax.axis_index("ctx") * 2 + lax.axis_index("tensor")


def member(index):
    return (lax.axis_index("dp"), index // 2, lax.rem(index, 2))


def meet(me):
    barrier = pltpu.get_barrier_semaphore()
    for k in range(1, GROUP):
        pl.semaphore_signal(
            barrier, inc=1, device_id=member(lax.rem(me + k, GROUP)), device_id_type=MESH
        )
    pl.semaphore_wait(barrier, GROUP - 1)


def to_heads(me, sources, landed, local_sem, send_sem, recv_sem):
    copies = []
    for k in range(1, GROUP):
        peer = lax.rem(me + k, GROUP)
        rows = pl.ds(pl.multiple_of(peer // 4 * 64, 64), 64)
        lanes = pl.ds(pl.multiple_of(lax.rem(peer, 4) * STRIDE, 128), WINDOW)
        for n, (src, dst) in enumerate(zip(sources, landed)):
            copy = pltpu.make_async_remote_copy(
                src_ref=src.at[rows, lanes],
                dst_ref=dst.at[pl.ds(pl.multiple_of(me * 64, 64), 64)],
                send_sem=send_sem.at[n, k],
                recv_sem=recv_sem.at[n, k],
                device_id=member(peer),
                device_id_type=MESH,
            )
            copy.start()
            copies.append(copy)
    rows = pl.ds(pl.multiple_of(me // 4 * 64, 64), 64)
    lanes = pl.ds(pl.multiple_of(lax.rem(me, 4) * STRIDE, 128), WINDOW)
    for n, (src, dst) in enumerate(zip(sources, landed)):
        copy = pltpu.make_async_copy(
            src.at[rows, lanes], dst.at[pl.ds(pl.multiple_of(me * 64, 64), 64)], local_sem.at[n]
        )
        copy.start()
        copies.append(copy)
    return copies


def to_rows(me, sources, landed, local_sem, send_sem, recv_sem):
    copies = []
    for k in range(1, GROUP):
        peer = lax.rem(me + k, GROUP)
        for n, (src, dst) in enumerate(zip(sources, landed)):
            copy = pltpu.make_async_remote_copy(
                src_ref=src.at[pl.ds(pl.multiple_of(peer * 64, 64), 64)],
                dst_ref=dst.at[me],
                send_sem=send_sem.at[n, k],
                recv_sem=recv_sem.at[n, k],
                device_id=member(peer),
                device_id_type=MESH,
            )
            copy.start()
            copies.append(copy)
    for n, (src, dst) in enumerate(zip(sources, landed)):
        copy = pltpu.make_async_copy(
            src.at[pl.ds(pl.multiple_of(me * 64, 64), 64)], dst.at[me], local_sem.at[n]
        )
        copy.start()
        copies.append(copy)
    return copies


def side_by_side(landed, out):
    for micro in range(2):
        rows = slice(micro * 64, micro * 64 + 64)
        for group in range(4):
            width = WINDOW if group == 3 else STRIDE
            out[rows, group * STRIDE : group * STRIDE + width] = landed[micro * 4 + group, :, :width]


def matmul(a, b, dims):
    return lax.dot_general(a, b, ((dims[:1], dims[1:]), ((), ())), preferred_element_type=F32)


def score_bias(docs):
    docs = lax.dynamic_index_in_dim(docs, lax.axis_index("ctx") // 2, 1, keepdims=False)
    docs = docs[:, :64].reshape(-1)
    place = jnp.arange(docs.shape[0], dtype=jnp.int32)
    allowed = (docs[:, None] == docs[None, :]) & (place[None, :] <= place[:, None])
    return jnp.where(allowed, 0.0, MASKED).astype(F32)


def tiles_of(width, step):
    return [(start, min(start + step, width)) for start in range(0, width, step)]


def normalise(inputs):
    centred = inputs - jnp.mean(inputs, 1, keepdims=True)
    spread = jnp.mean(centred * centred, 1, keepdims=True)
    scale = lax.rsqrt(spread + EPSILON)
    return centred * scale, scale


def gelu_and_slope(u):
    share = 0.5 * (1.0 + lax.erf(u * 0.7071067811865476))
    return u * share, share + u * jnp.exp(-0.5 * u * u) * 0.3989422804014327


def greet(peers, me):
    barrier = pltpu.get_barrier_semaphore()
    members = [member(lax.rem(me + k, GROUP)) for k in range(1, GROUP)]
    for peer in members + [peer_at(**peer) for peer in peers]:
        pl.semaphore_signal(barrier, inc=1, device_id=peer, device_id_type=MESH)
    pl.semaphore_wait(barrier, len(members) + len(peers))


def forward_kernel(*refs, carry):
    resid, vec, bias_up, mask, attn_in, mlp_in = refs[:6]
    refs = refs[6:]
    if carry:
        q_own, mt_own = refs[:2]
        refs = refs[2:]
    (
        resid_out, normed, q_all, k_all, v_all, o_all, log_total, o_out, midway, m_out, g_out, d_out,
    ) = refs[:12]
    refs = refs[12:]
    if carry:
        next_attn, next_mlp = refs[:2]
        refs = refs[2:]
    (
        attn, mlp, q, k, v, o_low, o_landed, part, part_got, load_sem, local_sem, send_sem, recv_sem,
    ) = refs[:13]
    me = group_place()
    greet([dict(c=1), dict(x=1), dict(x=-1)] if carry else [], me)
    loads = []
    for n, (src, dst) in enumerate(
        [(attn_in.at[0], attn.at[0]), (attn_in.at[1], attn.at[1]), (mlp_in.at[0], mlp.at[0]), (mlp_in.at[1], mlp.at[1])]
    ):
        copy = pltpu.make_async_copy(src, dst, load_sem.at[n])
        copy.start()
        loads.append(copy.wait)
    if carry:
        copies = Copies(*refs[13:15])
        quarter = pl.ds(pl.multiple_of(places()["z"] * Q_COLS, 128), Q_COLS)
        ring_q = RingX(copies, q_own, next_attn, quarter, False)
        ring_m = RingX(copies, mt_own.at[:, pl.ds(0, M_COLS)], next_mlp, slice(None), True)
        ring_t = RingX(copies, mt_own.at[:, pl.ds(M_COLS, T_COLS)], next_attn, pl.ds(T_START, T_COLS), True)
        ring_z = RingZ(copies, next_attn)
        ring_q.start()
    row = lambda n: vec[n : n + 1, :]
    width = resid.shape[1]
    x, _ = normalise(resid[...])
    a = (x * row(0)[:, :width] + row(1)[:, :width]).astype(BF16)
    normed[...] = a
    loads[0]()
    for start, stop in tiles_of(PADDED, 384):
        lanes = slice(start, stop)
        q[:, lanes] = (matmul(a, attn[0, :, lanes], (1, 0)) + vec[2:3, lanes]).astype(BF16)
        k[:, lanes] = matmul(a, attn[0, :, PADDED + start : PADDED + stop], (1, 0)).astype(BF16)
    loads[1]()
    if carry:
        ring_q.forward()
        ring_t.start()
        ring_m.start()
    for start, stop in tiles_of(PADDED, 384):
        lanes = slice(start, stop)
        v[:, lanes] = (matmul(a, attn[1, :, lanes], (1, 0)) + vec[3:4, lanes]).astype(BF16)
    exchanged = to_heads(me, (q, k, v), (q_all, k_all, v_all), local_sem, send_sem, recv_sem)
    o_low[...] = jnp.zeros_like(o_low)
    o_all[...] = jnp.zeros_like(o_all)
    log_total[...] = jnp.zeros_like(log_total)
    if carry:
        ring_q.finish()
        ring_q.close()
        ring_z.start()
    for copy in exchanged:
        copy.wait()
    for head in range(SLOTS):
        lanes = slice(head * HEAD, head * HEAD + HEAD)
        keys, values = k_all[:, lanes], v_all[:, lanes]
        for start in range(0, 512, CHUNK):
            rows, reach = slice(start, start + CHUNK), start + CHUNK
            queries = q_all[rows, lanes] * 0.125
            scores = matmul(queries, keys[:reach], (1, 1)) + mask[rows, :reach]
            top = jnp.max(scores, 1, keepdims=True)
            weights = jnp.exp(scores - top)
            total = jnp.sum(weights, 1, keepdims=True)
            result = matmul(weights.astype(BF16), values[:reach], (1, 0)) / total
            o_all[rows, lanes] = result
            o_low[rows, lanes] = result.astype(BF16)
            log_total[rows, head : head + 1] = top + jnp.log(total)
        if carry and head == 3:
            ring_t.forward()
            ring_m.forward()
    exchanged = to_rows(
        me, (o_low,), (o_landed,), local_sem.at[3:4], send_sem.at[3:4], recv_sem.at[3:4]
    )
    for copy in exchanged:
        copy.wait()
    if carry:
        ring_z.forward()
        ring_z.more()
    side_by_side(o_landed, o_out)
    o = o_out[:, :width]
    for start, stop in tiles_of(width, 384):
        lanes = slice(start, stop)
        midway[:, lanes] = (
            resid[:, lanes]
            + matmul(o, attn[1, :, PADDED + start : PADDED + stop], (1, 0))
            + vec[4:5, lanes]
        )
    x, _ = normalise(midway[...])
    m_out[0] = (x * row(5)[:, :width] + row(6)[:, :width]).astype(BF16)

    def to_pair(src, dst, n):
        copy = pltpu.make_async_remote_copy(
            src_ref=src,
            dst_ref=dst,
            send_sem=send_sem.at[4, n],
            recv_sem=recv_sem.at[4, n],
            device_id=peer_at(t=1),
            device_id_type=MESH,
        )
        copy.start()
        return copy

    rows_sent = to_pair(m_out.at[0], m_out.at[1], 0)
    loads[2]()

    def up(side):
        for start, stop in tiles_of(M_COLS, 256):
            lanes = slice(start, stop)
            u = matmul(m_out[side], mlp[0, :, lanes], (1, 0)) + bias_up[0:1, lanes]
            g, d = gelu_and_slope(u)
            g_out[side, :, lanes] = g.astype(BF16)
            d_out[side, :, lanes] = d.astype(BF16)

    up(0)
    rows_sent.wait()
    up(1)
    loads[3]()
    for start, stop in tiles_of(width, 256):
        part[:, start:stop] = matmul(g_out[1], mlp[1, start:stop, :], (1, 1)).astype(BF16)
    part_sent = to_pair(part, part_got, 1)
    for start, stop in tiles_of(width, 256):
        resid_out[:, start:stop] = matmul(g_out[0], mlp[1, start:stop, :], (1, 1))
    part_sent.wait()
    resid_out[...] += midway[...] + part_got[...].astype(F32) + row(7)[:, :width]
    if carry:
        ring_t.finish()
        ring_z.finish()
        ring_m.finish()
        for ring in (ring_t, ring_z, ring_m):
            ring.close()
        copies.close()


def forward_layer(resid, vec, bias_up, mask, weights, pieces, collective):
    shape = jax.ShapeDtypeStruct
    vmem = pl.BlockSpec(memory_space=pltpu.VMEM)
    hbm = pl.BlockSpec(memory_space=pl.ANY)
    rows, width = resid.shape
    carry = pieces is not None
    low = lambda *dims: pltpu.VMEM(dims, BF16)
    out_shape = [
        shape((rows, width), F32),
        shape((rows, width), BF16),
        shape((512, WINDOW), BF16),
        shape((512, WINDOW), BF16),
        shape((512, WINDOW), BF16),
        shape((512, WINDOW), F32),
        shape((512, 128), F32),
        shape((rows, PADDED), BF16),
        shape((rows, width), F32),
        shape((2, rows, width), BF16),
        shape((2, rows, M_COLS), BF16),
        shape((2, rows, M_COLS), BF16),
    ]
    scratch = [
        low(2, 4 * BLOCK, 2 * PADDED),
        low(2, 4 * BLOCK, M_COLS),
        low(rows, PADDED),
        low(rows, PADDED),
        low(rows, PADDED),
        low(512, WINDOW),
        low(GROUP, 64, WINDOW),
        low(rows, width),
        low(rows, width),
        pltpu.SemaphoreType.DMA((4,)),
        pltpu.SemaphoreType.DMA((4,)),
        pltpu.SemaphoreType.DMA((5, GROUP)),
        pltpu.SemaphoreType.DMA((5, GROUP)),
    ]
    if carry:
        out_shape += [shape(w.shape, w.dtype) for w in weights]
        scratch += [pltpu.SemaphoreType.DMA((40,))] * 2
    results = pl.pallas_call(
        functools.partial(forward_kernel, carry=carry),
        out_shape=out_shape,
        in_specs=[vmem] * 4 + [hbm] * (4 if carry else 2),
        out_specs=[vmem] * 12 + [hbm] * (2 if carry else 0),
        scratch_shapes=scratch,
        compiler_params=pltpu.CompilerParams(
            collective_id=collective, has_side_effects=True, vmem_limit_bytes=56 * 2**20
        ),
    )(resid, vec, bias_up, mask, *weights, *(pieces or ()))
    return results[:12], tuple(results[12:])


def norm_back(inputs, gain, back):
    x, scale = normalise(inputs)
    e = back * gain
    grad = scale * (
        e - jnp.mean(e, 1, keepdims=True) - x * jnp.mean(e * x, 1, keepdims=True)
    )
    return grad, jnp.sum(back * x, 0, keepdims=True), jnp.sum(back, 0, keepdims=True)


def backward_kernel(*refs, carry):
    (
        grad, vec, mask, layer_in, midway, d_in, m_in, g_in, q_all, k_all, v_all, o_all, log_total,
        attn_in, mlp_in,
    ) = refs[:15]
    refs = refs[15:]
    if carry:
        attn_sum, mlp_sum = refs[:2]
        refs = refs[2:]
    grad_out, dz, dq, dk, dv, small, bias_back, mlp_total = refs[:8]
    refs = refs[8:]
    if carry:
        attn_near, mlp_near = refs[:2]
        refs = refs[2:]
    (
        attn, mlp, part, part_got, through, do, do_all, dq_low, dk_low, dv_low, dq_landed, dk_landed, dv_landed,
        dk_sum, dv_sum, load_sem, local_sem, send_sem, recv_sem, dy, du, mlp_got, turned,
    ) = refs[:23]
    me = group_place()
    greet([dict(c=1)] + ([dict(x=1), dict(x=-1)] if carry else []), me)
    width = grad.shape[1]
    dy[0] = grad[...].astype(BF16)

    def to_pair(src, dst, n, peer=peer_at(t=1)):
        copy = pltpu.make_async_remote_copy(
            src_ref=src,
            dst_ref=dst,
            send_sem=send_sem.at[4, n],
            recv_sem=recv_sem.at[4, n],
            device_id=peer,
            device_id_type=MESH,
        )
        copy.start()
        return copy

    def mlp_products(up, write):
        for side in range(2):
            left = jnp.where(up, m_in[side].astype(F32), dy[side].astype(F32))
            turned[:, side * 128 : side * 128 + 128] = jnp.transpose(left).astype(BF16)
        for start, stop in tiles_of(M_COLS, 256):
            lanes = slice(start, stop)
            right = [jnp.where(up, du[n, :, lanes].astype(F32), g_in[n, :, lanes].astype(F32)) for n in range(2)]
            right = jnp.concatenate(right, 0).astype(BF16)
            write(lanes, matmul(turned[...], right, (1, 0)))

    rows_sent = to_pair(dy.at[0], dy.at[1], 0)
    loads = []
    for n, (src, dst) in enumerate(
        [(mlp_in.at[1], mlp.at[1]), (mlp_in.at[0], mlp.at[0]), (attn_in.at[1], attn.at[1]), (attn_in.at[0], attn.at[0])]
    ):
        copy = pltpu.make_async_copy(src, dst, load_sem.at[n])
        copy.start()
        loads.append(copy.wait)
    if carry:
        attn_via, attn_stage, mlp_via, mlp_stage = refs[23:27]
        copies = Copies(*refs[27:29])
        ring_a = attn_ring(copies, attn_sum, attn_near, attn_via, attn_stage)
        ring_m = mlp_ring(copies, mlp_sum, mlp_near, mlp_via, mlp_stage)
        ring_a.start_far()
        ring_a.start_near((0,))
        ring_m.start()
    loads[0]()

    def hidden_back(side):
        for start, stop in tiles_of(M_COLS, 256):
            lanes = slice(start, stop)
            back = matmul(dy[side], mlp[1, :, lanes], (1, 0)) * d_in[side, :, lanes].astype(F32)
            du[side, :, lanes] = back.astype(BF16)

    hidden_back(0)
    rows_sent.wait()
    hidden_back(1)
    loads[1]()
    for start, stop in tiles_of(width, 256):
        part[:, start:stop] = matmul(du[1], mlp[0, start:stop, :], (1, 1)).astype(BF16)
    part_sent = to_pair(part, part_got, 1)
    for start, stop in tiles_of(width, 256):
        through[:, start:stop] = matmul(du[0], mlp[0, start:stop, :], (1, 1))
    part_sent.wait()
    dm = through[...] + part_got[...].astype(F32)
    step, gain, shift = norm_back(midway[...], vec[5:6, :width], dm)
    small[5:6, :] = gain
    small[6:7, :] = shift
    through[...] = grad[...] + step
    dz[...] = jnp.zeros_like(dz)
    dz[:, :width] = through[...].astype(BF16)
    do[...] = jnp.zeros_like(do)
    loads[2]()
    for start, stop in tiles_of(width, 256):
        do[:, start:stop] = matmul(dz[...], attn[1, start:stop, PADDED:], (1, 1)).astype(BF16)
    exchanged = to_heads(
        me, (do,), (do_all,), local_sem.at[3:4], send_sem.at[3:4], recv_sem.at[3:4]
    )
    dq_low[...] = jnp.zeros_like(dq_low)
    dk_low[...] = jnp.zeros_like(dk_low)
    dv_low[...] = jnp.zeros_like(dv_low)
    low_sum = lambda value: jnp.sum(value.astype(F32), 0, keepdims=True)
    small[4:5, :] = low_sum(dz[:, :width])
    small[7:8, :] = low_sum(dy[0])
    bias_back[...] = jnp.broadcast_to(low_sum(du[0]) + low_sum(du[1]), bias_back.shape)

    def give(lanes, value):
        mlp[0, :, lanes] = value.astype(BF16)

    mlp_products(places()["c"] == 1, give)
    mlp_sent = to_pair(mlp.at[0], mlp_got, 2, peer_at(c=1))
    for copy in exchanged:
        copy.wait()
    if carry:
        ring_a.start_near((1,))
        ring_a.forward()
    for head in range(SLOTS):
        lanes = slice(head * HEAD, head * HEAD + HEAD)
        keys, values = k_all[:, lanes], v_all[:, lanes]
        dk_sum[...] = jnp.zeros_like(dk_sum)
        dv_sum[...] = jnp.zeros_like(dv_sum)
        for start in range(0, 512, CHUNK):
            rows, reach = slice(start, start + CHUNK), start + CHUNK
            queries = q_all[rows, lanes] * 0.125
            grads = do_all[rows, lanes]
            scores = matmul(queries, keys[:reach], (1, 1)) + mask[rows, :reach]
            probs = jnp.exp(scores - log_total[rows, head : head + 1])
            probs_back = matmul(grads, values[:reach], (1, 1))
            delta = jnp.sum(grads.astype(F32) * o_all[rows, lanes], 1, keepdims=True)
            scores_back = (probs * (probs_back - delta)).astype(BF16)
            dq_low[rows, lanes] = (matmul(scores_back, keys[:reach], (1, 0)) * 0.125).astype(BF16)
            dk_sum[:reach] += matmul(scores_back, queries, (0, 0))
            dv_sum[:reach] += matmul(probs.astype(BF16), grads, (0, 0))
        dk_low[:, lanes] = dk_sum[...].astype(BF16)
        dv_low[:, lanes] = dv_sum[...].astype(BF16)
        if carry and head == 2:
            ring_m.forward()
    exchanged = to_rows(
        me,
        (dq_low, dk_low, dv_low),
        (dq_landed, dk_landed, dv_landed),
        local_sem,
        send_sem,
        recv_sem,
    )
    loads[3]()
    mlp_sent.wait()

    def keep(lanes, value):
        mlp[1, :, lanes] = (value + mlp_got[:, lanes].astype(F32)).astype(BF16)

    mlp_products(places()["c"] == 0, keep)
    store = pltpu.make_async_copy(mlp.at[1], mlp_total, load_sem.at[0])
    store.start()
    for copy in exchanged:
        copy.wait()
    side_by_side(dq_landed, dq)
    side_by_side(dk_landed, dk)
    side_by_side(dv_landed, dv)
    small[2:3, :] = low_sum(dq[:, :width])
    small[3:4, :] = low_sum(dv[:, :width])
    for start, stop in tiles_of(width, 256):
        back = matmul(dq[...], attn[0, start:stop, :PADDED], (1, 1))
        back += matmul(dk[...], attn[0, start:stop, PADDED:], (1, 1))
        grad_out[:, start:stop] = back + matmul(dv[...], attn[1, start:stop, :PADDED], (1, 1))
    step, gain, shift = norm_back(layer_in[...], vec[0:1, :width], grad_out[...])
    small[0:1, :] = gain
    small[1:2, :] = shift
    grad_out[...] = through[...] + step
    store.wait()
    if carry:
        ring_a.land()
        ring_m.land()
        copies.close()


def backward_layer(grad, vec, mask, kept, weights, sums, collective):
    shape = jax.ShapeDtypeStruct
    vmem = pl.BlockSpec(memory_space=pltpu.VMEM)
    hbm = pl.BlockSpec(memory_space=pl.ANY)
    rows, width = grad.shape
    carry = sums is not None
    low = lambda *dims: pltpu.VMEM(dims, BF16)
    out_shape = [
        shape((rows, width), F32),
        *[shape((rows, PADDED), BF16)] * 4,
        shape((8, width), F32),
        shape((8, M_COLS), F32),
        shape((4 * BLOCK, M_COLS), BF16),
    ]
    scratch = [
        low(2, 4 * BLOCK, 2 * PADDED),
        low(2, 4 * BLOCK, M_COLS),
        low(rows, width),
        low(rows, width),
        pltpu.VMEM((rows, width), F32),
        low(rows, PADDED),
        *[low(512, WINDOW)] * 4,
        *[low(GROUP, 64, WINDOW)] * 3,
        *[pltpu.VMEM((512, HEAD), F32)] * 2,
        pltpu.SemaphoreType.DMA((4,)),
        pltpu.SemaphoreType.DMA((4,)),
        pltpu.SemaphoreType.DMA((5, GROUP)),
        pltpu.SemaphoreType.DMA((5, GROUP)),
        low(2, rows, width),
        low(2, rows, M_COLS),
        low(4 * BLOCK, M_COLS),
        low(4 * BLOCK, 256),
    ]
    if carry:
        out_shape += [shape((2, 4 * BLOCK, PIECE), BF16), shape((2, BLOCK, M_COLS), BF16)]
        scratch += [low(2, 2 * BLOCK, PIECE)] * 2 + [low(2, NEAR, M_COLS)] * 2
        scratch += [pltpu.SemaphoreType.DMA((24,))] * 2
    results = pl.pallas_call(
        functools.partial(backward_kernel, carry=carry),
        out_shape=out_shape,
        in_specs=[vmem] * 13 + [hbm] * (4 if carry else 2),
        out_specs=[vmem] * 7 + [hbm] * (3 if carry else 1),
        scratch_shapes=scratch,
        compiler_params=pltpu.CompilerParams(
            collective_id=collective, has_side_effects=True, vmem_limit_bytes=58 * 2**20
        ),
    )(grad, vec, mask, *kept, *weights, *(sums or ()))
    return results[:8], tuple(results[8:])


def body(tokens, qkv_weight, out_weight, up_weight, down_weight, vectors, segments, cotangent):
    micro_count, row_count, width = tokens.shape
    layers = qkv_weight.shape[0]
    hidden_half = up_weight.shape[2]
    total_rows = micro_count * row_count
    at = places()
    docs = jnp.pad(segments, ((0, 8 - micro_count), (0, 128 - row_count)))
    *first, tail, q_next, mt_next, docs = gather_first(
        [
            shard_rows(
                qkv_weight[l],
                out_weight[l],
                up_weight[l],
                down_weight[l],
                vectors.reshape(12 * layers, -1).T if l == 0 else None,
                at["z"],
            )
            for l in range(layers)
        ],
        docs,
        3,
    )
    bias = score_bias(docs)
    all_vectors = tail[:, width - PADDED + 128 :].T.astype(F32)
    weights = [tuple(first)]
    residual = tokens.reshape(total_rows, width).astype(F32)
    memory = []
    for l in range(layers):
        vec = all_vectors[12 * l : 12 * l + 12]
        bias_up = lax.dynamic_slice_in_dim(vec[8:].reshape(-1), at["t"] * hidden_half, hidden_half)
        vec = jnp.pad(vec, ((0, 4), (0, PADDED - width)))
        kept, following = forward_layer(
            residual,
            vec,
            jnp.broadcast_to(bias_up, (8, hidden_half)),
            bias,
            weights[l],
            (q_next, mt_next) if l == 0 else None,
            5 + l,
        )
        if l == 0:
            weights.append(following)
        memory.append((vec, residual, *kept[1:]))
        residual = kept[0]
    result = residual
    gradient = cotangent.reshape(total_rows, width)
    sums = [None] * layers
    near = None
    for l in reversed(range(layers)):
        vec, layer_in, normed, *saved, o, midway, m, g, d = memory[l]
        kept, passed = backward_layer(
            gradient,
            vec,
            bias,
            (layer_in, midway, d, m, g, *saved),
            weights[l],
            sums[1] if l == 0 else None,
            7 + l,
        )
        near = passed or near
        gradient, dz, dq, dk, dv, small, bias_back, mlp_sum = kept
        bias_back = lax.dynamic_update_slice_in_dim(
            jnp.zeros((2 * hidden_half,), F32), bias_back[0], at["t"] * hidden_half, 0
        )
        vec_back = jnp.concatenate([small, bias_back.reshape(-1, width)], 0)
        sums[l] = (attn_sums(at, (normed, dq, dk, dv, o[:, :width], dz, vec_back)), mlp_sum)
    parts = reduce_layers(sums, near, 4)
    totals = [owned_gradients(parts[l], width) for l in range(layers)]
    stacked = [jnp.stack([totals[l][n] for l in range(layers)]) for n in range(5)]
    shape = (micro_count, row_count, width)
    return (result.reshape(shape), gradient.reshape(shape), *stacked)


def solution(mesh):
    return jax.shard_map(
        body,
        mesh=mesh,
        in_specs=(
            P(None, ("dp", "ctx", "tensor"), None),
            P(None, "dp", None),
            P(None, "dp", None),
            P(None, "dp", "tensor"),
            P(None, "dp", "tensor"),
            P(None, None, "dp"),
            P(None, ("dp", "ctx", "tensor")),
            P(None, ("dp", "ctx", "tensor"), None),
        ),
        out_specs=(
            P(None, ("dp", "ctx", "tensor"), None),
            P(None, ("dp", "ctx", "tensor"), None),
            P(None, "dp", None),
            P(None, "dp", None),
            P(None, "dp", "tensor"),
            P(None, "dp", "tensor"),
            P(None, None, "dp"),
        ),
        check_vma=False,
    )
```
